128 devices in a mesh: section: 2 (over core), seq: 16 (over z, y), wshard: 4 (over x).
Axes of the slice: x: 4, y: 4, z: 4, core: 2. Of those that a mesh axis runs over, the one named last changes fastest.
Arguments:
- hidden: bfloat16 [8, 2048, 1024], P('wshard', 'seq'), may hold values from -6 to 6
- out_grad: bfloat16 [8, 2048, 1024], P('wshard', 'seq'), may hold values from -6 to 6
- norm_gain: float32 [2, 1024], P('section'), may hold values from 0.1 to 1.9
- in_weight: bfloat16 [2, 1024, 4384], P('section', 'wshard'), may hold values from -0.1875 to 0.1875
- conv_weight: float32 [2, 4, 2304], P('section'), may hold values from -3 to 3
- conv_bias: float32 [2, 2304], P('section'), may hold values from -3 to 3
- dt_bias: float32 [2, 32], P('section'), may hold values from -7 to -3
- a_log: float32 [2, 32], P('section'), may hold values from -1 to 2
- d_skip: float32 [2, 32], P('section'), may hold values from -4 to 4
- out_gain: float32 [2, 2048], P('section'), may hold values from 0.1 to 1.9
- out_weight: bfloat16 [2, 2048, 1024], P('section', 'wshard'), may hold values from -0.125 to 0.125
Outputs:
- layer_out: bfloat16 [2, 8, 2048, 1024], P('section', 'wshard', 'seq')
- section_grad: float32 [2, 8, 2048, 1024], P('section', 'wshard', 'seq')
- grad_norm_gain: float32 [2, 1024], P('section')
- grad_in_weight: float32 [2, 1024, 4384], P('section', 'wshard')
- grad_conv_weight: float32 [2, 4, 2304], P('section')
- grad_conv_bias: float32 [2, 2304], P('section')
- grad_dt_bias: float32 [2, 32], P('section')
- grad_a_log: float32 [2, 32], P('section')
- grad_d_skip: float32 [2, 32], P('section')
- grad_out_gain: float32 [2, 2048], P('section')
- grad_out_weight: float32 [2, 2048, 1024], P('section', 'wshard')
The draws below stay inside these ranges and needn't reach their ends.
All inputs are finite; a program needn't handle non-finite values.
Results may differ from the reference program's by a relative error of at most 0.022.
Values may be sent and summed in bfloat16 or wider, within the bound.
A program may use at most 192 MiB of HBM per device.

```python
import jax
import jax.numpy as jnp
from jax import lax

D = 1024
HEADS = 32
KCONV = 4
SPAN = 256
LAYERS = 2
LEN = 2048
SEQS = 8
DI = 2048
PROJ = 4384
CHAN = 2304


def steps_of(own_key, shape, split, low, top_value):
    def one(dim, blocks):
        heights = jax.random.uniform(jax.random.fold_in(jax.random.fold_in(own_key, 6), dim), (blocks,), jnp.float32, low / len(split), top_value / len(split))
        return jnp.repeat(jnp.exp(heights), shape[dim] // blocks).reshape((-1,) + (1,) * (len(shape) - dim - 1))

    level = one(*split[0])
    for cut in split[1:]:
        level = level * one(*cut)
    return level


def normal_values(rng, dims, spread, most, cuts=(), kind=jnp.bfloat16):
    entries = spread * jax.random.normal(rng, dims, jnp.float32)
    if cuts:
        entries = entries * steps_of(rng, dims, cuts, -0.22, 0.18)
    return jnp.clip(entries, -most, most).astype(kind)


def setup_inputs(seed: int = 0) -> dict:
    streams_of = jax.random.split(jax.random.key(seed), 12)
    return {
        "hidden": normal_values(streams_of[0], (SEQS, LEN, D), 1.0, 6.0, ((0, 4), (1, 16))),
        "out_grad": normal_values(streams_of[1], (SEQS, LEN, D), 1.0, 6.0, ((0, 4), (1, 16))),
        "norm_gain": jnp.clip(1.0 + 0.18 * jax.random.normal(streams_of[2], (LAYERS, D), jnp.float32), 0.1, 1.9),
        "in_weight": normal_values(streams_of[3], (LAYERS, D, PROJ), D ** -0.5, 0.1875, ((0, 2), (1, 4))),
        "conv_weight": normal_values(streams_of[4], (LAYERS, KCONV, CHAN), KCONV ** -0.5, 3.0, ((0, 2),), jnp.float32),
        "conv_bias": normal_values(streams_of[5], (LAYERS, CHAN), 0.5, 3.0, ((0, 2),), jnp.float32),
        "dt_bias": jnp.clip(-7.0 + 4.0 * jax.random.uniform(streams_of[6], (LAYERS, HEADS), jnp.float32) ** steps_of(streams_of[6], (LAYERS, HEADS), ((0, 2),), -0.2, 0.2), -7.0, -3.0),
        "a_log": jnp.clip(-1.0 + 3.0 * jax.random.uniform(streams_of[7], (LAYERS, HEADS), jnp.float32) ** steps_of(streams_of[7], (LAYERS, HEADS), ((0, 2),), -0.2, 0.2), -1.0, 2.0),
        "d_skip": normal_values(streams_of[8], (LAYERS, HEADS), 1.0, 4.0, ((0, 2),), jnp.float32),
        "out_gain": jnp.clip(1.0 + 0.18 * jax.random.normal(streams_of[9], (LAYERS, DI), jnp.float32), 0.1, 1.9),
        "out_weight": normal_values(streams_of[10], (LAYERS, DI, D), DI ** -0.5, 0.125, ((0, 2), (1, 4))),
    }


@jax.custom_vjp
def low(v):
    return lax.optimization_barrier(v.astype(jnp.bfloat16)).astype(jnp.float32)

@jax.custom_vjp
def low_back(v):
    return v

def low_keep(v):
    return (low(v), None)

def low_pass(kept, grad):
    return (grad,)

def back_keep(v):
    return (v, None)

def back_low(kept, grad):
    return (low(grad),)
low.defvjp(low_keep, low_pass)
low_back.defvjp(back_keep, back_low)
epsilon = 1e-05
highest = lax.Precision.HIGHEST

def rms_scale(values, gain):
    return values * lax.rsqrt(lax.optimization_barrier(jnp.mean(values * values, axis=-1, keepdims=True)) + epsilon) * gain

def scan_blocks(x_conv, step_size, decay_rates, b_conv, c_conv):
    length, head_count, head_width = x_conv.shape
    states = b_conv.shape[1]
    blocks = length // SPAN
    x_blocks = x_conv.reshape(blocks, SPAN, head_count, head_width)
    step_blocks = step_size.reshape(blocks, SPAN, head_count)
    b_blocks = b_conv.reshape(blocks, SPAN, states)
    c_blocks = c_conv.reshape(blocks, SPAN, states)
    row_ids = jnp.arange(SPAN)
    causal = (row_ids[:, None] >= row_ids[None, :])[None]

    def advance(state_now, pieces):
        x_piece, step_piece, b_piece, c_piece = pieces
        cumulus = jnp.cumsum(step_piece * decay_rates[None, :], axis=0).T
        differ = cumulus[:, :, None] - cumulus[:, None, :]
        decay_mask = jnp.where(causal, jnp.exp(jnp.where(causal, differ, 0.0)), 0.0)
        scores = jnp.dot(c_piece, b_piece.T, precision=highest)
        weights = scores[None] * decay_mask * step_piece.T[:, None, :]
        inner_out = jnp.einsum('hij,jhp->ihp', weights, x_piece, precision=highest)
        carried = jnp.einsum('in,hpn->ihp', c_piece, state_now, precision=highest) * jnp.exp(cumulus).T[:, :, None]
        tail_weight = jnp.exp(cumulus[:, -1:] - cumulus) * step_piece.T
        fresh_state = jnp.einsum('hj,jhp,jn->hpn', tail_weight, x_piece, b_piece, precision=highest)
        new_state = state_now * jnp.exp(cumulus[:, -1])[:, None, None] + fresh_state
        return (new_state, inner_out + carried)
    zero_state = jnp.zeros((head_count, head_width, states), jnp.float32)
    last_state, block_outs = lax.scan(jax.checkpoint(advance), zero_state, (x_blocks, step_blocks, b_blocks, c_blocks))
    return block_outs.reshape(length, head_count, head_width)

def mixer_heads(x_part, bc_part, dt_part, conv_w, conv_b, dt_shift, log_rate, skip_gain):
    length = x_part.shape[0]
    head_count = dt_part.shape[1]
    kernel = conv_w.shape[0]
    states = bc_part.shape[1] // 2
    inner_width = x_part.shape[1]
    joined = jnp.concatenate([x_part, bc_part], axis=1)
    padded = jnp.pad(joined, ((kernel - 1, 0), (0, 0)))
    conv_sum = conv_b[None, :] + sum((conv_w[offset][None, :] * padded[offset:offset + length] for offset in range(kernel)))
    active = jax.nn.silu(conv_sum)
    x_conv = active[:, :inner_width].reshape(length, head_count, inner_width // head_count)
    b_conv = active[:, inner_width:inner_width + states]
    c_conv = active[:, inner_width + states:]
    step_size = jax.nn.softplus(dt_part + dt_shift[None, :])
    decay_rates = -jnp.exp(log_rate)
    mixed_out = scan_blocks(x_conv, step_size, decay_rates, b_conv, c_conv) + skip_gain[None, :, None] * x_conv
    return mixed_out.reshape(length, inner_width)

def layer(inputs, gain_in, w_in, conv_w, conv_b, dt_shift, log_rate, skip_gain, gain_out, w_out):
    inner_width = w_out.shape[0]
    head_count = dt_shift.shape[0]
    states = (w_in.shape[1] - 2 * inner_width - head_count) // 2
    normed = low(rms_scale(inputs, gain_in))
    projected = low_back(jnp.dot(normed, w_in, precision=highest))
    gate_part = projected[:, :inner_width]
    x_part = low_back(low(projected[:, inner_width:2 * inner_width]))
    bc_part = low(projected[:, 2 * inner_width:2 * inner_width + 2 * states])
    dt_part = low_back(low(projected[:, 2 * inner_width + 2 * states:]))
    mixed_out = low_back(low(mixer_heads(x_part, bc_part, dt_part, conv_w, conv_b, dt_shift, log_rate, skip_gain)))
    gated_out = low(rms_scale(mixed_out * jax.nn.silu(gate_part), gain_out))
    branch = low_back(jnp.dot(gated_out, w_out, precision=highest))
    return low(inputs + branch)

def reference(hidden, out_grad, norm_gain, in_weight, conv_weight, conv_bias, dt_bias, a_log, d_skip, out_gain, out_weight):
    params = tuple((param.astype(jnp.float32) for param in (norm_gain, in_weight, conv_weight, conv_bias, dt_bias, a_log, d_skip, out_gain, out_weight)))

    def forward(inputs, probe, stacked):
        first_out = layer(inputs, *[param[0] for param in stacked])
        passed = low_back(first_out + probe)
        second_out = layer(passed, *[param[1] for param in stacked])
        return (second_out, first_out)

    def per_sequence(totals, pair):
        seq_input, seq_grad = pair
        inputs = seq_input.astype(jnp.float32)
        probe = jnp.zeros_like(inputs)
        second_out, pullback, first_out = jax.vjp(forward, inputs, probe, params, has_aux=True)
        grad_input, grad_probe, grad_params = pullback(seq_grad.astype(jnp.float32))
        totals = jax.tree.map(jnp.add, totals, grad_params)
        return (totals, (first_out.astype(jnp.bfloat16), second_out.astype(jnp.bfloat16), grad_input, grad_probe))
    zero_grads = jax.tree.map(jnp.zeros_like, params)
    totals, (firsts, seconds, grad_inputs, grad_probes) = lax.scan(per_sequence, zero_grads, (hidden, out_grad))
    layer_out = jnp.stack([firsts, seconds])
    section_grad = jnp.stack([grad_inputs, grad_probes])
    return (layer_out, section_grad, totals[0], totals[1], totals[2], totals[3], totals[4], totals[5], totals[6], totals[7], totals[8])
```

```python
import functools

import jax
import jax.numpy as jnp
from jax import lax
from jax.experimental import pallas as pl
from jax.experimental.pallas import tpu as pltpu
from jax.sharding import PartitionSpec as P

F32 = jnp.float32
BF16 = jnp.bfloat16
HI = lax.Precision.HIGHEST
EPS = 1e-05
HDIM = 64
LANE = 128
TAIL = 16


def shift(x, axis, by):
    devices = lax.axis_size(axis)
    pairs = [(i, i + by) for i in range(devices) if 0 <= i + by < devices]
    return lax.ppermute(x, axis, pairs)


def swap(x):
    return lax.ppermute(x, "section", [(0, 1), (1, 0)])


def half(a, which):
    width = a.shape[-1] // 8
    b = a.reshape(a.shape[:-1] + (4, 2, width))
    b = lax.dynamic_index_in_dim(b, which, axis=b.ndim - 2, keepdims=False)
    return b.reshape(a.shape[:-1] + (4 * width,))


def whole(own, other, core):
    width = own.shape[-1] // 4
    lead = own.shape[:-1]
    own, other = own.reshape(lead + (4, 1, width)), other.reshape(lead + (4, 1, width))
    first, second = jnp.where(core == 0, own, other), jnp.where(core == 0, other, own)
    return jnp.concatenate([first, second], axis=-2).reshape(lead + (8 * width,))


def mm(a, b):
    return jnp.dot(a.astype(BF16), b.astype(BF16), preferred_element_type=F32)


def mm_nt(a, b):
    return lax.dot_general(
        a.astype(BF16), b.astype(BF16), (((1,), (1,)), ((), ())), preferred_element_type=F32
    )


def mm_tn(a, b):
    return lax.dot_general(
        a.astype(BF16), b.astype(BF16), (((0,), (0,)), ((), ())), preferred_element_type=F32
    )


def spread_matrix(width):
    head = lax.broadcasted_iota(jnp.int32, (LANE, width), 0)
    lane = lax.broadcasted_iota(jnp.int32, (LANE, width), 1)
    return jnp.where(lane // HDIM == head, 1.0, 0.0).astype(F32)


def spread(heads, matrix):
    return jnp.dot(heads, matrix, precision=HI, preferred_element_type=F32)


def gather_heads(lanes, matrix):
    return lax.dot_general(
        lanes, matrix, (((1,), (1,)), ((), ())), precision=HI, preferred_element_type=F32
    )


def tri(rows, upper):
    r = lax.broadcasted_iota(jnp.int32, (rows, rows), 0)
    c = lax.broadcasted_iota(jnp.int32, (rows, rows), 1)
    return jnp.where((c >= r) if upper else (r >= c), 1.0, 0.0).astype(F32)


def steps(dt, hp):
    shifted = dt + hp[0:1, :]
    step = jnp.maximum(shifted, 0.0) + jnp.log1p(jnp.exp(-jnp.abs(shifted)))
    rate = -jnp.exp(hp[1:2, :])
    return shifted, step, rate


def sigmoid(v):
    return 1.0 / (1.0 + jnp.exp(-v))


def conv_pre(buf, cw, cb, taps, rows):
    pre = cb[0:1, :]
    for k in range(taps):
        start = TAIL - (taps - 1) + k
        pre = pre + cw[k : k + 1, :] * buf[start : start + rows, :]
    return pre


def chunk_kernel(taps, xbc, halo, dt, cw, cb, hp, act_o, cum_o, step_o, sloc_o, buf):
    rows, inner = xbc.shape[1], sloc_o.shape[0] * LANE
    buf[0:TAIL, :] = halo[0].astype(F32)
    buf[TAIL : TAIL + rows, :] = xbc[0].astype(F32)
    pre = conv_pre(buf, cw, cb, taps, rows)
    act = pre * sigmoid(pre)
    act_o[0] = act
    _, step, rate = steps(dt[0].astype(F32), hp)
    cum = jnp.dot(tri(rows, False), step * rate, precision=HI, preferred_element_type=F32)
    cum_o[0] = cum
    step_o[0] = step
    last = cum[rows - 1 : rows, :]
    matrix = spread_matrix(inner)
    weight = spread(jnp.exp(last - cum) * step, matrix)
    decay = spread(jnp.broadcast_to(jnp.exp(last), (8, LANE)), matrix)[0:1, :]
    d_hi = decay.astype(BF16).astype(F32)
    d_mid = (decay - d_hi).astype(BF16).astype(F32)
    d_lo = decay - d_hi - d_mid
    row = lax.broadcasted_iota(jnp.int32, (TAIL, inner), 0)
    extra = jnp.where(row == 0, d_hi, jnp.where(row == 1, d_mid, jnp.where(row == 2, d_lo, 0.0)))
    extra = extra.astype(BF16)
    xw = (act[:, :inner] * weight).astype(BF16)
    b = act[:, inner : inner + LANE].astype(BF16)
    sloc = mm_tn(b, xw).astype(BF16)
    states = sloc.shape[0]
    for i in range(inner // LANE):
        sloc_o[i, 0:states, :] = sloc[:, i * LANE : (i + 1) * LANE]
        sloc_o[i, states : states + TAIL, :] = extra[:, i * LANE : (i + 1) * LANE]


def prefix_kernel(reverse, with_decay, r, *refs):
    pieces, states = r.shape[0], refs[-1].shape[1]
    if with_decay:
        decay_o, out = refs
        for j in range(pieces):
            tail = r[j, states : states + TAIL, :].astype(F32)
            decay_o[j : j + 1, :] = tail[0:1, :] + tail[1:2, :] + tail[2:3, :]
        decay = decay_o
    else:
        decay, out = refs
    carry = jnp.zeros((states, LANE), F32)
    order = range(pieces - 1, -1, -1) if reverse else range(pieces)
    for j in order:
        out[j] = carry.astype(BF16)
        carry = carry * decay[j : j + 1, :] + r[j, 0:states, :].astype(F32)


def intra_kernel(act, cum, step, yi_o):
    rows, inner = yi_o.shape[1], yi_o.shape[2]
    b = act[0, :, inner : inner + LANE]
    c = act[0, :, inner + LANE : inner + 2 * LANE]
    cb = mm_nt(c, b)
    cum_v = cum[0]
    cum_t = jnp.transpose(cum_v)
    xs = act[0, :, :inner] * spread(step[0], spread_matrix(inner))
    keep = tri(rows, False) > 0
    low = lax.broadcasted_iota(jnp.int32, (rows, LANE), 1) < HDIM
    for i in range(inner // LANE):
        xs_i = xs[:, i * LANE : (i + 1) * LANE].astype(BF16)
        parts = []
        for h in (2 * i, 2 * i + 1):
            diff = cum_v[:, h : h + 1] - cum_t[h : h + 1, :]
            decay = jnp.exp(jnp.where(keep, diff, -1e30))
            parts.append(mm(cb * decay, xs_i))
        yi_o[0, :, i * LANE : (i + 1) * LANE] = jnp.where(low, parts[0], parts[1])


def finish_kernel(act, cum, yi, sin, z, hp, gain, yy_o, gg_o, ss_o):
    inner = yi.shape[2]
    matrix = spread_matrix(inner)
    grown = spread(jnp.exp(cum[0]), matrix)
    skip = spread(jnp.broadcast_to(hp[2:3, :], (8, LANE)), matrix)[0:1, :]
    c = act[0, :, inner + LANE : inner + 2 * LANE].astype(BF16)
    total = jnp.zeros((yi.shape[1], LANE), F32)
    for i in range(inner // LANE):
        at = slice(i * LANE, (i + 1) * LANE)
        yy = yi[0, :, at] + grown[:, at] * mm(c, sin[i])
        yy_o[0, :, at] = yy
        mixed = (yy + skip[:, at] * act[0, :, at]).astype(BF16).astype(F32)
        zi = z[0, :, at]
        g = mixed * (zi * sigmoid(zi))
        total = total + g * g
        gg_o[0, :, at] = (g * gain[0:1, at]).astype(BF16)
    ss_o[0] = jnp.sum(total, axis=1, keepdims=True)


def gate_back_kernel(
    gr, z, yy, act, cum, rn, rs, hp, gain, dy_o, gz_o, dsl_o, dgain_o, gated_o
):
    inner = gr.shape[2]
    matrix = spread_matrix(inner)
    grown = spread(jnp.exp(cum[0]), matrix)
    skip = spread(jnp.broadcast_to(hp[2:3, :], (8, LANE)), matrix)[0:1, :]
    c = act[0, :, inner + LANE : inner + 2 * LANE].astype(BF16)
    r = rn[0]
    k = r * r * r * rs[0] * (1.0 / (2 * inner))
    for i in range(inner // LANE):
        at = slice(i * LANE, (i + 1) * LANE)
        mixed = (yy[0, :, at] + skip[:, at] * act[0, :, at]).astype(BF16).astype(F32)
        zi = z[0, :, at]
        sg = sigmoid(zi)
        silu = zi * sg
        g = mixed * silu
        gr_i = gr[0, :, at]
        gain_i = gain[0:1, at]
        normal = g * r
        dgain_o[0, :, at] = jnp.broadcast_to(
            jnp.sum(gr_i * normal, axis=0, keepdims=True), (8, LANE)
        )
        gated_o[0, :, at] = (normal * gain_i).astype(BF16)
        dg = r * (gain_i * gr_i) - g * k
        dy = (dg * silu).astype(BF16)
        dy_o[0, :, at] = dy
        gz_o[0, :, at] = (dg * mixed * (sg * (1.0 + zi * (1.0 - sg)))).astype(BF16)
        dsl_o[i] = mm_tn(c, dy.astype(F32) * grown[:, at]).astype(BF16)


def intra_back_kernel(act, cum, step, dy, dxs_o, dbc_o, dcum_o):
    rows, inner = dxs_o.shape[1], dxs_o.shape[2]
    b = act[0, :, inner : inner + LANE].astype(BF16)
    c = act[0, :, inner + LANE : inner + 2 * LANE].astype(BF16)
    cb = mm_nt(c, b)
    cum_v = cum[0]
    cum_t = jnp.transpose(cum_v)
    xs = act[0, :, :inner] * spread(step[0], spread_matrix(inner))
    keep = tri(rows, False) > 0
    low = lax.broadcasted_iota(jnp.int32, (rows, LANE), 1) < HDIM
    dcb = jnp.zeros((rows, rows), F32)
    lane = lax.broadcasted_iota(jnp.int32, (rows, LANE), 1)
    row_sums = jnp.zeros((rows, LANE), F32)
    col_sums = []
    for i in range(inner // LANE):
        at = slice(i * LANE, (i + 1) * LANE)
        xs_i = xs[:, at]
        dy_i = dy[0, :, at].astype(F32)
        parts = []
        for n, h in enumerate((2 * i, 2 * i + 1)):
            diff = cum_v[:, h : h + 1] - cum_t[h : h + 1, :]
            decay = jnp.exp(jnp.where(keep, diff, -1e30))
            mine = jnp.where(low, dy_i, 0.0) if n == 0 else jnp.where(low, 0.0, dy_i)
            flow = mm_nt(mine, xs_i) * decay
            dcb = dcb + flow
            both = flow * cb
            row_sums = jnp.where(lane == h, jnp.sum(both, axis=1, keepdims=True), row_sums)
            col_sums.append(jnp.sum(both, axis=0, keepdims=True))
            parts.append(mm_tn(cb * decay, dy_i))
        dxs_o[0, :, at] = jnp.where(low, parts[0], parts[1])
    col_sums.append(jnp.zeros((LANE - len(col_sums), rows), F32))
    dcum_o[0] = row_sums - jnp.transpose(jnp.concatenate(col_sums, axis=0))
    dbc_o[0, :, 0:LANE] = mm_tn(dcb, c)
    dbc_o[0, :, LANE : 2 * LANE] = mm(dcb, b)


def mix_back_kernel(
    taps, xbc, halo, dt, cw, cb, hp, act, cum, step, dy, dxs, dbc, dci, grad, sin,
    dpre_o, ddt_o, conv_o, head_o, buf, dact,
):
    rows, inner = dy.shape[1], dy.shape[2]
    matrix = spread_matrix(inner)
    cum_v, step_v = cum[0], step[0]
    last = cum_v[rows - 1 : rows, :]
    step_e = spread(step_v, matrix)
    tail_e = spread(jnp.exp(last - cum_v), matrix)
    grown = spread(jnp.exp(cum_v), matrix)
    d_e = grown[rows - 1 : rows, :]
    skip = spread(jnp.broadcast_to(hp[2:3, :], (8, LANE)), matrix)[0:1, :]
    b = act[0, :, inner : inner + LANE].astype(BF16)
    c = act[0, :, inner + LANE : inner + 2 * LANE].astype(BF16)
    q1 = dci[0]
    qb = jnp.zeros((rows, LANE), F32)
    q2 = jnp.zeros((rows, LANE), F32)
    flows = jnp.zeros((8, LANE), F32)
    skips = jnp.zeros((8, LANE), F32)
    db, dc = dbc[0, :, 0:LANE], dbc[0, :, LANE : 2 * LANE]
    for i in range(inner // LANE):
        at = slice(i * LANE, (i + 1) * LANE)
        g = grad[i]
        x = act[0, :, at]
        dy_i = dy[0, :, at].astype(F32)
        s_i = sin[i]
        back = tail_e[:, at] * mm(b, g)
        v = dxs[0, :, at] + back
        dact[:, at] = step_e[:, at] * v + skip[:, at] * dy_i
        part = matrix[:, at]
        q1 = q1 + gather_heads(dy_i * grown[:, at] * mm(c, s_i), part)
        q2 = q2 + gather_heads(x * v, part)
        qb = qb + gather_heads(x * back, part)
        flow = d_e[:, at] * jnp.sum(g.astype(F32) * s_i.astype(F32), axis=0, keepdims=True)
        flows = flows + gather_heads(jnp.broadcast_to(flow, (8, LANE)), part)
        skip_i = jnp.sum(dy_i * x, axis=0, keepdims=True)
        skips = skips + gather_heads(jnp.broadcast_to(skip_i, (8, LANE)), part)
        db = db + mm_nt(tail_e[:, at] * step_e[:, at] * x, g)
        dc = dc + mm_nt(dy_i * grown[:, at], s_i)
    dact[:, inner : inner + LANE] = db
    dact[:, inner + LANE : inner + 2 * LANE] = dc
    shifted, _, rate = steps(dt[0].astype(F32), hp)
    later = jnp.dot(tri(rows, True), q1, precision=HI, preferred_element_type=F32)
    strict = 1.0 - tri(rows, True)
    sooner = jnp.dot(strict, step_v * qb, precision=HI, preferred_element_type=F32)
    da = later + sooner + flows[0:1, :]
    ddt = (q2 + rate * da) * sigmoid(shifted)
    ddt_o[0] = ddt.astype(BF16)
    row = lax.broadcasted_iota(jnp.int32, (8, LANE), 0)
    g_bias = jnp.sum(ddt, axis=0, keepdims=True)
    g_rate = jnp.sum(da * step_v, axis=0, keepdims=True) * rate
    head_o[0] = jnp.where(
        row == 0, g_bias, jnp.where(row == 1, g_rate, jnp.where(row == 2, skips, 0.0))
    )
    buf[0:TAIL, :] = halo[0].astype(F32)
    buf[TAIL : TAIL + rows, :] = xbc[0].astype(F32)
    pre = conv_pre(buf, cw, cb, taps, rows)
    sg = sigmoid(pre)
    dpre = dact[...] * (sg * (1.0 + pre * (1.0 - sg)))
    dpre_o[0] = dpre
    conv_o[0] = jnp.zeros(conv_o.shape[1:], F32)
    for k in range(taps):
        start = TAIL - (taps - 1) + k
        conv_o[0, k : k + 1, :] = jnp.sum(
            dpre * buf[start : start + rows, :], axis=0, keepdims=True
        )
    conv_o[0, taps : taps + 1, :] = jnp.sum(dpre, axis=0, keepdims=True)


def conv_back_kernel(taps, dpre, after, gz, ddt, cw, out, buf):
    rows, chan = dpre.shape[1], dpre.shape[2]
    inner = gz.shape[2]
    buf[0:rows, :] = dpre[0]
    buf[rows : rows + 8, :] = after[0]
    total = cw[taps - 1 : taps, :] * buf[0:rows, :]
    for k in range(taps - 1):
        start = taps - 1 - k
        total = total + cw[k : k + 1, :] * buf[start : start + rows, :]
    out[0, :, 0:inner] = gz[0]
    out[0, :, inner : inner + chan] = total.astype(BF16)
    out[0, :, inner + chan : inner + chan + LANE] = ddt[0]


def per_seq(shape):
    block = (shape[0] // 2,) + shape[1:]
    return pl.BlockSpec(block, lambda s: (s,) + (0,) * (len(shape) - 1))


def same(shape):
    return pl.BlockSpec(shape, lambda s: (0,) * len(shape))


def run(kernel, ins, outs, scratch=(), shared=()):
    return pl.pallas_call(
        kernel,
        grid=(2,),
        in_specs=[(same if n in shared else per_seq)(a.shape) for n, a in enumerate(ins)],
        out_specs=[per_seq(o.shape) for o in outs],
        out_shape=list(outs),
        scratch_shapes=list(scratch),
        compiler_params=pltpu.CompilerParams(vmem_limit_bytes=40 * 2**20),
    )(*ins)


def sds(shape, dtype):
    return jax.ShapeDtypeStruct(shape, dtype)


def prefix(r, decay, reverse, states):
    pieces = r.shape[0]
    out = sds((pieces, states, LANE), BF16)
    params = pltpu.CompilerParams(vmem_limit_bytes=40 * 2**20)
    if decay is None:
        return pl.pallas_call(
            functools.partial(prefix_kernel, reverse, True),
            out_shape=[sds((pieces, LANE), F32), out],
            compiler_params=params,
        )(r)
    return decay, pl.pallas_call(
        functools.partial(prefix_kernel, reverse, False), out_shape=out, compiler_params=params
    )(r, decay)


def exchange(x):
    return lax.all_to_all(x, "seq", split_axis=0, concat_axis=0, tiled=True)


def forward(u, w_in, w_out, p):
    gain_in, cw, cb, hp, gain_out = p
    seqs, rows, width = u.shape
    chan = cw.shape[1]
    taps = 4
    inner = gain_out.shape[1]
    states = LANE
    heads = inner // HDIM
    uf = u.astype(F32)
    inv = lax.rsqrt(jnp.mean(uf * uf, axis=-1, keepdims=True) + EPS)
    normed = (uf * inv * gain_in).astype(BF16).reshape(seqs * rows, width)
    proj = jnp.dot(normed, w_in, preferred_element_type=F32).reshape(seqs, rows, -1)
    z = proj[:, :, :inner]
    xbc = proj[:, :, inner : inner + chan].astype(BF16)
    dt = jnp.pad(
        proj[:, :, inner + chan : inner + chan + heads].astype(BF16),
        ((0, 0), (0, 0), (0, LANE - heads)),
    )
    halo = shift(xbc[:, rows - TAIL :], "seq", 1)
    act, cum, step, sloc = run(
        functools.partial(chunk_kernel, taps),
        (xbc, halo, dt, cw, cb, hp),
        (
            sds((seqs, rows, chan), F32),
            sds((seqs, rows, LANE), F32),
            sds((seqs, rows, LANE), F32),
            sds((seqs * inner // LANE, states + TAIL, LANE), BF16),
        ),
        [pltpu.VMEM((TAIL + rows, chan), F32)],
        (3, 4, 5),
    )
    moved = exchange(sloc)
    (yi,) = run(intra_kernel, (act, cum, step), (sds((seqs, rows, inner), F32),))
    decay, states_in = prefix(moved, None, False, states)
    sin = exchange(states_in)
    yy, gg, ss = run(
        finish_kernel,
        (act, cum, yi, sin, z, hp, gain_out),
        (
            sds((seqs, rows, inner), F32),
            sds((seqs, rows, inner), BF16),
            sds((seqs, rows, 1), F32),
        ),
        (),
        (5, 6),
    )
    mine = jnp.dot(gg.reshape(seqs * rows, inner), w_out, preferred_element_type=F32)
    mine = mine.astype(BF16).reshape(seqs, rows, width)
    theirs, ss_theirs = swap(mine), swap(ss)
    branch = mine.astype(F32) + theirs.astype(F32)
    rn = lax.rsqrt((ss + ss_theirs) * (1.0 / (2 * inner)) + EPS)
    result = (uf + rn * branch).astype(BF16)
    kept = (u, inv, normed, z, xbc, halo, dt, act, cum, step, decay, sin, yy, branch, rn)
    return result, kept


def backward(e, kept, w_in, w_out, p):
    gain_in, cw, cb, hp, gain_out = p
    u, inv, normed, z, xbc, halo, dt, act, cum, step, decay, sin, yy, branch, rn = kept
    seqs, rows, width = e.shape
    chan = cw.shape[1]
    taps = 4
    inner = gain_out.shape[1]
    states = LANE
    ef = e.astype(F32)
    e2 = e.reshape(seqs * rows, width)
    nt = (((1,), (1,)), ((), ()))
    tn = (((0,), (0,)), ((), ()))
    gr = lax.dot_general(e2, w_out, nt, preferred_element_type=F32).reshape(seqs, rows, inner)
    rs = jnp.sum(ef * branch, axis=-1, keepdims=True)
    dy, gz, dsl, dgain, gated = run(
        gate_back_kernel,
        (gr, z, yy, act, cum, rn, rs, hp, gain_out),
        (
            sds((seqs, rows, inner), BF16),
            sds((seqs, rows, inner), BF16),
            sds((seqs * inner // LANE, states, LANE), BF16),
            sds((seqs, 8, inner), F32),
            sds((seqs, rows, inner), BF16),
        ),
        (),
        (7, 8),
    )
    moved = exchange(dsl)
    dxs, dbc, dci = run(
        intra_back_kernel,
        (act, cum, step, dy),
        (
            sds((seqs, rows, inner), F32),
            sds((seqs, rows, 2 * LANE), F32),
            sds((seqs, rows, LANE), F32),
        ),
    )
    _, grads_in = prefix(moved, decay, True, states)
    grad = exchange(grads_in)
    dpre, ddt, conv_g, head_g = run(
        functools.partial(mix_back_kernel, taps),
        (xbc, halo, dt, cw, cb, hp, act, cum, step, dy, dxs, dbc, dci, grad, sin),
        (
            sds((seqs, rows, chan), F32),
            sds((seqs, rows, LANE), BF16),
            sds((seqs, 8, chan), F32),
            sds((seqs, 8, LANE), F32),
        ),
        [pltpu.VMEM((TAIL + rows, chan), F32), pltpu.VMEM((rows, chan), F32)],
        (3, 4, 5),
    )
    after = shift(dpre[:, :8], "seq", -1)
    (gp,) = run(
        functools.partial(conv_back_kernel, taps),
        (dpre, after, gz, ddt, cw),
        (sds((seqs, rows, inner + chan + LANE), BF16),),
        [pltpu.VMEM((rows + 8, chan), F32)],
        (4,),
    )
    gp = gp.reshape(seqs * rows, -1)[:, : w_in.shape[1]]
    mine = lax.dot_general(gp, w_in, nt, preferred_element_type=F32)
    mine = mine.astype(BF16).reshape(seqs, rows, width)
    theirs = swap(mine)
    gn = mine.astype(F32) + theirs.astype(F32)
    uf = u.astype(F32)
    unit = uf * inv
    g_gain_in = jnp.sum(gn * unit, axis=(0, 1))
    scaled = gn * gain_in
    dot = jnp.mean(scaled * unit, axis=-1, keepdims=True)
    grad_u = ef + inv * (scaled - unit * dot)
    g_in = lax.dot_general(normed, gp, tn, preferred_element_type=F32)
    g_out = lax.dot_general(
        gated.reshape(seqs * rows, inner), e2, tn, preferred_element_type=F32
    )
    products = jnp.concatenate([g_in, g_out], axis=1).astype(BF16)
    heads = inner // HDIM
    conv_sum, head_sum = conv_g.sum(0), head_g.sum(0)
    smalls = (
        g_gain_in,
        conv_sum[: taps + 1, :inner],
        conv_sum[: taps + 1, inner:],
        head_sum[:3, :heads],
        dgain.sum(0)[0],
    )
    return grad_u, products, smalls


def body(
    hidden, out_grad, norm_gain, in_weight, conv_weight, conv_bias, dt_bias, a_log, d_skip,
    out_gain, out_weight,
):
    core = lax.axis_index("section")
    width = hidden.shape[2]
    full = out_gain.shape[1]
    taps = conv_weight.shape[1]
    head_count = dt_bias.shape[1]
    proj = in_weight.shape[2]
    bc_at, dt_at = 2 * full, proj - head_count

    wi, wo = in_weight[0], out_weight[0]

    def pack(which):
        out_rows = wo.reshape(2, wo.shape[0] // 2, wo.shape[1])
        return jnp.concatenate(
            [
                half(wi[:, :full], which),
                half(wi[:, full:bc_at], which),
                wi[:, bc_at:dt_at],
                half(wi[:, dt_at:], which),
            ],
            axis=1,
        ), lax.dynamic_index_in_dim(out_rows, which, 0, keepdims=False)

    own, sent = pack(core), pack(1 - core)
    came = jax.tree.map(swap, sent)
    sizes = (norm_gain, conv_weight, conv_bias, dt_bias, a_log, d_skip, out_gain)
    flat = jnp.concatenate([a[0].reshape(-1) for a in sizes])
    flat_other = swap(flat)

    def params(layer):
        mine = core == layer
        w_in = jnp.where(mine, own[0], came[0])
        w_out = jnp.where(mine, own[1], came[1])
        w_in = lax.all_gather(w_in, "wshard", axis=0, tiled=True)
        w_out = lax.all_gather(w_out, "wshard", axis=0, tiled=True)
        v = jnp.where(mine, flat, flat_other)
        parts, at = [], 0
        for a in sizes:
            count = a[0].size
            parts.append(v[at : at + count].reshape(a[0].shape))
            at += count
        gain_in, cw, cb, dtb, al, ds, gain_out = parts

        def channels(a):
            return jnp.concatenate([half(a[..., :full], core), a[..., full:]], axis=-1)

        hp = jnp.stack([half(a, core) for a in (dtb, al, ds)])
        hp = jnp.pad(hp, ((0, 5), (0, LANE - hp.shape[1])))
        cw = jnp.pad(channels(cw), ((0, 8 - taps), (0, 0)))
        return w_in, w_out, (
            gain_in[None],
            cw,
            channels(cb)[None],
            hp,
            half(gain_out, core)[None],
        )

    w_in0, w_out0, p0 = params(0)
    w_in1, w_out1, p1 = params(1)
    first, kept0 = forward(hidden, w_in0, w_out0, p0)
    second, kept1 = forward(first, w_in1, w_out1, p1)
    layer_out = jnp.where(core == 0, first, second)[None]
    grad1, products1, smalls1 = backward(out_grad, kept1, w_in1, w_out1, p1)
    passed = grad1.astype(BF16)
    grad0, products0, smalls0 = backward(passed, kept0, w_in0, w_out0, p0)
    section_grad = jnp.where(core == 0, grad0, passed.astype(F32))[None]

    columns = products0.shape[1]

    def owned(products):
        part = lax.psum_scatter(products, "wshard", scatter_dimension=0, tiled=True)
        part = part.astype(BF16)
        return part

    seq_count = lax.axis_size("seq")
    rows = width // lax.axis_size("wshard") // seq_count
    both = jnp.concatenate(
        [owned(p).reshape(seq_count, rows, columns) for p in (products0, products1)], axis=1
    )
    moved = exchange(both)
    piece = moved.astype(F32).sum(0).astype(BF16).reshape(2, rows, columns)
    mine = lax.dynamic_index_in_dim(piece, core, 0, keepdims=False)
    other = swap(lax.dynamic_index_in_dim(piece, 1 - core, 0, keepdims=False))
    inner = full // 2
    at = (0, inner, 2 * inner, 2 * inner + (dt_at - bc_at), columns - width, columns)
    cut_mine = [mine[:, a:b] for a, b in zip(at, at[1:])]
    cut_other = [other[:, a:b] for a, b in zip(at, at[1:])]
    zg, xg, dg = (whole(cut_mine[n], cut_other[n], core) for n in (0, 1, 3))
    bcg = (cut_mine[2].astype(F32) + cut_other[2].astype(F32)).astype(BF16)
    low_half = jnp.where(core == 0, cut_mine[4], cut_other[4])
    high_half = jnp.where(core == 0, cut_other[4], cut_mine[4])
    ready = jnp.concatenate([zg, xg, bcg, dg, low_half, high_half], axis=1)
    everyone = lax.all_gather(ready, "seq", axis=0, tiled=True)
    grad_w_in = everyone[:, :proj].astype(F32)
    grad_w_out = jnp.concatenate(
        [everyone[:, proj : proj + width], everyone[:, proj + width :]], axis=0
    ).astype(F32)

    small_mine = jax.tree.map(lambda a, b: jnp.where(core == 0, a, b), smalls0, smalls1)
    small_send = jax.tree.map(lambda a, b: jnp.where(core == 0, b, a), smalls0, smalls1)
    shapes = [a.shape for a in small_send]
    flat_send = swap(jnp.concatenate([a.reshape(-1) for a in small_send]))
    small_other, pos = [], 0
    for shape in shapes:
        count = 1
        for n in shape:
            count *= n
        small_other.append(flat_send[pos : pos + count].reshape(shape))
        pos += count
    vector = jnp.concatenate(
        [
            small_mine[0],
            jnp.concatenate(
                [
                    whole(small_mine[1], small_other[1], core),
                    small_mine[2] + small_other[2],
                ],
                axis=1,
            ).reshape(-1),
            whole(small_mine[3], small_other[3], core).reshape(-1),
            whole(small_mine[4], small_other[4], core),
        ]
    )
    share = -(-vector.size // (seq_count * 1024)) * 1024
    vector = jnp.pad(vector, (0, seq_count * share - vector.size)).reshape(seq_count, share)
    part = exchange(vector).sum(0)
    parts = lax.all_gather(part, ("seq", "wshard"), axis=0)
    vector = parts.reshape(seq_count, -1, share).sum(1).reshape(-1)
    chan = full + dt_at - bc_at
    cuts = (width, taps * chan, chan, head_count, head_count, head_count, full)
    small, pos = [], 0
    for count in cuts:
        small.append(vector[pos : pos + count])
        pos += count
    return (
        layer_out,
        section_grad,
        small[0][None],
        grad_w_in[None],
        small[1].reshape(1, taps, chan),
        small[2][None],
        small[3][None],
        small[4][None],
        small[5][None],
        small[6][None],
        grad_w_out[None],
    )


def solution(mesh):
    by_layer = P("section", None)
    weights = P("section", "wshard", None)
    tokens = P("wshard", "seq", None)
    stacked = P("section", "wshard", "seq", None)
    conv = P("section", None, None)
    in_specs = (
        tokens, tokens, by_layer, weights, conv, by_layer, by_layer, by_layer, by_layer, by_layer,
        weights,
    )
    out_specs = (
        stacked, stacked, by_layer, weights, conv, by_layer, by_layer, by_layer, by_layer,
        by_layer, weights,
    )
    return jax.shard_map(body, mesh=mesh, in_specs=in_specs, out_specs=out_specs, check_vma=False)
```

```python
import functools

import jax
import jax.numpy as jnp
from jax import lax
from jax.experimental import pallas as pl
from jax.experimental.pallas import tpu as pltpu
from jax.sharding import PartitionSpec as P

F32 = jnp.float32
BF16 = jnp.bfloat16
HI = lax.Precision.HIGHEST
EPS = 1e-05
HDIM = 64
LANE = 128
TAIL = 16


def shift(x, axis, by):
    devices = lax.axis_size(axis)
    pairs = [(i, i + by) for i in range(devices) if 0 <= i + by < devices]
    return lax.ppermute(x, axis, pairs)


def swap(x):
    return lax.ppermute(x, "section", [(0, 1), (1, 0)])


def half(a, which):
    width = a.shape[-1] // 8
    b = a.reshape(a.shape[:-1] + (4, 2, width))
    b = lax.dynamic_index_in_dim(b, which, axis=b.ndim - 2, keepdims=False)
    return b.reshape(a.shape[:-1] + (4 * width,))


def whole(own, other, core):
    width = own.shape[-1] // 4
    lead = own.shape[:-1]
    own, other = own.reshape(lead + (4, 1, width)), other.reshape(lead + (4, 1, width))
    first, second = jnp.where(core == 0, own, other), jnp.where(core == 0, other, own)
    return jnp.concatenate([first, second], axis=-2).reshape(lead + (8 * width,))


def mm(a, b):
    return jnp.dot(a.astype(BF16), b.astype(BF16), preferred_element_type=F32)


def mm_nt(a, b):
    return lax.dot_general(
        a.astype(BF16), b.astype(BF16), (((1,), (1,)), ((), ())), preferred_element_type=F32
    )


def mm_tn(a, b):
    return lax.dot_general(
        a.astype(BF16), b.astype(BF16), (((0,), (0,)), ((), ())), preferred_element_type=F32
    )


def spread_matrix(width):
    head = lax.broadcasted_iota(jnp.int32, (LANE, width), 0)
    lane = lax.broadcasted_iota(jnp.int32, (LANE, width), 1)
    return jnp.where(lane // HDIM == head, 1.0, 0.0).astype(F32)


def spread(heads, matrix):
    return jnp.dot(heads, matrix, precision=HI, preferred_element_type=F32)


def gather_heads(lanes, matrix):
    return lax.dot_general(
        lanes, matrix, (((1,), (1,)), ((), ())), precision=HI, preferred_element_type=F32
    )


def tri(rows, upper):
    r = lax.broadcasted_iota(jnp.int32, (rows, rows), 0)
    c = lax.broadcasted_iota(jnp.int32, (rows, rows), 1)
    return jnp.where((c >= r) if upper else (r >= c), 1.0, 0.0).astype(F32)


def steps(dt, hp):
    shifted = dt + hp[0:1, :]
    step = jnp.maximum(shifted, 0.0) + jnp.log1p(jnp.exp(-jnp.abs(shifted)))
    rate = -jnp.exp(hp[1:2, :])
    return shifted, step, rate


def sigmoid(v):
    return 1.0 / (1.0 + jnp.exp(-v))


def conv_pre(buf, cw, cb, taps, rows):
    pre = cb[0:1, :]
    for k in range(taps):
        start = TAIL - (taps - 1) + k
        pre = pre + cw[k : k + 1, :] * buf[start : start + rows, :]
    return pre


MESH = pl.DeviceIdType.MESH


class Sender:
    def __init__(self, send, recv):
        self.send, self.recv, self.used = send, recv, 0

    def start(self, src, dst, device):
        n = self.used
        self.used += 1
        copy = pltpu.make_async_remote_copy(
            src_ref=src,
            dst_ref=dst,
            send_sem=self.send.at[n],
            recv_sem=self.recv.at[n],
            device_id=device,
            device_id_type=MESH,
        )
        copy.start()
        return copy


def greet(devices):
    barrier = pltpu.get_barrier_semaphore()
    for device in devices:
        pl.semaphore_signal(barrier, inc=1, device_id=device, device_id_type=MESH)
    pl.semaphore_wait(barrier, len(devices))


def chunk_kernel(taps, xd, halo, cw, cb, hp, act_o, cum_o, step_o, sloc_o, buf):
    rows, inner, chan = xd.shape[1], sloc_o.shape[0] * LANE, cw.shape[1]
    buf[0:TAIL, :] = halo[0].astype(F32)
    buf[TAIL : TAIL + rows, :] = xd[0, :, 0:chan].astype(F32)
    pre = conv_pre(buf, cw, cb, taps, rows)
    act = pre * sigmoid(pre)
    act_o[0] = act
    _, step, rate = steps(xd[0, :, chan : chan + LANE].astype(F32), hp)
    cum = jnp.dot(tri(rows, False), step * rate, precision=HI, preferred_element_type=F32)
    cum_o[0] = cum
    step_o[0] = step
    last = cum[rows - 1 : rows, :]
    matrix = spread_matrix(inner)
    weight = spread(jnp.exp(last - cum) * step, matrix)
    decay = spread(jnp.broadcast_to(jnp.exp(last), (8, LANE)), matrix)[0:1, :]
    d_hi = decay.astype(BF16).astype(F32)
    d_mid = (decay - d_hi).astype(BF16).astype(F32)
    d_lo = decay - d_hi - d_mid
    row = lax.broadcasted_iota(jnp.int32, (TAIL, inner), 0)
    extra = jnp.where(row == 0, d_hi, jnp.where(row == 1, d_mid, jnp.where(row == 2, d_lo, 0.0)))
    extra = extra.astype(BF16)
    xw = (act[:, :inner] * weight).astype(BF16)
    b = act[:, inner : inner + LANE].astype(BF16)
    sloc = mm_tn(b, xw).astype(BF16)
    states = sloc.shape[0]
    for i in range(inner // LANE):
        sloc_o[i, 0:states, :] = sloc[:, i * LANE : (i + 1) * LANE]
        sloc_o[i, states : states + TAIL, :] = extra[:, i * LANE : (i + 1) * LANE]


def scan_kernel(reverse, with_decay, pieces_ref, *refs):
    if with_decay:
        decay, out, got, done, send_a, recv_a, send_b, recv_b = refs
    else:
        decay, out, got, done, send_a, recv_a, send_b, recv_b = refs
    count, states = out.shape[0], out.shape[1]
    q = lax.axis_index("seq")
    peers = [lax.rem(q + d, count) for d in range(1, count)]
    greet([{"seq": p} for p in peers])

    def copy(src, dst, send, recv, n, peer, slot):
        return pltpu.make_async_remote_copy(
            src_ref=src.at[peer],
            dst_ref=dst.at[slot],
            send_sem=send.at[n],
            recv_sem=recv.at[slot],
            device_id={"seq": peer},
            device_id_type=MESH,
        )

    sent = [copy(pieces_ref, got, send_a, recv_a, n, p, q) for n, p in enumerate(peers)]
    for c in sent:
        c.start()
    got[q] = pieces_ref[q]
    for n, p in enumerate(peers):
        copy(pieces_ref, got, send_a, recv_a, n, p, p).wait_recv()
    carry = jnp.zeros((states, LANE), F32)
    order = range(count - 1, -1, -1) if reverse else range(count)
    for j in order:
        if with_decay:
            tail = got[j, states : states + TAIL, :].astype(F32)
            decay[j : j + 1, :] = tail[0:1, :] + tail[1:2, :] + tail[2:3, :]
        done[j] = carry.astype(BF16)
        carry = carry * decay[j : j + 1, :] + got[j, 0:states, :].astype(F32)
    back = [copy(done, out, send_b, recv_b, n, p, q) for n, p in enumerate(peers)]
    for c in back:
        c.start()
    out[q] = done[q]
    for n, p in enumerate(peers):
        copy(done, out, send_b, recv_b, n, p, p).wait_recv()
    for c in sent + back:
        c.wait_send()


def intra_kernel(act, cum, step, yi_o):
    rows, inner = yi_o.shape[1], yi_o.shape[2]
    b = act[0, :, inner : inner + LANE]
    c = act[0, :, inner + LANE : inner + 2 * LANE]
    cb = mm_nt(c, b)
    cum_v = cum[0]
    cum_t = jnp.transpose(cum_v)
    xs = act[0, :, :inner] * spread(step[0], spread_matrix(inner))
    keep = tri(rows, False) > 0
    low = lax.broadcasted_iota(jnp.int32, (rows, LANE), 1) < HDIM
    for i in range(inner // LANE):
        xs_i = xs[:, i * LANE : (i + 1) * LANE].astype(BF16)
        parts = []
        for h in (2 * i, 2 * i + 1):
            diff = cum_v[:, h : h + 1] - cum_t[h : h + 1, :]
            decay = jnp.exp(jnp.where(keep, diff, -1e30))
            parts.append(mm(cb * decay, xs_i))
        yi_o[0, :, i * LANE : (i + 1) * LANE] = jnp.where(low, parts[0], parts[1])


def finish_kernel(act, cum, yi, sin, z, hp, gain, yy_o, gg_o, ss_o):
    inner = yi.shape[2]
    matrix = spread_matrix(inner)
    grown = spread(jnp.exp(cum[0]), matrix)
    skip = spread(jnp.broadcast_to(hp[2:3, :], (8, LANE)), matrix)[0:1, :]
    c = act[0, :, inner + LANE : inner + 2 * LANE].astype(BF16)
    total = jnp.zeros((yi.shape[1], LANE), F32)
    for i in range(inner // LANE):
        at = slice(i * LANE, (i + 1) * LANE)
        yy = yi[0, :, at] + grown[:, at] * mm(c, sin[i])
        yy_o[0, :, at] = yy
        mixed = (yy + skip[:, at] * act[0, :, at]).astype(BF16).astype(F32)
        zi = z[0, :, at]
        g = mixed * (zi * sigmoid(zi))
        total = total + g * g
        gg_o[0, :, at] = (g * gain[0:1, at]).astype(BF16)
    ss_o[0] = jnp.sum(total, axis=1, keepdims=True)


def gate_back_kernel(
    gr, z, yy, act, cum, rn, rs, hp, gain, dy_o, gz_o, dsl_o, dgain_o, gated_o
):
    inner = gr.shape[2]
    matrix = spread_matrix(inner)
    grown = spread(jnp.exp(cum[0]), matrix)
    skip = spread(jnp.broadcast_to(hp[2:3, :], (8, LANE)), matrix)[0:1, :]
    c = act[0, :, inner + LANE : inner + 2 * LANE].astype(BF16)
    r = rn[0]
    k = r * r * r * rs[0] * (1.0 / (2 * inner))
    for i in range(inner // LANE):
        at = slice(i * LANE, (i + 1) * LANE)
        mixed = (yy[0, :, at] + skip[:, at] * act[0, :, at]).astype(BF16).astype(F32)
        zi = z[0, :, at]
        sg = sigmoid(zi)
        silu = zi * sg
        g = mixed * silu
        gr_i = gr[0, :, at]
        gain_i = gain[0:1, at]
        normal = g * r
        dgain_o[0, :, at] = jnp.broadcast_to(
            jnp.sum(gr_i * normal, axis=0, keepdims=True), (8, LANE)
        )
        gated_o[0, :, at] = (normal * gain_i).astype(BF16)
        dg = r * (gain_i * gr_i) - g * k
        dy = (dg * silu).astype(BF16)
        dy_o[0, :, at] = dy
        gz_o[0, :, at] = (dg * mixed * (sg * (1.0 + zi * (1.0 - sg)))).astype(BF16)
        dsl_o[i] = mm_tn(c, dy.astype(F32) * grown[:, at]).astype(BF16)


def intra_back_kernel(act, cum, step, dy, dxs_o, dbc_o, dcum_o):
    rows, inner = dxs_o.shape[1], dxs_o.shape[2]
    b = act[0, :, inner : inner + LANE].astype(BF16)
    c = act[0, :, inner + LANE : inner + 2 * LANE].astype(BF16)
    cb = mm_nt(c, b)
    cum_v = cum[0]
    cum_t = jnp.transpose(cum_v)
    xs = act[0, :, :inner] * spread(step[0], spread_matrix(inner))
    keep = tri(rows, False) > 0
    low = lax.broadcasted_iota(jnp.int32, (rows, LANE), 1) < HDIM
    dcb = jnp.zeros((rows, rows), F32)
    lane = lax.broadcasted_iota(jnp.int32, (rows, LANE), 1)
    row_sums = jnp.zeros((rows, LANE), F32)
    col_sums = []
    for i in range(inner // LANE):
        at = slice(i * LANE, (i + 1) * LANE)
        xs_i = xs[:, at]
        dy_i = dy[0, :, at].astype(F32)
        parts = []
        for n, h in enumerate((2 * i, 2 * i + 1)):
            diff = cum_v[:, h : h + 1] - cum_t[h : h + 1, :]
            decay = jnp.exp(jnp.where(keep, diff, -1e30))
            mine = jnp.where(low, dy_i, 0.0) if n == 0 else jnp.where(low, 0.0, dy_i)
            flow = mm_nt(mine, xs_i) * decay
            dcb = dcb + flow
            both = flow * cb
            row_sums = jnp.where(lane == h, jnp.sum(both, axis=1, keepdims=True), row_sums)
            col_sums.append(jnp.sum(both, axis=0, keepdims=True))
            parts.append(mm_tn(cb * decay, dy_i))
        dxs_o[0, :, at] = jnp.where(low, parts[0], parts[1])
    col_sums.append(jnp.zeros((LANE - len(col_sums), rows), F32))
    dcum_o[0] = row_sums - jnp.transpose(jnp.concatenate(col_sums, axis=0))
    dbc_o[0, :, 0:LANE] = mm_tn(dcb, c)
    dbc_o[0, :, LANE : 2 * LANE] = mm(dcb, b)


def mix_back_kernel(
    taps, xd, halo, cw, cb, hp, act, cum, step, dy, dxs, dbc, dci, grad, sin,
    dpre_o, ddt_o, conv_o, head_o, buf, dact,
):
    rows, inner, chan = dy.shape[1], dy.shape[2], cw.shape[1]
    matrix = spread_matrix(inner)
    cum_v, step_v = cum[0], step[0]
    last = cum_v[rows - 1 : rows, :]
    step_e = spread(step_v, matrix)
    tail_e = spread(jnp.exp(last - cum_v), matrix)
    grown = spread(jnp.exp(cum_v), matrix)
    d_e = grown[rows - 1 : rows, :]
    skip = spread(jnp.broadcast_to(hp[2:3, :], (8, LANE)), matrix)[0:1, :]
    b = act[0, :, inner : inner + LANE].astype(BF16)
    c = act[0, :, inner + LANE : inner + 2 * LANE].astype(BF16)
    q1 = dci[0]
    qb = jnp.zeros((rows, LANE), F32)
    q2 = jnp.zeros((rows, LANE), F32)
    flows = jnp.zeros((8, LANE), F32)
    skips = jnp.zeros((8, LANE), F32)
    db, dc = dbc[0, :, 0:LANE], dbc[0, :, LANE : 2 * LANE]
    for i in range(inner // LANE):
        at = slice(i * LANE, (i + 1) * LANE)
        g = grad[i]
        x = act[0, :, at]
        dy_i = dy[0, :, at].astype(F32)
        s_i = sin[i]
        back = tail_e[:, at] * mm(b, g)
        v = dxs[0, :, at] + back
        dact[:, at] = step_e[:, at] * v + skip[:, at] * dy_i
        part = matrix[:, at]
        q1 = q1 + gather_heads(dy_i * grown[:, at] * mm(c, s_i), part)
        q2 = q2 + gather_heads(x * v, part)
        qb = qb + gather_heads(x * back, part)
        flow = d_e[:, at] * jnp.sum(g.astype(F32) * s_i.astype(F32), axis=0, keepdims=True)
        flows = flows + gather_heads(jnp.broadcast_to(flow, (8, LANE)), part)
        skip_i = jnp.sum(dy_i * x, axis=0, keepdims=True)
        skips = skips + gather_heads(jnp.broadcast_to(skip_i, (8, LANE)), part)
        db = db + mm_nt(tail_e[:, at] * step_e[:, at] * x, g)
        dc = dc + mm_nt(dy_i * grown[:, at], s_i)
    dact[:, inner : inner + LANE] = db
    dact[:, inner + LANE : inner + 2 * LANE] = dc
    shifted, _, rate = steps(xd[0, :, chan : chan + LANE].astype(F32), hp)
    later = jnp.dot(tri(rows, True), q1, precision=HI, preferred_element_type=F32)
    strict = 1.0 - tri(rows, True)
    sooner = jnp.dot(strict, step_v * qb, precision=HI, preferred_element_type=F32)
    da = later + sooner + flows[0:1, :]
    ddt = (q2 + rate * da) * sigmoid(shifted)
    ddt_o[0] = ddt.astype(BF16)
    row = lax.broadcasted_iota(jnp.int32, (8, LANE), 0)
    g_bias = jnp.sum(ddt, axis=0, keepdims=True)
    g_rate = jnp.sum(da * step_v, axis=0, keepdims=True) * rate
    head_o[0] = jnp.where(
        row == 0, g_bias, jnp.where(row == 1, g_rate, jnp.where(row == 2, skips, 0.0))
    )
    buf[0:TAIL, :] = halo[0].astype(F32)
    buf[TAIL : TAIL + rows, :] = xd[0, :, 0:chan].astype(F32)
    pre = conv_pre(buf, cw, cb, taps, rows)
    sg = sigmoid(pre)
    dpre = dact[...] * (sg * (1.0 + pre * (1.0 - sg)))
    dpre_o[0] = dpre
    conv_o[0] = jnp.zeros(conv_o.shape[1:], F32)
    for k in range(taps):
        start = TAIL - (taps - 1) + k
        conv_o[0, k : k + 1, :] = jnp.sum(
            dpre * buf[start : start + rows, :], axis=0, keepdims=True
        )
    conv_o[0, taps : taps + 1, :] = jnp.sum(dpre, axis=0, keepdims=True)


def conv_back_kernel(taps, dpre, after, ddt, cw, out, buf):
    rows, chan = dpre.shape[1], dpre.shape[2]
    buf[0:rows, :] = dpre[0]
    buf[rows : rows + 8, :] = after[0]
    total = cw[taps - 1 : taps, :] * buf[0:rows, :]
    for k in range(taps - 1):
        start = taps - 1 - k
        total = total + cw[k : k + 1, :] * buf[start : start + rows, :]
    out[0, :, 0:chan] = total.astype(BF16)
    out[0, :, chan : chan + LANE] = ddt[0]


def per_seq(shape):
    block = (shape[0] // 2,) + shape[1:]
    return pl.BlockSpec(block, lambda s: (s,) + (0,) * (len(shape) - 1))


def same(shape):
    return pl.BlockSpec(shape, lambda s: (0,) * len(shape))


def run(kernel, ins, outs, scratch=(), shared=()):
    return pl.pallas_call(
        kernel,
        grid=(2,),
        in_specs=[(same if n in shared else per_seq)(a.shape) for n, a in enumerate(ins)],
        out_specs=[per_seq(o.shape) for o in outs],
        out_shape=list(outs),
        scratch_shapes=list(scratch),
        compiler_params=pltpu.CompilerParams(vmem_limit_bytes=40 * 2**20),
    )(*ins)


def sds(shape, dtype):
    return jax.ShapeDtypeStruct(shape, dtype)


def scan_chunks(pieces, decay, reverse, states):
    count, height = pieces.shape[0], pieces.shape[1]
    place = pl.BlockSpec(memory_space=pltpu.VMEM)
    out = sds((count, states, LANE), BF16)
    outs = [sds((count, LANE), F32), out] if decay is None else [out]
    ins = (pieces,) if decay is None else (pieces, decay)
    sems = [pltpu.SemaphoreType.DMA((count,))] * 4
    return pl.pallas_call(
        functools.partial(scan_kernel, reverse, decay is None),
        out_shape=outs,
        in_specs=[place] * len(ins),
        out_specs=[place] * len(outs),
        scratch_shapes=[
            pltpu.VMEM((count, height, LANE), BF16),
            pltpu.VMEM((count, states, LANE), BF16),
            *sems,
        ],
        compiler_params=pltpu.CompilerParams(
            collective_id=1 + reverse, has_side_effects=True, vmem_limit_bytes=40 * 2**20
        ),
    )(*ins)


def assemble_kernel(head_count, core, e, l, eo, lo, in_o, out_o):
    rows, full = e.shape[0], e.shape[1]
    inner = full // 2
    wide = 2 * inner // 8
    bc = l.shape[1] - inner - LANE
    zero = core[0] == 0
    for n in range(4):
        src = slice(n * wide, (n + 1) * wide)
        for base, a, b in ((0, e, eo), (2 * inner, l, lo)):
            mine, other = a[:, src].astype(F32), b[:, src].astype(F32)
            low = base + 2 * n * wide
            in_o[:, low : low + wide] = jnp.where(zero, mine, other)
            in_o[:, low + wide : low + 2 * wide] = jnp.where(zero, other, mine)
    at = slice(inner, inner + bc)
    in_o[:, 4 * inner : 4 * inner + bc] = l[:, at].astype(F32) + lo[:, at].astype(F32)
    i = lax.broadcasted_iota(jnp.int32, (LANE, LANE), 0)
    j = lax.broadcasted_iota(jnp.int32, (LANE, LANE), 1)
    per = head_count // 8
    spot = 2 * per * (i // per) + lax.rem(i, per)
    valid = i < head_count // 2
    first = jnp.where(valid & (j == spot), 1.0, 0.0)
    second = jnp.where(valid & (j == spot + per), 1.0, 0.0)
    at = slice(inner + bc, inner + bc + LANE)
    heads = mm(l[:, at], jnp.where(zero, first, second)) + mm(
        lo[:, at], jnp.where(zero, second, first)
    )
    in_o[:, 4 * inner + bc : 4 * inner + bc + head_count] = heads[:, 0:head_count]
    mine, other = e[:, inner:].astype(F32), eo[:, inner:].astype(F32)
    out_o[0] = jnp.where(zero, mine, other)
    out_o[1] = jnp.where(zero, other, mine)


def assemble(core, early, late, early_o, late_o, proj, head_count):
    flat = [a.reshape(-1, a.shape[-1]) for a in (early, late, early_o, late_o)]
    rows, step = flat[0].shape[0], 64
    inner = flat[0].shape[1] // 2
    return pl.pallas_call(
        functools.partial(assemble_kernel, head_count),
        grid=(rows // step,),
        in_specs=[pl.BlockSpec(memory_space=pltpu.SMEM)]
        + [pl.BlockSpec((step, a.shape[1]), lambda r: (r, 0)) for a in flat],
        out_specs=[
            pl.BlockSpec((step, proj), lambda r: (r, 0)),
            pl.BlockSpec((2, step, inner), lambda r: (0, r, 0)),
        ],
        out_shape=[sds((rows, proj), F32), sds((2, rows, inner), F32)],
        compiler_params=pltpu.CompilerParams(vmem_limit_bytes=40 * 2**20),
    )(core.astype(jnp.int32).reshape(1), *flat)


def spread_kernel(x_own, z_own, o_own, x_all, z_all, o_all, send, recv, local):
    sender = Sender(send, recv)
    q = lax.axis_index("seq")
    x = lax.axis_index("wshard")
    z, y = q // 4, lax.rem(q, 4)
    shards = [lax.rem(x + d, 4) for d in (1, 2, 3)]
    z_up, z_down = lax.rem(z + 1, 4), lax.rem(z + 3, 4)
    y_up, y_down = lax.rem(y + 1, 4), lax.rem(y + 3, 4)
    to_z_up, to_z_down = {"seq": z_up * 4 + y}, {"seq": z_down * 4 + y}
    to_y_up, to_y_down = {"seq": z * 4 + y_up}, {"seq": z * 4 + y_down}
    greet([{"wshard": p} for p in shards] + [to_z_up, to_z_down, to_y_up, to_y_down])
    pairs = ((x_own, x_all), (z_own, z_all), (o_own, o_all))
    sent = [
        sender.start(own.at[z, y], full.at[x, z, y], {"wshard": p})
        for p in shards
        for own, full in pairs
    ]
    kept = [
        pltpu.make_async_copy(own, full.at[x], local.at[n]) for n, (own, full) in enumerate(pairs)
    ]
    for copy in kept:
        copy.start()
    for copy in sent:
        copy.wait()
    cut = 384
    over_y = ((x_all, slice(0, x_all.shape[-1])), (o_all, slice(0, cut)))
    over_z = ((z_all, slice(0, z_all.shape[-1])), (o_all, slice(cut, o_all.shape[-1])))
    ups, downs = [], []

    def both_ways(refs, up, down):
        ups.append([sender.start(r, r, up) for r in refs])
        downs.append([sender.start(r, r, down) for r in refs])

    for p in shards:
        both_ways([a.at[p, z, y, :, c] for a, c in over_y], to_y_up, to_y_down)
        both_ways([a.at[p, z, y, :, c] for a, c in over_z], to_z_up, to_z_down)
    rest = []
    for n, p in enumerate(shards):
        for copy in ups[2 * n] + ups[2 * n + 1] + downs[2 * n] + downs[2 * n + 1]:
            copy.wait()
        if n != 1:
            refs = [a.at[p, z, y_down, :, c] for a, c in over_y[: 2 if n == 0 else 1]]
            rest += [sender.start(r, r, to_y_up) for r in refs]
            refs = [a.at[p, z_down, y, :, c] for a, c in over_z[: 2 if n == 0 else 1]]
            rest += [sender.start(r, r, to_z_up) for r in refs]
        if n != 0:
            refs = [a.at[p, z, y_up, :, c] for a, c in over_y[0 if n == 1 else 1 :]]
            rest += [sender.start(r, r, to_y_down) for r in refs]
            refs = [a.at[p, z_up, y, :, c] for a, c in over_z[0 if n == 1 else 1 :]]
            rest += [sender.start(r, r, to_z_down) for r in refs]
    for copy in rest:
        copy.wait()
    ups.clear()
    downs.clear()
    for p in shards:
        both_ways([a.at[p, z, :, :, c] for a, c in over_y], to_z_up, to_z_down)
        both_ways([a.at[p, :, y, :, c] for a, c in over_z], to_y_up, to_y_down)
    rest = []
    low, high = slice(0, 2), slice(2, 4)
    for n, p in enumerate(shards):
        for copy in ups[2 * n] + ups[2 * n + 1] + downs[2 * n] + downs[2 * n + 1]:
            copy.wait()
        for a, c in over_y:
            here, there = a.at[p, z_down, low, :, c], a.at[p, z_up, high, :, c]
            rest += [sender.start(here, here, to_z_up), sender.start(there, there, to_z_down)]
        for a, c in over_z:
            here, there = a.at[p, low, y_down, :, c], a.at[p, high, y_up, :, c]
            rest += [sender.start(here, here, to_y_up), sender.start(there, there, to_y_down)]
    for copy in rest:
        copy.wait()
    for copy in kept:
        copy.wait()


def spread_weights(x_own, z_own, o_own):
    own = [a.reshape(4, 4, a.shape[0] // 16, a.shape[1]) for a in (x_own, z_own, o_own)]
    place = pl.BlockSpec(memory_space=pltpu.VMEM)
    count = 9 + 24 + 12 + 24 + 24
    full = pl.pallas_call(
        spread_kernel,
        out_shape=[sds((4,) + a.shape, BF16) for a in own],
        in_specs=[place] * 3,
        out_specs=[place] * 3,
        scratch_shapes=[
            pltpu.SemaphoreType.DMA((count,)),
            pltpu.SemaphoreType.DMA((count,)),
            pltpu.SemaphoreType.DMA((3,)),
        ],
        compiler_params=pltpu.CompilerParams(
            collective_id=3, has_side_effects=True, vmem_limit_bytes=40 * 2**20
        ),
    )(*own)
    return tuple(a.reshape(-1, a.shape[-1]) for a in full)


def reduce_kernel(a0, b0, a1, b1, small, *refs):
    g_own, g_other = refs[0:3], refs[3:6]
    xr, xs = refs[6:8]
    r1, t, r2 = (refs[8:11], refs[11:14]), (refs[14:17], refs[17:20]), (refs[20:23], refs[23:26])
    f, o = refs[26:29], refs[29:32]
    sender = Sender(refs[32], refs[33])
    core = lax.axis_index("section")
    q = lax.axis_index("seq")
    x = lax.axis_index("wshard")
    z, y = q // 4, lax.rem(q, 4)

    def on_x(d):
        return {"wshard": lax.rem(x + d, 4)}

    def on_y(d):
        return {"seq": z * 4 + lax.rem(y + d, 4)}

    def on_z(d):
        return {"seq": lax.rem(z + d, 4) * 4 + y}

    twin = {"section": 1 - core}
    greet([on(d) for on in (on_x, on_y, on_z) for d in (1, 2, 3)] + [twin])

    def first(layer, arrays, places):
        copies = []
        for n, a in zip(places, arrays):
            for d in (1, 2, 3):
                if layer == 0:
                    peer, src = on_y(d), a.at[:, lax.rem(y + d, 4)]
                else:
                    peer, src = on_z(d), a.at[lax.rem(z + d, 4)]
                copies.append(sender.start(src, r1[layer][n].at[d - 1], peer))
        return copies

    x_copies = [sender.start(small, xr.at[d - 1], on_x(d)) for d in (1, 2, 3)]
    layers = ((a0, b0, xs.at[0]), (a1, b1, xs.at[1]))
    copies = [first(layer, layers[layer][0:2], (0, 1)) for layer in (0, 1)]
    for copy in x_copies:
        copy.wait()
    xs[...] = small[...] + xr[0] + xr[1] + xr[2]
    for layer in (0, 1):
        copies[layer] += first(layer, layers[layer][2:3], (2,))
    second = []
    for layer in (0, 1):
        for copy in copies[layer]:
            copy.wait()
        for n, a in enumerate(layers[layer]):
            for j in range(4):
                own = a[j, y] if layer == 0 else a[z, j]
                total = own.astype(F32)
                for d in range(3):
                    total = total + r1[layer][n][d, j].astype(F32)
                t[layer][n][j] = total.astype(t[layer][n].dtype)
        for n in range(3):
            for d in (1, 2, 3):
                to = lax.rem(z + d, 4) if layer == 0 else lax.rem(y + d, 4)
                peer = on_z(d) if layer == 0 else on_y(d)
                second.append(sender.start(t[layer][n].at[to], r2[layer][n].at[d - 1], peer))
    for copy in second:
        copy.wait()
    for layer in (0, 1):
        for n in range(3):
            total = t[layer][n][z if layer == 0 else y].astype(F32)
            for d in range(3):
                total = total + r2[layer][n][d].astype(F32)
            f[n][layer] = total.astype(f[n].dtype)
    twins = [sender.start(f[n].at[1 - core], o[n], twin) for n in range(3)]
    gather = []
    for n in range(3):
        g_own[n][z, y] = f[n][core]
        for d in (1, 2, 3):
            gather.append(sender.start(f[n].at[core], g_own[n].at[z, y], on_y(d)))
    for copy in twins:
        copy.wait()
    for n in range(3):
        g_other[n][z, y] = o[n][...]
        for d in (1, 2, 3):
            gather.append(sender.start(o[n], g_other[n].at[z, y], on_z(d)))
    for copy in gather:
        copy.wait()
    gather = []
    for n in range(3):
        for d in (1, 2, 3):
            gather.append(sender.start(g_own[n].at[z], g_own[n].at[z], on_z(d)))
            gather.append(sender.start(g_other[n].at[:, y], g_other[n].at[:, y], on_y(d)))
    for copy in gather:
        copy.wait()


def reduce_all(grids, small):
    kinds = [(a.shape[2:], a.dtype) for a in (grids[0], grids[1], small[0])]
    full = [sds((4, 4) + shape, dtype) for shape, dtype in kinds]

    def vmem(*lead):
        return [pltpu.VMEM(lead + shape, dtype) for shape, dtype in kinds]

    scratch = [
        pltpu.VMEM((3,) + small.shape, F32),
        pltpu.VMEM(small.shape, F32),
        *vmem(3, 4), *vmem(3, 4), *vmem(4), *vmem(4), *vmem(3), *vmem(3), *vmem(2), *vmem(),
        pltpu.SemaphoreType.DMA((3 + 18 + 18 + 3 + 18 + 18,)),
        pltpu.SemaphoreType.DMA((3 + 18 + 18 + 3 + 18 + 18,)),
    ]
    place = pl.BlockSpec(memory_space=pltpu.VMEM)
    out = pl.pallas_call(
        reduce_kernel,
        out_shape=full + full,
        in_specs=[place] * 5,
        out_specs=[place] * 6,
        scratch_shapes=scratch,
        compiler_params=pltpu.CompilerParams(
            collective_id=0, has_side_effects=True, vmem_limit_bytes=40 * 2**20
        ),
    )(*grids, small)
    return out[0:3], out[3:6]


def forward(u, w, p):
    w_x, w_z, w_out = w
    gain_in, cw, cb, hp, gain_out = p
    seqs, rows, width = u.shape
    chan = cw.shape[1]
    taps = 4
    inner = gain_out.shape[1]
    states = LANE
    uf = u.astype(F32)
    inv = lax.rsqrt(jnp.mean(uf * uf, axis=-1, keepdims=True) + EPS)
    normed = (uf * inv * gain_in).astype(BF16).reshape(seqs * rows, width)
    xd = jnp.dot(normed, w_x, preferred_element_type=F32).astype(BF16)
    xd = xd.reshape(seqs, rows, chan + LANE)
    z = jnp.dot(normed, w_z, preferred_element_type=F32).reshape(seqs, rows, inner)
    halo = shift(xd[:, rows - TAIL :, :chan], "seq", 1)
    act, cum, step, sloc = run(
        functools.partial(chunk_kernel, taps),
        (xd, halo, cw, cb, hp),
        (
            sds((seqs, rows, chan), F32),
            sds((seqs, rows, LANE), F32),
            sds((seqs, rows, LANE), F32),
            sds((seqs * inner // LANE, states + TAIL, LANE), BF16),
        ),
        [pltpu.VMEM((TAIL + rows, chan), F32)],
        (2, 3, 4),
    )
    (yi,) = run(intra_kernel, (act, cum, step), (sds((seqs, rows, inner), F32),))
    decay, sin = scan_chunks(sloc, None, False, states)
    yy, gg, ss = run(
        finish_kernel,
        (act, cum, yi, sin, z, hp, gain_out),
        (
            sds((seqs, rows, inner), F32),
            sds((seqs, rows, inner), BF16),
            sds((seqs, rows, 1), F32),
        ),
        (),
        (5, 6),
    )
    mine = jnp.dot(gg.reshape(seqs * rows, inner), w_out, preferred_element_type=F32)
    mine = mine.astype(BF16).reshape(seqs, rows, width)
    theirs, ss_theirs = swap(mine), swap(ss)
    branch = mine.astype(F32) + theirs.astype(F32)
    rn = lax.rsqrt((ss + ss_theirs) * (1.0 / (2 * inner)) + EPS)
    result = (uf + rn * branch).astype(BF16)
    kept = (u, inv, normed, z, xd, halo, act, cum, step, decay, sin, yy, branch, rn)
    return result, kept


def backward(e, kept, w, p):
    w_x, w_z, w_out = w
    gain_in, cw, cb, hp, gain_out = p
    u, inv, normed, z, xd, halo, act, cum, step, decay, sin, yy, branch, rn = kept
    seqs, rows, width = e.shape
    chan = cw.shape[1]
    taps = 4
    inner = gain_out.shape[1]
    states = LANE
    ef = e.astype(F32)
    e2 = e.reshape(seqs * rows, width)
    nt = (((1,), (1,)), ((), ()))
    tn = (((0,), (0,)), ((), ()))
    gr = lax.dot_general(e2, w_out, nt, preferred_element_type=F32).reshape(seqs, rows, inner)
    rs = jnp.sum(ef * branch, axis=-1, keepdims=True)
    dy, gz, dsl, dgain, gated = run(
        gate_back_kernel,
        (gr, z, yy, act, cum, rn, rs, hp, gain_out),
        (
            sds((seqs, rows, inner), BF16),
            sds((seqs, rows, inner), BF16),
            sds((seqs * inner // LANE, states, LANE), BF16),
            sds((seqs, 8, inner), F32),
            sds((seqs, rows, inner), BF16),
        ),
        (),
        (7, 8),
    )
    gz = gz.reshape(seqs * rows, inner)
    part_z = lax.dot_general(gz, w_z, nt, preferred_element_type=F32)
    early = jnp.concatenate(
        [
            lax.dot_general(normed, gz, tn, preferred_element_type=F32),
            lax.dot_general(
                gated.reshape(seqs * rows, inner), e2, tn, preferred_element_type=F32
            ),
        ],
        axis=1,
    ).astype(BF16)
    early = lax.psum_scatter(early, "wshard", scatter_dimension=0, tiled=True)
    dxs, dbc, dci = run(
        intra_back_kernel,
        (act, cum, step, dy),
        (
            sds((seqs, rows, inner), F32),
            sds((seqs, rows, 2 * LANE), F32),
            sds((seqs, rows, LANE), F32),
        ),
    )
    (grad,) = scan_chunks(dsl, decay, True, states)
    dpre, ddt, conv_g, head_g = run(
        functools.partial(mix_back_kernel, taps),
        (xd, halo, cw, cb, hp, act, cum, step, dy, dxs, dbc, dci, grad, sin),
        (
            sds((seqs, rows, chan), F32),
            sds((seqs, rows, LANE), BF16),
            sds((seqs, 8, chan), F32),
            sds((seqs, 8, LANE), F32),
        ),
        [pltpu.VMEM((TAIL + rows, chan), F32), pltpu.VMEM((rows, chan), F32)],
        (2, 3, 4),
    )
    after = shift(dpre[:, :8], "seq", -1)
    (gp,) = run(
        functools.partial(conv_back_kernel, taps),
        (dpre, after, ddt, cw),
        (sds((seqs, rows, chan + LANE), BF16),),
        [pltpu.VMEM((rows + 8, chan), F32)],
        (3,),
    )
    gp = gp.reshape(seqs * rows, -1)
    mine = part_z + lax.dot_general(gp, w_x, nt, preferred_element_type=F32)
    mine = mine.astype(BF16).reshape(seqs, rows, width)
    theirs = swap(mine)
    gn = mine.astype(F32) + theirs.astype(F32)
    uf = u.astype(F32)
    unit = uf * inv
    g_gain_in = jnp.sum(gn * unit, axis=(0, 1))
    scaled = gn * gain_in
    dot = jnp.mean(scaled * unit, axis=-1, keepdims=True)
    grad_u = ef + inv * (scaled - unit * dot)
    late = lax.dot_general(normed, gp, tn, preferred_element_type=F32).astype(BF16)
    late = lax.psum_scatter(late, "wshard", scatter_dimension=0, tiled=True)
    heads = inner // HDIM
    conv_sum, head_sum = conv_g.sum(0), head_g.sum(0)
    smalls = (
        g_gain_in,
        conv_sum[: taps + 1, :inner],
        conv_sum[: taps + 1, inner:],
        head_sum[:3, :heads],
        dgain.sum(0)[0],
    )
    return grad_u, (early, late), smalls


def body(
    hidden, out_grad, norm_gain, in_weight, conv_weight, conv_bias, dt_bias, a_log, d_skip,
    out_gain, out_weight,
):
    core = lax.axis_index("section")
    width = hidden.shape[2]
    full = out_gain.shape[1]
    taps = conv_weight.shape[1]
    head_count = dt_bias.shape[1]
    proj = in_weight.shape[2]
    bc_at, dt_at = 2 * full, proj - head_count

    wi, wo = in_weight[0], out_weight[0]

    def pack(which):
        out_rows = wo.reshape(2, wo.shape[0] // 2, wo.shape[1])
        x_part = jnp.concatenate(
            [
                half(wi[:, full:bc_at], which),
                wi[:, bc_at:dt_at],
                jnp.pad(half(wi[:, dt_at:], which), ((0, 0), (0, LANE - head_count // 2))),
            ],
            axis=1,
        )
        out_part = lax.dynamic_index_in_dim(out_rows, which, 0, keepdims=False)
        return x_part, half(wi[:, :full], which), out_part

    own, sent = pack(core), pack(1 - core)
    came = jax.tree.map(swap, sent)
    sizes = (norm_gain, conv_weight, conv_bias, dt_bias, a_log, d_skip, out_gain)
    flat = jnp.concatenate([a[0].reshape(-1) for a in sizes])
    flat_other = swap(flat)

    def params(layer):
        mine = core == layer
        w = tuple(jnp.where(mine, a, b) for a, b in zip(own, came))
        if layer == 0:
            w = spread_weights(*w)
        else:
            w = tuple(lax.all_gather(a, "wshard", axis=0, tiled=True) for a in w)
        v = jnp.where(mine, flat, flat_other)
        parts, at = [], 0
        for a in sizes:
            count = a[0].size
            parts.append(v[at : at + count].reshape(a[0].shape))
            at += count
        gain_in, cw, cb, dtb, al, ds, gain_out = parts

        def channels(a):
            return jnp.concatenate([half(a[..., :full], core), a[..., full:]], axis=-1)

        hp = jnp.stack([half(a, core) for a in (dtb, al, ds)])
        hp = jnp.pad(hp, ((0, 5), (0, LANE - hp.shape[1])))
        cw = jnp.pad(channels(cw), ((0, 8 - taps), (0, 0)))
        return w, (
            gain_in[None],
            cw,
            channels(cb)[None],
            hp,
            half(gain_out, core)[None],
        )

    w0, p0 = params(0)
    w1, p1 = params(1)
    first, kept0 = forward(hidden, w0, p0)
    second, kept1 = forward(first, w1, p1)
    layer_out = jnp.where(core == 0, first, second)[None]
    grad1, products1, smalls1 = backward(out_grad, kept1, w1, p1)
    passed = grad1.astype(BF16)
    grad0, products0, smalls0 = backward(passed, kept0, w0, p0)
    section_grad = jnp.where(core == 0, grad0, passed.astype(F32))[None]

    flat = [jnp.concatenate([a.reshape(-1) for a in g]) for g in (smalls0, smalls1)]
    count = flat[0].size
    block = 8 * LANE
    flat = [jnp.pad(v, (0, 16 * block - count)).reshape(4, 4, 8, LANE) for v in flat]
    rows = width // 64

    def blocks(a):
        return a.reshape(4, 4, rows, a.shape[1])

    grids = [blocks(a) for a in products0 + products1]
    mine, other = reduce_all(grids, jnp.stack(flat))
    (early, late, small_mine), (early_o, late_o, small_o) = mine, other
    grad_w_in, grad_w_out = assemble(core, early, late, early_o, late_o, proj, head_count)
    grad_w_out = grad_w_out.reshape(-1, width)

    def unflatten(v):
        parts, pos = [], 0
        for a in smalls0:
            parts.append(v.reshape(-1)[pos : pos + a.size].reshape(a.shape))
            pos += a.size
        return parts

    small_mine, small_o = unflatten(small_mine), unflatten(small_o)
    vector = jnp.concatenate(
        [
            small_mine[0],
            jnp.concatenate(
                [whole(small_mine[1], small_o[1], core), small_mine[2] + small_o[2]], axis=1
            ).reshape(-1),
            whole(small_mine[3], small_o[3], core).reshape(-1),
            whole(small_mine[4], small_o[4], core),
        ]
    )
    chan = full + dt_at - bc_at
    cuts = (width, taps * chan, chan, head_count, head_count, head_count, full)
    small, pos = [], 0
    for count in cuts:
        small.append(vector[pos : pos + count])
        pos += count
    return (
        layer_out,
        section_grad,
        small[0][None],
        grad_w_in[None],
        small[1].reshape(1, taps, chan),
        small[2][None],
        small[3][None],
        small[4][None],
        small[5][None],
        small[6][None],
        grad_w_out[None],
    )


def solution(mesh):
    by_layer = P("section", None)
    weights = P("section", "wshard", None)
    tokens = P("wshard", "seq", None)
    stacked = P("section", "wshard", "seq", None)
    conv = P("section", None, None)
    in_specs = (
        tokens, tokens, by_layer, weights, conv, by_layer, by_layer, by_layer, by_layer, by_layer,
        weights,
    )
    out_specs = (
        stacked, stacked, by_layer, weights, conv, by_layer, by_layer, by_layer, by_layer,
        by_layer, weights,
    )
    return jax.shard_map(body, mesh=mesh, in_specs=in_specs, out_specs=out_specs, check_vma=False)
```

```python
import functools

import jax
import jax.numpy as jnp
from jax import lax
from jax.experimental import pallas as pl
from jax.experimental.pallas import tpu as pltpu
from jax.sharding import PartitionSpec as P

F32 = jnp.float32
BF16 = jnp.bfloat16
HI = lax.Precision.HIGHEST
EPS = 1e-05
HDIM = 64
LANE = 128
TAIL = 16


def shift(x, axis, by):
    devices = lax.axis_size(axis)
    pairs = [(i, i + by) for i in range(devices) if 0 <= i + by < devices]
    return lax.ppermute(x, axis, pairs)


def swap(x):
    return lax.ppermute(x, "section", [(0, 1), (1, 0)])


def half(a, which):
    width = a.shape[-1] // 8
    b = a.reshape(a.shape[:-1] + (4, 2, width))
    b = lax.dynamic_index_in_dim(b, which, axis=b.ndim - 2, keepdims=False)
    return b.reshape(a.shape[:-1] + (4 * width,))


def whole(own, other, core):
    width = own.shape[-1] // 4
    lead = own.shape[:-1]
    own, other = own.reshape(lead + (4, 1, width)), other.reshape(lead + (4, 1, width))
    first, second = jnp.where(core == 0, own, other), jnp.where(core == 0, other, own)
    return jnp.concatenate([first, second], axis=-2).reshape(lead + (8 * width,))


def mm(a, b):
    return jnp.dot(a.astype(BF16), b.astype(BF16), preferred_element_type=F32)


def mm_nt(a, b):
    return lax.dot_general(
        a.astype(BF16), b.astype(BF16), (((1,), (1,)), ((), ())), preferred_element_type=F32
    )


def mm_tn(a, b):
    return lax.dot_general(
        a.astype(BF16), b.astype(BF16), (((0,), (0,)), ((), ())), preferred_element_type=F32
    )


def spread_matrix(width):
    head = lax.broadcasted_iota(jnp.int32, (LANE, width), 0)
    lane = lax.broadcasted_iota(jnp.int32, (LANE, width), 1)
    return jnp.where(lane // HDIM == head, 1.0, 0.0).astype(BF16)


def split(v):
    high = v.astype(BF16)
    return high, (v - high.astype(F32)).astype(BF16)


def spread(heads, matrix):
    high, rest = split(heads)
    return mm(high, matrix) + mm(rest, matrix)


def gather_heads(lanes, matrix):
    high, rest = split(lanes)
    return mm_nt(high, matrix) + mm_nt(rest, matrix)


def tri(rows, upper):
    r = lax.broadcasted_iota(jnp.int32, (rows, rows), 0)
    c = lax.broadcasted_iota(jnp.int32, (rows, rows), 1)
    return jnp.where((c >= r) if upper else (r >= c), 1.0, 0.0).astype(F32)


def steps(dt, hp):
    shifted = dt + hp[0:1, :]
    step = jnp.maximum(shifted, 0.0) + jnp.log1p(jnp.exp(-jnp.abs(shifted)))
    rate = -jnp.exp(hp[1:2, :])
    return shifted, step, rate


def sigmoid(v):
    return 1.0 / (1.0 + jnp.exp(-v))


def conv_pre(buf, cw, cb, taps, rows):
    pre = cb[0:1, :]
    for k in range(taps):
        start = TAIL - (taps - 1) + k
        pre = pre + cw[k : k + 1, :] * buf[start : start + rows, :]
    return pre


MESH = pl.DeviceIdType.MESH


class Sender:
    def __init__(self, send, recv):
        self.send, self.recv, self.used = send, recv, 0

    def start(self, src, dst, device):
        n = self.used
        self.used += 1
        copy = pltpu.make_async_remote_copy(
            src_ref=src,
            dst_ref=dst,
            send_sem=self.send.at[n],
            recv_sem=self.recv.at[n],
            device_id=device,
            device_id_type=MESH,
        )
        copy.start()
        return copy


def greet(devices):
    barrier = pltpu.get_barrier_semaphore()
    for device in devices:
        pl.semaphore_signal(barrier, inc=1, device_id=device, device_id_type=MESH)
    pl.semaphore_wait(barrier, len(devices))


def chunk_kernel(taps, xd, halo, cw, cb, hp, act_o, cum_o, step_o, sloc_o, buf):
    rows, inner, chan = xd.shape[1], sloc_o.shape[0] * LANE, cw.shape[1]
    buf[0:TAIL, :] = halo[0].astype(F32)
    buf[TAIL : TAIL + rows, :] = xd[0, :, 0:chan].astype(F32)
    pre = conv_pre(buf, cw, cb, taps, rows)
    act = pre * sigmoid(pre)
    act_o[0] = act
    _, step, rate = steps(xd[0, :, chan : chan + LANE].astype(F32), hp)
    cum = jnp.dot(tri(rows, False), step * rate, precision=HI, preferred_element_type=F32)
    cum_o[0] = cum
    step_o[0] = step
    last = cum[rows - 1 : rows, :]
    matrix = spread_matrix(inner)
    weight = spread(jnp.exp(last - cum) * step, matrix)
    decay = spread(jnp.broadcast_to(jnp.exp(last), (8, LANE)), matrix)[0:1, :]
    d_hi = decay.astype(BF16).astype(F32)
    d_mid = (decay - d_hi).astype(BF16).astype(F32)
    d_lo = decay - d_hi - d_mid
    row = lax.broadcasted_iota(jnp.int32, (TAIL, inner), 0)
    extra = jnp.where(row == 0, d_hi, jnp.where(row == 1, d_mid, jnp.where(row == 2, d_lo, 0.0)))
    extra = extra.astype(BF16)
    xw = (act[:, :inner] * weight).astype(BF16)
    b = act[:, inner : inner + LANE].astype(BF16)
    sloc = mm_tn(b, xw).astype(BF16)
    states = sloc.shape[0]
    for i in range(inner // LANE):
        sloc_o[i, 0:states, :] = sloc[:, i * LANE : (i + 1) * LANE]
        sloc_o[i, states : states + TAIL, :] = extra[:, i * LANE : (i + 1) * LANE]


def scan_kernel(reverse, with_decay, pieces_ref, *refs):
    if with_decay:
        decay, out, got, done, send_a, recv_a, send_b, recv_b = refs
    else:
        decay, out, got, done, send_a, recv_a, send_b, recv_b = refs
    count, states = out.shape[0], out.shape[1]
    q = lax.axis_index("seq")
    peers = [lax.rem(q + d, count) for d in range(1, count)]
    greet([{"seq": p} for p in peers])

    def copy(src, dst, send, recv, n, peer, slot):
        return pltpu.make_async_remote_copy(
            src_ref=src.at[peer],
            dst_ref=dst.at[slot],
            send_sem=send.at[n],
            recv_sem=recv.at[slot],
            device_id={"seq": peer},
            device_id_type=MESH,
        )

    sent = [copy(pieces_ref, got, send_a, recv_a, n, p, q) for n, p in enumerate(peers)]
    for c in sent:
        c.start()
    got[q] = pieces_ref[q]
    for n, p in enumerate(peers):
        copy(pieces_ref, got, send_a, recv_a, n, p, p).wait_recv()
    carry = jnp.zeros((states, LANE), F32)
    order = range(count - 1, -1, -1) if reverse else range(count)
    for j in order:
        if with_decay:
            tail = got[j, states : states + TAIL, :].astype(F32)
            decay[j : j + 1, :] = tail[0:1, :] + tail[1:2, :] + tail[2:3, :]
        done[j] = carry.astype(BF16)
        carry = carry * decay[j : j + 1, :] + got[j, 0:states, :].astype(F32)
    back = [copy(done, out, send_b, recv_b, n, p, q) for n, p in enumerate(peers)]
    for c in back:
        c.start()
    out[q] = done[q]
    for n, p in enumerate(peers):
        copy(done, out, send_b, recv_b, n, p, p).wait_recv()
    for c in sent + back:
        c.wait_send()


def intra_kernel(act, cum, step, yi_o):
    rows, inner = yi_o.shape[1], yi_o.shape[2]
    b = act[0, :, inner : inner + LANE]
    c = act[0, :, inner + LANE : inner + 2 * LANE]
    cb = mm_nt(c, b)
    cum_v = cum[0]
    cum_t = jnp.transpose(cum_v)
    xs = act[0, :, :inner] * spread(step[0], spread_matrix(inner))
    keep = tri(rows, False) > 0
    low = lax.broadcasted_iota(jnp.int32, (rows, LANE), 1) < HDIM
    for i in range(inner // LANE):
        xs_i = xs[:, i * LANE : (i + 1) * LANE].astype(BF16)
        parts = []
        for h in (2 * i, 2 * i + 1):
            diff = cum_v[:, h : h + 1] - cum_t[h : h + 1, :]
            decay = jnp.exp(jnp.where(keep, diff, -1e30))
            parts.append(mm(cb * decay, xs_i))
        yi_o[0, :, i * LANE : (i + 1) * LANE] = jnp.where(low, parts[0], parts[1])


def finish_kernel(act, cum, yi, sin, z, hp, gain, yy_o, gg_o, ss_o):
    inner = yi.shape[2]
    matrix = spread_matrix(inner)
    grown = spread(jnp.exp(cum[0]), matrix)
    skip = spread(jnp.broadcast_to(hp[2:3, :], (8, LANE)), matrix)[0:1, :]
    c = act[0, :, inner + LANE : inner + 2 * LANE].astype(BF16)
    total = jnp.zeros((yi.shape[1], LANE), F32)
    for i in range(inner // LANE):
        at = slice(i * LANE, (i + 1) * LANE)
        yy = yi[0, :, at] + grown[:, at] * mm(c, sin[i])
        yy_o[0, :, at] = yy
        mixed = (yy + skip[:, at] * act[0, :, at]).astype(BF16).astype(F32)
        zi = z[0, :, at]
        g = mixed * (zi * sigmoid(zi))
        total = total + g * g
        gg_o[0, :, at] = (g * gain[0:1, at]).astype(BF16)
    ss_o[0] = jnp.sum(total, axis=1, keepdims=True)


def gate_back_kernel(
    gr, z, yy, act, cum, rn, rs, hp, gain, dy_o, gz_o, dsl_o, dgain_o, gated_o
):
    inner = gr.shape[2]
    matrix = spread_matrix(inner)
    grown = spread(jnp.exp(cum[0]), matrix)
    skip = spread(jnp.broadcast_to(hp[2:3, :], (8, LANE)), matrix)[0:1, :]
    c = act[0, :, inner + LANE : inner + 2 * LANE].astype(BF16)
    r = rn[0]
    k = r * r * r * rs[0] * (1.0 / (2 * inner))
    for i in range(inner // LANE):
        at = slice(i * LANE, (i + 1) * LANE)
        mixed = (yy[0, :, at] + skip[:, at] * act[0, :, at]).astype(BF16).astype(F32)
        zi = z[0, :, at]
        sg = sigmoid(zi)
        silu = zi * sg
        g = mixed * silu
        gr_i = gr[0, :, at]
        gain_i = gain[0:1, at]
        normal = g * r
        dgain_o[0, i : i + 1, :] = jnp.sum(gr_i * normal, axis=0, keepdims=True)
        gated_o[0, :, at] = (normal * gain_i).astype(BF16)
        dg = r * (gain_i * gr_i) - g * k
        dy = (dg * silu).astype(BF16)
        dy_o[0, :, at] = dy
        gz_o[0, :, at] = (dg * mixed * (sg * (1.0 + zi * (1.0 - sg)))).astype(BF16)
        dsl_o[i] = mm_tn(c, dy.astype(F32) * grown[:, at]).astype(BF16)


def intra_back_kernel(act, cum, step, dy, dxs_o, dbc_o, dcum_o):
    rows, inner = dxs_o.shape[1], dxs_o.shape[2]
    b = act[0, :, inner : inner + LANE].astype(BF16)
    c = act[0, :, inner + LANE : inner + 2 * LANE].astype(BF16)
    cb = mm_nt(c, b)
    cum_v = cum[0]
    cum_t = jnp.transpose(cum_v)
    xs = act[0, :, :inner] * spread(step[0], spread_matrix(inner))
    keep = tri(rows, False) > 0
    low = lax.broadcasted_iota(jnp.int32, (rows, LANE), 1) < HDIM
    dcb = jnp.zeros((rows, rows), F32)
    lane = lax.broadcasted_iota(jnp.int32, (rows, LANE), 1)
    row_sums = jnp.zeros((rows, LANE), F32)
    col_sums = []
    for i in range(inner // LANE):
        at = slice(i * LANE, (i + 1) * LANE)
        xs_i = xs[:, at]
        dy_i = dy[0, :, at].astype(F32)
        parts = []
        for n, h in enumerate((2 * i, 2 * i + 1)):
            diff = cum_v[:, h : h + 1] - cum_t[h : h + 1, :]
            decay = jnp.exp(jnp.where(keep, diff, -1e30))
            mine = jnp.where(low, dy_i, 0.0) if n == 0 else jnp.where(low, 0.0, dy_i)
            flow = mm_nt(mine, xs_i) * decay
            dcb = dcb + flow
            both = flow * cb
            row_sums = jnp.where(lane == h, jnp.sum(both, axis=1, keepdims=True), row_sums)
            col_sums.append(jnp.sum(both, axis=0, keepdims=True))
            parts.append(mm_tn(cb * decay, dy_i))
        dxs_o[0, :, at] = jnp.where(low, parts[0], parts[1])
    col_sums.append(jnp.zeros((LANE - len(col_sums), rows), F32))
    dcum_o[0] = row_sums - jnp.transpose(jnp.concatenate(col_sums, axis=0))
    dbc_o[0, :, 0:LANE] = mm_tn(dcb, c)
    dbc_o[0, :, LANE : 2 * LANE] = mm(dcb, b)


def mix_back_kernel(
    taps, xd, halo, cw, cb, hp, act, cum, step, dy, dxs, dbc, dci, grad, sin,
    dpre_o, ddt_o, small_o, buf, dact,
):
    rows, inner, chan = dy.shape[1], dy.shape[2], cw.shape[1]
    matrix = spread_matrix(inner)
    cum_v, step_v = cum[0], step[0]
    last = cum_v[rows - 1 : rows, :]
    step_e = spread(step_v, matrix)
    tail_e = spread(jnp.exp(last - cum_v), matrix)
    grown = spread(jnp.exp(cum_v), matrix)
    d_e = grown[rows - 1 : rows, :]
    skip = spread(jnp.broadcast_to(hp[2:3, :], (8, LANE)), matrix)[0:1, :]
    b = act[0, :, inner : inner + LANE].astype(BF16)
    c = act[0, :, inner + LANE : inner + 2 * LANE].astype(BF16)
    q1 = dci[0]
    qb = jnp.zeros((rows, LANE), F32)
    q2 = jnp.zeros((rows, LANE), F32)
    flows = jnp.zeros((8, LANE), F32)
    skips = jnp.zeros((8, LANE), F32)
    db, dc = dbc[0, :, 0:LANE], dbc[0, :, LANE : 2 * LANE]
    for i in range(inner // LANE):
        at = slice(i * LANE, (i + 1) * LANE)
        g = grad[i]
        x = act[0, :, at]
        dy_i = dy[0, :, at].astype(F32)
        s_i = sin[i]
        back = tail_e[:, at] * mm(b, g)
        v = dxs[0, :, at] + back
        dact[:, at] = step_e[:, at] * v + skip[:, at] * dy_i
        part = matrix[:, at]
        q1 = q1 + gather_heads(dy_i * grown[:, at] * mm(c, s_i), part)
        q2 = q2 + gather_heads(x * v, part)
        qb = qb + gather_heads(x * back, part)
        flow = d_e[:, at] * jnp.sum(g.astype(F32) * s_i.astype(F32), axis=0, keepdims=True)
        flows = flows + gather_heads(jnp.broadcast_to(flow, (8, LANE)), part)
        skip_i = jnp.sum(dy_i * x, axis=0, keepdims=True)
        skips = skips + gather_heads(jnp.broadcast_to(skip_i, (8, LANE)), part)
        db = db + mm_nt(tail_e[:, at] * step_e[:, at] * x, g)
        dc = dc + mm_nt(dy_i * grown[:, at], s_i)
    dact[:, inner : inner + LANE] = db
    dact[:, inner + LANE : inner + 2 * LANE] = dc
    shifted, _, rate = steps(xd[0, :, chan : chan + LANE].astype(F32), hp)
    later = jnp.dot(tri(rows, True), q1, precision=HI, preferred_element_type=F32)
    strict = 1.0 - tri(rows, True)
    sooner = jnp.dot(strict, step_v * qb, precision=HI, preferred_element_type=F32)
    da = later + sooner + flows[0:1, :]
    ddt = (q2 + rate * da) * sigmoid(shifted)
    ddt_o[0] = ddt.astype(BF16)
    small_o[0] = jnp.zeros(small_o.shape[1:], F32)
    top, low = inner // LANE, 2
    at = (taps + 1) * (top + low)
    small_o[0, at : at + 1, :] = jnp.sum(ddt, axis=0, keepdims=True)
    small_o[0, at + 1 : at + 2, :] = jnp.sum(da * step_v, axis=0, keepdims=True) * rate
    small_o[0, at + 2 : at + 3, :] = skips[0:1, :]
    buf[0:TAIL, :] = halo[0].astype(F32)
    buf[TAIL : TAIL + rows, :] = xd[0, :, 0:chan].astype(F32)
    pre = conv_pre(buf, cw, cb, taps, rows)
    sg = sigmoid(pre)
    dpre = dact[...] * (sg * (1.0 + pre * (1.0 - sg)))
    dpre_o[0] = dpre
    for k in range(taps + 1):
        start = TAIL - (taps - 1) + k
        terms = dpre if k == taps else dpre * buf[start : start + rows, :]
        total = jnp.sum(terms, axis=0, keepdims=True)
        for i in range(top + low):
            to = k * top + i if i < top else (taps + 1) * top + k * low + i - top
            small_o[0, to : to + 1, :] = total[:, i * LANE : (i + 1) * LANE]


def conv_back_kernel(taps, dpre, after, ddt, cw, out, buf):
    rows, chan = dpre.shape[1], dpre.shape[2]
    buf[0:rows, :] = dpre[0]
    buf[rows : rows + 8, :] = after[0]
    total = cw[taps - 1 : taps, :] * buf[0:rows, :]
    for k in range(taps - 1):
        start = taps - 1 - k
        total = total + cw[k : k + 1, :] * buf[start : start + rows, :]
    out[0, :, 0:chan] = total.astype(BF16)
    out[0, :, chan : chan + LANE] = ddt[0]


def per_seq(shape):
    block = (shape[0] // 2,) + shape[1:]
    return pl.BlockSpec(block, lambda s: (s,) + (0,) * (len(shape) - 1))


def same(shape):
    return pl.BlockSpec(shape, lambda s: (0,) * len(shape))


def run(kernel, ins, outs, scratch=(), shared=()):
    return pl.pallas_call(
        kernel,
        grid=(2,),
        in_specs=[(same if n in shared else per_seq)(a.shape) for n, a in enumerate(ins)],
        out_specs=[per_seq(o.shape) for o in outs],
        out_shape=list(outs),
        scratch_shapes=list(scratch),
        compiler_params=pltpu.CompilerParams(vmem_limit_bytes=40 * 2**20),
    )(*ins)


def sds(shape, dtype):
    return jax.ShapeDtypeStruct(shape, dtype)


def scan_chunks(pieces, decay, reverse, states):
    count, height = pieces.shape[0], pieces.shape[1]
    place = pl.BlockSpec(memory_space=pltpu.VMEM)
    out = sds((count, states, LANE), BF16)
    outs = [sds((count, LANE), F32), out] if decay is None else [out]
    ins = (pieces,) if decay is None else (pieces, decay)
    sems = [pltpu.SemaphoreType.DMA((count,))] * 4
    return pl.pallas_call(
        functools.partial(scan_kernel, reverse, decay is None),
        out_shape=outs,
        in_specs=[place] * len(ins),
        out_specs=[place] * len(outs),
        scratch_shapes=[
            pltpu.VMEM((count, height, LANE), BF16),
            pltpu.VMEM((count, states, LANE), BF16),
            *sems,
        ],
        compiler_params=pltpu.CompilerParams(
            collective_id=1 + reverse, has_side_effects=True, vmem_limit_bytes=40 * 2**20
        ),
    )(*ins)


def assemble_kernel(
    head_count, taps, core, e, l, v, eo, lo, vo, in_o, out_o, gain_o, conv_o, bias_o, heads_o, og_o
):
    full = e.shape[1]
    inner = full // 2
    wide = inner // 4
    bc = l.shape[1] - inner - LANE
    zero = core[0] == 0
    i = lax.broadcasted_iota(jnp.int32, (LANE, LANE), 0)
    j = lax.broadcasted_iota(jnp.int32, (LANE, LANE), 1)
    per = head_count // 8
    spot = 2 * per * (i // per) + lax.rem(i, per)
    valid = i < head_count // 2
    first = jnp.where(valid & (j == spot), 1.0, 0.0)
    second = jnp.where(valid & (j == spot + per), 1.0, 0.0)
    mine_to, other_to = jnp.where(zero, first, second), jnp.where(zero, second, first)

    for n in range(4):
        src = slice(n * wide, (n + 1) * wide)
        for base, a, b in ((0, e, eo), (2 * inner, l, lo)):
            mine, other = a[:, src].astype(F32).T, b[:, src].astype(F32).T
            low = base + 2 * n * wide
            in_o[low : low + wide, :] = jnp.where(zero, mine, other)
            in_o[low + wide : low + 2 * wide, :] = jnp.where(zero, other, mine)
    at = slice(inner, inner + bc)
    in_o[4 * inner : 4 * inner + bc, :] = (l[:, at].astype(F32) + lo[:, at].astype(F32)).T
    at = slice(inner + bc, inner + bc + LANE)
    heads = mm(l[:, at], mine_to) + mm(lo[:, at], other_to)
    in_o[4 * inner + bc : 4 * inner + bc + head_count, :] = heads.T[0:head_count, :]
    mine, other = e[:, inner:].astype(F32), eo[:, inner:].astype(F32)
    out_o[0] = jnp.where(zero, mine, other)
    out_o[1] = jnp.where(zero, other, mine)

    top, low = inner // LANE, bc // LANE
    wide = wide // LANE

    def halves(target, row, source):
        for n in range(top):
            mine, other = v[source + n : source + n + 1, :], vo[source + n : source + n + 1, :]
            to = ((n // wide) * 2 * wide + n % wide) * LANE
            target[row : row + 1, to : to + LANE] = jnp.where(zero, mine, other)
            to += wide * LANE
            target[row : row + 1, to : to + LANE] = jnp.where(zero, other, mine)

    for k in range(taps + 1):
        target, row = (conv_o, k) if k < taps else (bias_o, 0)
        halves(target, row, k * top)
        for n in range(low):
            at = (taps + 1) * top + k * low + n
            to = 2 * inner + n * LANE
            target[row : row + 1, to : to + LANE] = v[at : at + 1, :] + vo[at : at + 1, :]
    at = (taps + 1) * (top + low)

    def exact(a, b):
        return jnp.dot(a, b, precision=HI, preferred_element_type=F32)

    heads_o[...] = exact(v[at : at + 8, :], mine_to) + exact(vo[at : at + 8, :], other_to)
    halves(og_o, 0, at + 3)
    gain_o[...] = v[at + 3 + top : at + 3 + 2 * top, :]


def assemble(core, mine, other, proj, head_count, taps):
    flat = [a.reshape(-1, a.shape[-1]) for a in tuple(mine) + tuple(other)]
    rows, inner = flat[0].shape[0], flat[0].shape[1] // 2
    chan = 2 * inner + flat[1].shape[1] - inner - LANE
    place = pl.BlockSpec(memory_space=pltpu.VMEM)
    outs = [
        (proj, rows), (2, rows, inner), (8, LANE), (taps, chan), (1, chan), (8, LANE),
        (1, 2 * inner),
    ]
    return pl.pallas_call(
        functools.partial(assemble_kernel, head_count, taps),
        in_specs=[pl.BlockSpec(memory_space=pltpu.SMEM)] + [place] * 6,
        out_specs=[place] * len(outs),
        out_shape=[sds(shape, F32) for shape in outs],
        compiler_params=pltpu.CompilerParams(vmem_limit_bytes=40 * 2**20),
    )(core.astype(jnp.int32).reshape(1), *flat)


def spread_kernel(x_own, z_own, o_own, x_all, z_all, o_all, send, recv, local):
    sender = Sender(send, recv)
    q = lax.axis_index("seq")
    x = lax.axis_index("wshard")
    z, y = q // 4, lax.rem(q, 4)
    shards = [lax.rem(x + d, 4) for d in (1, 2, 3)]
    z_up, z_down = lax.rem(z + 1, 4), lax.rem(z + 3, 4)
    y_up, y_down = lax.rem(y + 1, 4), lax.rem(y + 3, 4)
    to_z_up, to_z_down = {"seq": z_up * 4 + y}, {"seq": z_down * 4 + y}
    to_y_up, to_y_down = {"seq": z * 4 + y_up}, {"seq": z * 4 + y_down}
    greet([{"wshard": p} for p in shards] + [to_z_up, to_z_down, to_y_up, to_y_down])
    pairs = ((x_own, x_all), (z_own, z_all), (o_own, o_all))
    sent = [
        sender.start(own.at[z, y], full.at[x, z, y], {"wshard": p})
        for p in shards
        for own, full in pairs
    ]
    kept = [
        pltpu.make_async_copy(own, full.at[x], local.at[n]) for n, (own, full) in enumerate(pairs)
    ]
    for copy in kept:
        copy.start()
    for copy in sent:
        copy.wait()
    cut = 384
    over_y = ((x_all, slice(0, x_all.shape[-1])), (o_all, slice(0, cut)))
    over_z = ((z_all, slice(0, z_all.shape[-1])), (o_all, slice(cut, o_all.shape[-1])))
    ups, downs = [], []

    def both_ways(refs, up, down):
        ups.append([sender.start(r, r, up) for r in refs])
        downs.append([sender.start(r, r, down) for r in refs])

    for p in shards:
        both_ways([a.at[p, z, y, :, c] for a, c in over_y], to_y_up, to_y_down)
        both_ways([a.at[p, z, y, :, c] for a, c in over_z], to_z_up, to_z_down)
    rest = []
    for n, p in enumerate(shards):
        for copy in ups[2 * n] + ups[2 * n + 1] + downs[2 * n] + downs[2 * n + 1]:
            copy.wait()
        if n != 1:
            refs = [a.at[p, z, y_down, :, c] for a, c in over_y[: 2 if n == 0 else 1]]
            rest += [sender.start(r, r, to_y_up) for r in refs]
            refs = [a.at[p, z_down, y, :, c] for a, c in over_z[: 2 if n == 0 else 1]]
            rest += [sender.start(r, r, to_z_up) for r in refs]
        if n != 0:
            refs = [a.at[p, z, y_up, :, c] for a, c in over_y[0 if n == 1 else 1 :]]
            rest += [sender.start(r, r, to_y_down) for r in refs]
            refs = [a.at[p, z_up, y, :, c] for a, c in over_z[0 if n == 1 else 1 :]]
            rest += [sender.start(r, r, to_z_down) for r in refs]
    for copy in rest:
        copy.wait()
    ups.clear()
    downs.clear()
    for p in shards:
        both_ways([a.at[p, z, :, :, c] for a, c in over_y], to_z_up, to_z_down)
        both_ways([a.at[p, :, y, :, c] for a, c in over_z], to_y_up, to_y_down)
    rest = []
    low, high = slice(0, 2), slice(2, 4)
    for n, p in enumerate(shards):
        for copy in ups[2 * n] + ups[2 * n + 1] + downs[2 * n] + downs[2 * n + 1]:
            copy.wait()
        for a, c in over_y:
            here, there = a.at[p, z_down, low, :, c], a.at[p, z_up, high, :, c]
            rest += [sender.start(here, here, to_z_up), sender.start(there, there, to_z_down)]
        for a, c in over_z:
            here, there = a.at[p, low, y_down, :, c], a.at[p, high, y_up, :, c]
            rest += [sender.start(here, here, to_y_up), sender.start(there, there, to_y_down)]
    for copy in rest:
        copy.wait()
    for copy in kept:
        copy.wait()


def spread_weights(x_own, z_own, o_own):
    own = [a.reshape(4, 4, a.shape[0] // 16, a.shape[1]) for a in (x_own, z_own, o_own)]
    place = pl.BlockSpec(memory_space=pltpu.VMEM)
    count = 9 + 24 + 12 + 24 + 24
    full = pl.pallas_call(
        spread_kernel,
        out_shape=[sds((4,) + a.shape, BF16) for a in own],
        in_specs=[place] * 3,
        out_specs=[place] * 3,
        scratch_shapes=[
            pltpu.SemaphoreType.DMA((count,)),
            pltpu.SemaphoreType.DMA((count,)),
            pltpu.SemaphoreType.DMA((3,)),
        ],
        compiler_params=pltpu.CompilerParams(
            collective_id=3, has_side_effects=True, vmem_limit_bytes=40 * 2**20
        ),
    )(*own)
    return tuple(a.reshape(-1, a.shape[-1]) for a in full)


class Ring:
    def __init__(self, sender, src, index, me, up, down, buf):
        self.sender, self.src, self.index, self.buf = sender, src, index, buf
        self.me, (self.up, self.to_up), (self.down, self.to_down) = me, up, down

    def start(self):
        src, buf, index = self.src, self.buf, self.index
        far = lax.rem(self.me + 2, 4)
        begin = self.sender.start
        self.copies = [
            begin(src.at[index(far, 0)], buf.at[0], self.to_up),
            begin(src.at[index(far, 1)], buf.at[1], self.to_down),
            begin(src.at[index(self.up, 1)], buf.at[4], self.to_up),
            begin(src.at[index(self.down, 0)], buf.at[5], self.to_down),
        ]

    def middle(self):
        src, buf, index = self.src, self.buf, self.index
        for n, (p, device) in enumerate(((self.up, self.to_up), (self.down, self.to_down))):
            self.copies[n].wait()
            total = buf[n].astype(F32) + src[index(p, n)].astype(F32)
            buf[2 + n] = total.astype(buf.dtype)
            self.copies.append(self.sender.start(buf.at[2 + n], buf.at[6 + n], device))

    def finish(self):
        src, buf, index = self.src, self.buf, self.index
        for copy in self.copies[2:]:
            copy.wait()
        for n, other in ((0, 5), (1, 4)):
            total = src[index(self.me, n)].astype(F32) + buf[other].astype(F32)
            yield n, total + buf[6 + n].astype(F32)


def reduce_kernel(cut, a0, b0, a1, b1, small, *refs):
    g_own, g_other = refs[0:3], refs[3:6]
    xr, xs, bx, ring_x, ring_a, total_a, far_a, sum_a, last_a = refs[6:15]
    rings, totals, far = refs[15:21], refs[21:27], refs[27:33]
    f, o = refs[33:36], refs[36:39]
    sender = Sender(refs[39], refs[40])
    core = lax.axis_index("section")
    q = lax.axis_index("seq")
    x = lax.axis_index("wshard")
    z, y = q // 4, lax.rem(q, 4)

    def on_x(d):
        return {"wshard": lax.rem(x + d, 4)}

    def on_y(d):
        return {"seq": z * 4 + lax.rem(y + d, 4)}

    def on_z(d):
        return {"seq": lax.rem(z + d, 4) * 4 + y}

    twin = {"section": 1 - core}
    greet([on(d) for on in (on_x, on_y, on_z) for d in (1, 2, 3)] + [twin])

    def near(me, on):
        return me, (lax.rem(me + 1, 4), on(1)), (lax.rem(me + 3, 4), on(3))

    halves = (slice(0, 2), slice(2, 4))
    everything = slice(None)
    over_x = Ring(sender, b0, lambda p, h: (p, halves[h]), *near(x, on_x), ring_x)
    over_x.start()
    small_x = [sender.start(small, xr.at[d - 1], on_x(d)) for d in (1, 2, 3)]

    low, high = slice(0, cut), slice(cut, b1.shape[-1])
    parts = [
        (a1, everything, 1, False, 0),
        (b1, low, 1, True, 1),
        (b1, high, 1, False, 1),
        (xs.at[0], everything, 0, True, 2),
        (xs.at[1], everything, 1, False, 2),
        (bx, low, 0, True, 1),
        (bx, high, 0, False, 1),
    ]

    def ring_of(n):
        src, cols, _, y_first, _ = parts[n]
        if y_first:
            return Ring(
                sender, src, lambda p, h: (halves[h], p, everything, cols), *near(y, on_y), bufs(n)
            )
        return Ring(
            sender, src, lambda p, h: (p, halves[h], everything, cols), *near(z, on_z), bufs(n)
        )

    def bufs(n):
        return rings[n] if n < 5 else rings[5].at[:, :, :, parts[n][1]]

    def ending(n, ring):
        total = totals[n] if n < 5 else totals[5].at[:, :, parts[n][1]]
        for half, value in ring.finish():
            total[halves[half]] = value.astype(total.dtype)
        y_first = parts[n][3]
        there = far[n] if n < 5 else far[5].at[:, :, parts[n][1]]
        copies = []
        for d in (1, 2, 3):
            to, peer = (lax.rem(z + d, 4), on_z(d)) if y_first else (lax.rem(y + d, 4), on_y(d))
            copies.append(sender.start(total.at[to], there.at[d - 1], peer))
        return total, there, copies

    def closing(n, total, there, copies):
        _, cols, layer, y_first, kind = parts[n]
        for copy in copies:
            copy.wait()
        value = total[z if y_first else y].astype(F32)
        for d in range(3):
            value = value + there[d].astype(F32)
        f[kind][layer, :, cols] = value.astype(f[kind].dtype)

    mid = a0.shape[-1] // 2
    sides = (slice(0, mid), slice(mid, 2 * mid))
    wide = [
        Ring(
            sender, a0, lambda p, h: (halves[h], everything, p, everything, sides[0]),
            *near(y, on_y), ring_a.at[0],
        ),
        Ring(
            sender, a0, lambda p, h: (halves[h], p, everything, everything, sides[1]),
            *near(z, on_z), ring_a.at[1],
        ),
    ]
    running = [ring_of(n) for n in range(7)]
    for ring in wide:
        ring.start()
    for n in range(3):
        running[n].start()
    for copy in small_x:
        copy.wait()
    xs[...] = small[...] + xr[0] + xr[1] + xr[2]
    running[3].start()
    running[4].start()
    for ring in wide:
        ring.middle()
    over_x.middle()
    for n in range(5):
        running[n].middle()
    wide_copies = []
    for side, ring in enumerate(wide):
        for half, value in ring.finish():
            total_a[side, halves[half]] = value.astype(BF16)
        for d in (1, 2, 3):
            to, peer = (lax.rem(y + d, 4), on_y(d)) if side else (lax.rem(z + d, 4), on_z(d))
            wide_copies.append(
                sender.start(total_a.at[side, :, to], far_a.at[side, d - 1], peer)
            )
    for half, value in over_x.finish():
        bx[halves[half]] = value.astype(bx.dtype)
    running[5].start()
    running[6].start()
    ended = [ending(n, running[n]) for n in range(5)]
    last_copies = []
    for side in (0, 1):
        for copy in wide_copies[3 * side : 3 * side + 3]:
            copy.wait()
        value = total_a[side, :, y if side else z].astype(F32)
        for d in range(3):
            value = value + far_a[side, d].astype(F32)
        sum_a[side] = value.astype(BF16)
        for d in (1, 2, 3):
            here = sum_a.at[side, lax.rem(x + d, 4)]
            last_copies.append(sender.start(here, last_a.at[side, d - 1], on_x(d)))
    running[5].middle()
    running[6].middle()
    for n in range(5):
        closing(n, *ended[n])
    ended += [ending(n, running[n]) for n in (5, 6)]
    for side in (0, 1):
        for copy in last_copies[3 * side : 3 * side + 3]:
            copy.wait()
        value = sum_a[side, x].astype(F32)
        for d in range(3):
            value = value + last_a[side, d].astype(F32)
        f[0][0, :, sides[side]] = value.astype(BF16)
    for n in (5, 6):
        closing(n, *ended[n])
    twins = [sender.start(f[n].at[1 - core], o[n], twin) for n in range(3)]
    gather = []
    for n in range(3):
        g_own[n][z, y] = f[n][core]
        for d in (1, 2, 3):
            gather.append(sender.start(f[n].at[core], g_own[n].at[z, y], on_y(d)))
    for copy in twins:
        copy.wait()
    for n in range(3):
        g_other[n][z, y] = o[n][...]
        for d in (1, 2, 3):
            gather.append(sender.start(o[n], g_other[n].at[z, y], on_z(d)))
    for copy in gather:
        copy.wait()
    _, (z_up, to_z_up), (z_down, to_z_down) = near(z, on_z)
    _, (y_up, to_y_up), (y_down, to_y_down) = near(y, on_y)
    gather = []
    for own, other in zip(g_own, g_other):
        for device in (to_z_up, to_z_down):
            gather.append(sender.start(own.at[z], own.at[z], device))
        for device in (to_y_up, to_y_down):
            gather.append(sender.start(other.at[:, y], other.at[:, y], device))
    last = []
    for n, (own, other) in enumerate(zip(g_own, g_other)):
        for copy in gather[4 * n : 4 * n + 4]:
            copy.wait()
        for half, z_to, y_to, z_from, y_from in (
            (halves[0], to_z_up, to_y_up, z_down, y_down),
            (halves[1], to_z_down, to_y_down, z_up, y_up),
        ):
            here = own.at[z_from, half]
            last.append(sender.start(here, here, z_to))
            here = other.at[half, y_from]
            last.append(sender.start(here, here, y_to))
    for copy in last:
        copy.wait()


def reduce_all(a0, b0, a1, b1, small):
    kinds = [(a.shape[2:], a.dtype) for a in (a1, b1, small[0])]
    cut = 6 * LANE
    wide = b1.shape[-1]
    rows, mid = a1.shape[2], a1.shape[3] // 2
    thin = [((rows, c), BF16) for c in (cut, wide - cut)]
    full = [sds((4, 4) + shape, dtype) for shape, dtype in kinds]
    order = [kinds[0], thin[0], thin[1], kinds[2], kinds[2], kinds[1]]

    def vmem(shapes, *lead):
        return [pltpu.VMEM(lead + shape, dtype) for shape, dtype in shapes]

    count = 6 + 3 + 2 * 12 + 7 * 9 + 3 + 18 + 12 + 12
    scratch = [
        pltpu.VMEM((3,) + small.shape, F32),
        pltpu.VMEM(small.shape, F32),
        pltpu.VMEM(b1.shape, BF16),
        pltpu.VMEM((8, 2) + b1.shape[1:], BF16),
        pltpu.VMEM((2, 8, 2, 4, rows, mid), BF16),
        pltpu.VMEM((2, 4, 4, rows, mid), BF16),
        pltpu.VMEM((2, 3, 4, rows, mid), BF16),
        pltpu.VMEM((2, 4, rows, mid), BF16),
        pltpu.VMEM((2, 3, rows, mid), BF16),
        *vmem(order, 8, 2), *vmem(order, 4), *vmem(order, 3), *vmem(kinds, 2), *vmem(kinds),
        pltpu.SemaphoreType.DMA((count,)),
        pltpu.SemaphoreType.DMA((count,)),
    ]
    place = pl.BlockSpec(memory_space=pltpu.VMEM)
    out = pl.pallas_call(
        functools.partial(reduce_kernel, cut),
        out_shape=full + full,
        in_specs=[place] * 5,
        out_specs=[place] * 6,
        scratch_shapes=scratch,
        compiler_params=pltpu.CompilerParams(
            collective_id=0, has_side_effects=True, vmem_limit_bytes=48 * 2**20
        ),
    )(a0, b0, a1, b1, small)
    return out[0:3], out[3:6]


def forward(u, w, p):
    w_x, w_z, w_out = w
    gain_in, cw, cb, hp, gain_out = p
    seqs, rows, width = u.shape
    chan = cw.shape[1]
    taps = 4
    inner = gain_out.shape[1]
    states = LANE
    uf = u.astype(F32)
    inv = lax.rsqrt(jnp.mean(uf * uf, axis=-1, keepdims=True) + EPS)
    normed = (uf * inv * gain_in).astype(BF16).reshape(seqs * rows, width)
    xd = jnp.dot(normed, w_x, preferred_element_type=F32).astype(BF16)
    xd = xd.reshape(seqs, rows, chan + LANE)
    z = jnp.dot(normed, w_z, preferred_element_type=F32).reshape(seqs, rows, inner)
    halo = shift(xd[:, rows - TAIL :, :chan], "seq", 1)
    act, cum, step, sloc = run(
        functools.partial(chunk_kernel, taps),
        (xd, halo, cw, cb, hp),
        (
            sds((seqs, rows, chan), F32),
            sds((seqs, rows, LANE), F32),
            sds((seqs, rows, LANE), F32),
            sds((seqs * inner // LANE, states + TAIL, LANE), BF16),
        ),
        [pltpu.VMEM((TAIL + rows, chan), F32)],
        (2, 3, 4),
    )
    (yi,) = run(intra_kernel, (act, cum, step), (sds((seqs, rows, inner), F32),))
    decay, sin = scan_chunks(sloc, None, False, states)
    yy, gg, ss = run(
        finish_kernel,
        (act, cum, yi, sin, z, hp, gain_out),
        (
            sds((seqs, rows, inner), F32),
            sds((seqs, rows, inner), BF16),
            sds((seqs, rows, 1), F32),
        ),
        (),
        (5, 6),
    )
    mine = jnp.dot(gg.reshape(seqs * rows, inner), w_out, preferred_element_type=F32)
    mine = mine.astype(BF16).reshape(seqs, rows, width)
    theirs, ss_theirs = swap(mine), swap(ss)
    branch = mine.astype(F32) + theirs.astype(F32)
    rn = lax.rsqrt((ss + ss_theirs) * (1.0 / (2 * inner)) + EPS)
    result = (uf + rn * branch).astype(BF16)
    kept = (u, inv, normed, z, xd, halo, act, cum, step, decay, sin, yy, branch, rn)
    return result, kept


def backward(e, kept, w, p, over_wshard):
    w_x, w_z, w_out = w
    gain_in, cw, cb, hp, gain_out = p
    u, inv, normed, z, xd, halo, act, cum, step, decay, sin, yy, branch, rn = kept
    seqs, rows, width = e.shape
    chan = cw.shape[1]
    taps = 4
    inner = gain_out.shape[1]
    states = LANE
    ef = e.astype(F32)
    e2 = e.reshape(seqs * rows, width)
    nt = (((1,), (1,)), ((), ()))
    tn = (((0,), (0,)), ((), ()))
    gr = lax.dot_general(e2, w_out, nt, preferred_element_type=F32).reshape(seqs, rows, inner)
    rs = jnp.sum(ef * branch, axis=-1, keepdims=True)
    dy, gz, dsl, dgain, gated = run(
        gate_back_kernel,
        (gr, z, yy, act, cum, rn, rs, hp, gain_out),
        (
            sds((seqs, rows, inner), BF16),
            sds((seqs, rows, inner), BF16),
            sds((seqs * inner // LANE, states, LANE), BF16),
            sds((seqs, inner // LANE, LANE), F32),
            sds((seqs, rows, inner), BF16),
        ),
        (),
        (7, 8),
    )
    gz = gz.reshape(seqs * rows, inner)
    part_z = lax.dot_general(gz, w_z, nt, preferred_element_type=F32)
    early = jnp.concatenate(
        [
            lax.dot_general(normed, gz, tn, preferred_element_type=F32),
            lax.dot_general(
                gated.reshape(seqs * rows, inner), e2, tn, preferred_element_type=F32
            ),
        ],
        axis=1,
    ).astype(BF16)
    if over_wshard:
        early = lax.psum_scatter(early, "wshard", scatter_dimension=0, tiled=True)
    dxs, dbc, dci = run(
        intra_back_kernel,
        (act, cum, step, dy),
        (
            sds((seqs, rows, inner), F32),
            sds((seqs, rows, 2 * LANE), F32),
            sds((seqs, rows, LANE), F32),
        ),
    )
    (grad,) = scan_chunks(dsl, decay, True, states)
    dpre, ddt, small = run(
        functools.partial(mix_back_kernel, taps),
        (xd, halo, cw, cb, hp, act, cum, step, dy, dxs, dbc, dci, grad, sin),
        (
            sds((seqs, rows, chan), F32),
            sds((seqs, rows, LANE), BF16),
            sds((seqs, 56, LANE), F32),
        ),
        [pltpu.VMEM((TAIL + rows, chan), F32), pltpu.VMEM((rows, chan), F32)],
        (2, 3, 4),
    )
    after = shift(dpre[:, :8], "seq", -1)
    (gp,) = run(
        functools.partial(conv_back_kernel, taps),
        (dpre, after, ddt, cw),
        (sds((seqs, rows, chan + LANE), BF16),),
        [pltpu.VMEM((rows + 8, chan), F32)],
        (3,),
    )
    gp = gp.reshape(seqs * rows, -1)
    mine = part_z + lax.dot_general(gp, w_x, nt, preferred_element_type=F32)
    mine = mine.astype(BF16).reshape(seqs, rows, width)
    theirs = swap(mine)
    gn = mine.astype(F32) + theirs.astype(F32)
    uf = u.astype(F32)
    unit = uf * inv
    g_gain_in = jnp.sum(gn * unit, axis=(0, 1))
    scaled = gn * gain_in
    dot = jnp.mean(scaled * unit, axis=-1, keepdims=True)
    grad_u = ef + inv * (scaled - unit * dot)
    late = lax.dot_general(normed, gp, tn, preferred_element_type=F32).astype(BF16)
    if over_wshard:
        late = lax.psum_scatter(late, "wshard", scatter_dimension=0, tiled=True)
    rows_of = [small.sum(0)[: small.shape[1] - 3], dgain.sum(0), g_gain_in.reshape(-1, LANE)]
    used = sum(a.shape[0] for a in rows_of)
    smalls = jnp.concatenate(rows_of + [jnp.zeros((16 * 8 - used, LANE), F32)], axis=0)
    return grad_u, (early, late), smalls.reshape(4, 4, 8, LANE)


def body(
    hidden, out_grad, norm_gain, in_weight, conv_weight, conv_bias, dt_bias, a_log, d_skip,
    out_gain, out_weight,
):
    core = lax.axis_index("section")
    width = hidden.shape[2]
    full = out_gain.shape[1]
    taps = conv_weight.shape[1]
    head_count = dt_bias.shape[1]
    proj = in_weight.shape[2]
    bc_at, dt_at = 2 * full, proj - head_count

    wi, wo = in_weight[0], out_weight[0]

    def pack(which):
        out_rows = wo.reshape(2, wo.shape[0] // 2, wo.shape[1])
        x_part = jnp.concatenate(
            [
                half(wi[:, full:bc_at], which),
                wi[:, bc_at:dt_at],
                jnp.pad(half(wi[:, dt_at:], which), ((0, 0), (0, LANE - head_count // 2))),
            ],
            axis=1,
        )
        out_part = lax.dynamic_index_in_dim(out_rows, which, 0, keepdims=False)
        return x_part, half(wi[:, :full], which), out_part

    own, sent = pack(core), pack(1 - core)
    came = jax.tree.map(swap, sent)
    sizes = (norm_gain, conv_weight, conv_bias, dt_bias, a_log, d_skip, out_gain)
    flat = jnp.concatenate([a[0].reshape(-1) for a in sizes])
    flat_other = swap(flat)

    def params(layer):
        mine = core == layer
        w = tuple(jnp.where(mine, a, b) for a, b in zip(own, came))
        if layer == 0:
            w = spread_weights(*w)
        else:
            w = tuple(lax.all_gather(a, "wshard", axis=0, tiled=True) for a in w)
        v = jnp.where(mine, flat, flat_other)
        parts, at = [], 0
        for a in sizes:
            count = a[0].size
            parts.append(v[at : at + count].reshape(a[0].shape))
            at += count
        gain_in, cw, cb, dtb, al, ds, gain_out = parts

        def channels(a):
            return jnp.concatenate([half(a[..., :full], core), a[..., full:]], axis=-1)

        hp = jnp.stack([half(a, core) for a in (dtb, al, ds)])
        hp = jnp.pad(hp, ((0, 5), (0, LANE - hp.shape[1])))
        cw = jnp.pad(channels(cw), ((0, 8 - taps), (0, 0)))
        return w, (
            gain_in[None],
            cw,
            channels(cb)[None],
            hp,
            half(gain_out, core)[None],
        )

    w0, p0 = params(0)
    w1, p1 = params(1)
    first, kept0 = forward(hidden, w0, p0)
    second, kept1 = forward(first, w1, p1)
    layer_out = jnp.where(core == 0, first, second)[None]
    grad1, products1, smalls1 = backward(out_grad, kept1, w1, p1, True)
    passed = grad1.astype(BF16)
    grad0, products0, smalls0 = backward(passed, kept0, w0, p0, False)
    section_grad = jnp.where(core == 0, grad0, passed.astype(F32))[None]

    rows = width // 64
    a0, b0 = (a.reshape(4, 4, 4, rows, a.shape[1]) for a in products0)
    a1, b1 = (a.reshape(4, 4, rows, a.shape[1]) for a in products1)
    mine, other = reduce_all(a0, b0, a1, b1, jnp.stack([smalls0, smalls1]))
    grad_in, grad_out, gains, conv_g, bias_g, heads_g, out_gains = assemble(
        core, mine, other, proj, head_count, taps
    )
    return (
        layer_out,
        section_grad,
        gains.reshape(1, width),
        grad_in.T[None],
        conv_g[None],
        bias_g,
        heads_g[0:1, :head_count],
        heads_g[1:2, :head_count],
        heads_g[2:3, :head_count],
        out_gains,
        grad_out.reshape(1, -1, width),
    )


def solution(mesh):
    by_layer = P("section", None)
    weights = P("section", "wshard", None)
    tokens = P("wshard", "seq", None)
    stacked = P("section", "wshard", "seq", None)
    conv = P("section", None, None)
    in_specs = (
        tokens, tokens, by_layer, weights, conv, by_layer, by_layer, by_layer, by_layer, by_layer,
        weights,
    )
    out_specs = (
        stacked, stacked, by_layer, weights, conv, by_layer, by_layer, by_layer, by_layer,
        by_layer, weights,
    )
    return jax.shard_map(body, mesh=mesh, in_specs=in_specs, out_specs=out_specs, check_vma=False)
```

```python
import functools

import jax
import jax.numpy as jnp
from jax import lax
from jax.experimental import pallas as pl
from jax.experimental.pallas import tpu as pltpu
from jax.sharding import PartitionSpec as P

F32 = jnp.float32
BF16 = jnp.bfloat16
HI = lax.Precision.HIGHEST
EPS = 1e-05
HDIM = 64
LANE = 128
TAIL = 16


def shift(x, axis, by):
    devices = lax.axis_size(axis)
    pairs = [(i, i + by) for i in range(devices) if 0 <= i + by < devices]
    return lax.ppermute(x, axis, pairs)


def swap(x):
    return lax.ppermute(x, "section", [(0, 1), (1, 0)])


def half(a, which):
    width = a.shape[-1] // 8
    b = a.reshape(a.shape[:-1] + (4, 2, width))
    b = lax.dynamic_index_in_dim(b, which, axis=b.ndim - 2, keepdims=False)
    return b.reshape(a.shape[:-1] + (4 * width,))


def whole(own, other, core):
    width = own.shape[-1] // 4
    lead = own.shape[:-1]
    own, other = own.reshape(lead + (4, 1, width)), other.reshape(lead + (4, 1, width))
    first, second = jnp.where(core == 0, own, other), jnp.where(core == 0, other, own)
    return jnp.concatenate([first, second], axis=-2).reshape(lead + (8 * width,))


def mm(a, b):
    return jnp.dot(a.astype(BF16), b.astype(BF16), preferred_element_type=F32)


def mm_nt(a, b):
    return lax.dot_general(
        a.astype(BF16), b.astype(BF16), (((1,), (1,)), ((), ())), preferred_element_type=F32
    )


def mm_tn(a, b):
    return lax.dot_general(
        a.astype(BF16), b.astype(BF16), (((0,), (0,)), ((), ())), preferred_element_type=F32
    )


def spread_matrix(width):
    head = lax.broadcasted_iota(jnp.int32, (LANE, width), 0)
    lane = lax.broadcasted_iota(jnp.int32, (LANE, width), 1)
    return jnp.where(lane // HDIM == head, 1.0, 0.0).astype(BF16)


def split(v):
    high = v.astype(BF16)
    return high, (v - high.astype(F32)).astype(BF16)


def spread(heads, matrix):
    high, rest = split(heads)
    return mm(high, matrix) + mm(rest, matrix)


def gather_heads(lanes, matrix):
    high, rest = split(lanes)
    return mm_nt(high, matrix) + mm_nt(rest, matrix)


def tri(rows, upper):
    r = lax.broadcasted_iota(jnp.int32, (rows, rows), 0)
    c = lax.broadcasted_iota(jnp.int32, (rows, rows), 1)
    return jnp.where((c >= r) if upper else (r >= c), 1.0, 0.0).astype(F32)


def steps(dt, hp):
    shifted = dt + hp[0:1, :]
    step = jnp.maximum(shifted, 0.0) + jnp.log1p(jnp.exp(-jnp.abs(shifted)))
    rate = -jnp.exp(hp[1:2, :])
    return shifted, step, rate


def sigmoid(v):
    return 1.0 / (1.0 + jnp.exp(-v))


def conv_pre(buf, cw, cb, taps, rows):
    pre = cb[0:1, :]
    for k in range(taps):
        start = TAIL - (taps - 1) + k
        pre = pre + cw[k : k + 1, :] * buf[start : start + rows, :]
    return pre


MESH = pl.DeviceIdType.MESH


class Sender:
    def __init__(self, send, recv):
        self.send, self.recv, self.used = send, recv, 0

    def start(self, src, dst, device):
        n = self.used
        self.used += 1
        copy = pltpu.make_async_remote_copy(
            src_ref=src,
            dst_ref=dst,
            send_sem=self.send.at[n],
            recv_sem=self.recv.at[n],
            device_id=device,
            device_id_type=MESH,
        )
        copy.start()
        return copy


def greet(devices):
    barrier = pltpu.get_barrier_semaphore()
    for device in devices:
        pl.semaphore_signal(barrier, inc=1, device_id=device, device_id_type=MESH)
    pl.semaphore_wait(barrier, len(devices))


def chunk_kernel(taps, xd, halo, cw, cb, hp, act_o, cum_o, step_o, sloc_o, buf):
    rows, inner, chan = xd.shape[1], sloc_o.shape[0] * LANE, cw.shape[1]
    buf[0:TAIL, :] = halo[0].astype(F32)
    buf[TAIL : TAIL + rows, :] = xd[0, :, 0:chan].astype(F32)
    pre = conv_pre(buf, cw, cb, taps, rows)
    act = pre * sigmoid(pre)
    act_o[0] = act
    _, step, rate = steps(xd[0, :, chan : chan + LANE].astype(F32), hp)
    cum = jnp.dot(tri(rows, False), step * rate, precision=HI, preferred_element_type=F32)
    cum_o[0] = cum
    step_o[0] = step
    last = cum[rows - 1 : rows, :]
    matrix = spread_matrix(inner)
    weight = spread(jnp.exp(last - cum) * step, matrix)
    decay = spread(jnp.broadcast_to(jnp.exp(last), (8, LANE)), matrix)[0:1, :]
    d_hi = decay.astype(BF16).astype(F32)
    d_mid = (decay - d_hi).astype(BF16).astype(F32)
    d_lo = decay - d_hi - d_mid
    row = lax.broadcasted_iota(jnp.int32, (TAIL, inner), 0)
    extra = jnp.where(row == 0, d_hi, jnp.where(row == 1, d_mid, jnp.where(row == 2, d_lo, 0.0)))
    extra = extra.astype(BF16)
    xw = (act[:, :inner] * weight).astype(BF16)
    b = act[:, inner : inner + LANE].astype(BF16)
    sloc = mm_tn(b, xw).astype(BF16)
    states = sloc.shape[0]
    for i in range(inner // LANE):
        sloc_o[i, 0:states, :] = sloc[:, i * LANE : (i + 1) * LANE]
        sloc_o[i, states : states + TAIL, :] = extra[:, i * LANE : (i + 1) * LANE]


def one(ref, s):
    count = ref.shape[0] // 2
    return ref.at[pl.ds(s * count, count)]


def scan_kernel(reverse, with_decay, pieces_ref, *refs):
    got, done, send_a, recv_a, send_b, recv_b = refs[-6:]
    if with_decay:
        decay, out = refs[3], refs[5]
        inside, ins, outs = intra_kernel, refs[0:3], refs[4:5]
    else:
        decay, out = refs[0], refs[8]
        inside, ins, outs = intra_back_kernel, refs[1:5], refs[5:8]
    count, states = out.shape[0], out.shape[1]
    q = lax.axis_index("seq")
    peers = [lax.rem(q + d, count) for d in range(1, count)]
    greet([{"seq": p} for p in peers])

    def copy(src, dst, send, recv, n, peer, slot):
        return pltpu.make_async_remote_copy(
            src_ref=src.at[peer],
            dst_ref=dst.at[slot],
            send_sem=send.at[n],
            recv_sem=recv.at[slot],
            device_id={"seq": peer},
            device_id_type=MESH,
        )

    sent = [copy(pieces_ref, got, send_a, recv_a, n, p, q) for n, p in enumerate(peers)]
    for c in sent:
        c.start()
    got[q] = pieces_ref[q]
    for s in range(2):
        inside(*[one(a, s) for a in ins + outs])
    for n, p in enumerate(peers):
        copy(pieces_ref, got, send_a, recv_a, n, p, p).wait_recv()
    carry = jnp.zeros((states, LANE), F32)
    order = range(count - 1, -1, -1) if reverse else range(count)
    for j in order:
        if with_decay:
            tail = got[j, states : states + TAIL, :].astype(F32)
            decay[j : j + 1, :] = tail[0:1, :] + tail[1:2, :] + tail[2:3, :]
        done[j] = carry.astype(BF16)
        carry = carry * decay[j : j + 1, :] + got[j, 0:states, :].astype(F32)
    back = [copy(done, out, send_b, recv_b, n, p, q) for n, p in enumerate(peers)]
    for c in back:
        c.start()
    out[q] = done[q]
    for n, p in enumerate(peers):
        copy(done, out, send_b, recv_b, n, p, p).wait_recv()
    for c in sent + back:
        c.wait_send()


def intra_kernel(act, cum, step, yi_o):
    rows, inner = yi_o.shape[1], yi_o.shape[2]
    b = act[0, :, inner : inner + LANE]
    c = act[0, :, inner + LANE : inner + 2 * LANE]
    cb = mm_nt(c, b)
    cum_v = cum[0]
    cum_t = jnp.transpose(cum_v)
    xs = act[0, :, :inner] * spread(step[0], spread_matrix(inner))
    keep = tri(rows, False) > 0
    low = lax.broadcasted_iota(jnp.int32, (rows, LANE), 1) < HDIM
    for i in range(inner // LANE):
        xs_i = xs[:, i * LANE : (i + 1) * LANE].astype(BF16)
        parts = []
        for h in (2 * i, 2 * i + 1):
            diff = cum_v[:, h : h + 1] - cum_t[h : h + 1, :]
            decay = jnp.exp(jnp.where(keep, diff, -1e30))
            parts.append(mm(cb * decay, xs_i))
        yi_o[0, :, i * LANE : (i + 1) * LANE] = jnp.where(low, parts[0], parts[1])


def finish_kernel(act, cum, yi, sin, z, hp, gain, yy_o, gg_o, ss_o):
    inner = yi.shape[2]
    matrix = spread_matrix(inner)
    grown = spread(jnp.exp(cum[0]), matrix)
    skip = spread(jnp.broadcast_to(hp[2:3, :], (8, LANE)), matrix)[0:1, :]
    c = act[0, :, inner + LANE : inner + 2 * LANE].astype(BF16)
    total = jnp.zeros((yi.shape[1], LANE), F32)
    for i in range(inner // LANE):
        at = slice(i * LANE, (i + 1) * LANE)
        yy = yi[0, :, at] + grown[:, at] * mm(c, sin[i])
        yy_o[0, :, at] = yy
        mixed = (yy + skip[:, at] * act[0, :, at]).astype(BF16).astype(F32)
        zi = z[0, :, at]
        g = mixed * (zi * sigmoid(zi))
        total = total + g * g
        gg_o[0, :, at] = (g * gain[0:1, at]).astype(BF16)
    ss_o[0] = jnp.sum(total, axis=1, keepdims=True)


def gate_back_kernel(
    gr, z, yy, act, cum, rn, rs, hp, gain, dy_o, gz_o, dsl_o, dgain_o, gated_o
):
    inner = gr.shape[2]
    matrix = spread_matrix(inner)
    grown = spread(jnp.exp(cum[0]), matrix)
    skip = spread(jnp.broadcast_to(hp[2:3, :], (8, LANE)), matrix)[0:1, :]
    c = act[0, :, inner + LANE : inner + 2 * LANE].astype(BF16)
    r = rn[0]
    k = r * r * r * rs[0] * (1.0 / (2 * inner))
    for i in range(inner // LANE):
        at = slice(i * LANE, (i + 1) * LANE)
        mixed = (yy[0, :, at] + skip[:, at] * act[0, :, at]).astype(BF16).astype(F32)
        zi = z[0, :, at]
        sg = sigmoid(zi)
        silu = zi * sg
        g = mixed * silu
        gr_i = gr[0, :, at]
        gain_i = gain[0:1, at]
        normal = g * r
        dgain_o[0, i : i + 1, :] = jnp.sum(gr_i * normal, axis=0, keepdims=True)
        gated_o[0, :, at] = (normal * gain_i).astype(BF16)
        dg = r * (gain_i * gr_i) - g * k
        dy = (dg * silu).astype(BF16)
        dy_o[0, :, at] = dy
        gz_o[0, :, at] = (dg * mixed * (sg * (1.0 + zi * (1.0 - sg)))).astype(BF16)
        dsl_o[i] = mm_tn(c, dy.astype(F32) * grown[:, at]).astype(BF16)


def intra_back_kernel(act, cum, step, dy, dxs_o, dbc_o, dcum_o):
    rows, inner = dxs_o.shape[1], dxs_o.shape[2]
    b = act[0, :, inner : inner + LANE].astype(BF16)
    c = act[0, :, inner + LANE : inner + 2 * LANE].astype(BF16)
    cb = mm_nt(c, b)
    cum_v = cum[0]
    cum_t = jnp.transpose(cum_v)
    xs = act[0, :, :inner] * spread(step[0], spread_matrix(inner))
    keep = tri(rows, False) > 0
    low = lax.broadcasted_iota(jnp.int32, (rows, LANE), 1) < HDIM
    dcb = jnp.zeros((rows, rows), F32)
    lane = lax.broadcasted_iota(jnp.int32, (rows, LANE), 1)
    row_sums = jnp.zeros((rows, LANE), F32)
    col_sums = []
    for i in range(inner // LANE):
        at = slice(i * LANE, (i + 1) * LANE)
        xs_i = xs[:, at]
        dy_i = dy[0, :, at].astype(F32)
        parts = []
        for n, h in enumerate((2 * i, 2 * i + 1)):
            diff = cum_v[:, h : h + 1] - cum_t[h : h + 1, :]
            decay = jnp.exp(jnp.where(keep, diff, -1e30))
            mine = jnp.where(low, dy_i, 0.0) if n == 0 else jnp.where(low, 0.0, dy_i)
            flow = mm_nt(mine, xs_i) * decay
            dcb = dcb + flow
            both = flow * cb
            row_sums = jnp.where(lane == h, jnp.sum(both, axis=1, keepdims=True), row_sums)
            col_sums.append(jnp.sum(both, axis=0, keepdims=True))
            parts.append(mm_tn(cb * decay, dy_i))
        dxs_o[0, :, at] = jnp.where(low, parts[0], parts[1])
    col_sums.append(jnp.zeros((LANE - len(col_sums), rows), F32))
    dcum_o[0] = row_sums - jnp.transpose(jnp.concatenate(col_sums, axis=0))
    dbc_o[0, :, 0:LANE] = mm_tn(dcb, c)
    dbc_o[0, :, LANE : 2 * LANE] = mm(dcb, b)


def mix_back_kernel(
    taps, xd, halo, cw, cb, hp, act, cum, step, dy, dxs, dbc, dci, grad, sin,
    dpre_o, ddt_o, small_o, buf, dact,
):
    rows, inner, chan = dy.shape[1], dy.shape[2], cw.shape[1]
    matrix = spread_matrix(inner)
    cum_v, step_v = cum[0], step[0]
    last = cum_v[rows - 1 : rows, :]
    step_e = spread(step_v, matrix)
    tail_e = spread(jnp.exp(last - cum_v), matrix)
    grown = spread(jnp.exp(cum_v), matrix)
    d_e = grown[rows - 1 : rows, :]
    skip = spread(jnp.broadcast_to(hp[2:3, :], (8, LANE)), matrix)[0:1, :]
    b = act[0, :, inner : inner + LANE].astype(BF16)
    c = act[0, :, inner + LANE : inner + 2 * LANE].astype(BF16)
    q1 = dci[0]
    qb = jnp.zeros((rows, LANE), F32)
    q2 = jnp.zeros((rows, LANE), F32)
    flows = jnp.zeros((8, LANE), F32)
    skips = jnp.zeros((8, LANE), F32)
    db, dc = dbc[0, :, 0:LANE], dbc[0, :, LANE : 2 * LANE]
    for i in range(inner // LANE):
        at = slice(i * LANE, (i + 1) * LANE)
        g = grad[i]
        x = act[0, :, at]
        dy_i = dy[0, :, at].astype(F32)
        s_i = sin[i]
        back = tail_e[:, at] * mm(b, g)
        v = dxs[0, :, at] + back
        dact[:, at] = step_e[:, at] * v + skip[:, at] * dy_i
        part = matrix[:, at]
        q1 = q1 + gather_heads(dy_i * grown[:, at] * mm(c, s_i), part)
        q2 = q2 + gather_heads(x * v, part)
        qb = qb + gather_heads(x * back, part)
        flow = d_e[:, at] * jnp.sum(g.astype(F32) * s_i.astype(F32), axis=0, keepdims=True)
        flows = flows + gather_heads(jnp.broadcast_to(flow, (8, LANE)), part)
        skip_i = jnp.sum(dy_i * x, axis=0, keepdims=True)
        skips = skips + gather_heads(jnp.broadcast_to(skip_i, (8, LANE)), part)
        db = db + mm_nt(tail_e[:, at] * step_e[:, at] * x, g)
        dc = dc + mm_nt(dy_i * grown[:, at], s_i)
    dact[:, inner : inner + LANE] = db
    dact[:, inner + LANE : inner + 2 * LANE] = dc
    shifted, _, rate = steps(xd[0, :, chan : chan + LANE].astype(F32), hp)
    later = jnp.dot(tri(rows, True), q1, precision=HI, preferred_element_type=F32)
    strict = 1.0 - tri(rows, True)
    sooner = jnp.dot(strict, step_v * qb, precision=HI, preferred_element_type=F32)
    da = later + sooner + flows[0:1, :]
    ddt = (q2 + rate * da) * sigmoid(shifted)
    ddt_o[0] = ddt.astype(BF16)
    small_o[0] = jnp.zeros(small_o.shape[1:], F32)
    top, low = inner // LANE, 2
    at = (taps + 1) * (top + low)
    small_o[0, at : at + 1, :] = jnp.sum(ddt, axis=0, keepdims=True)
    small_o[0, at + 1 : at + 2, :] = jnp.sum(da * step_v, axis=0, keepdims=True) * rate
    small_o[0, at + 2 : at + 3, :] = skips[0:1, :]
    buf[0:TAIL, :] = halo[0].astype(F32)
    buf[TAIL : TAIL + rows, :] = xd[0, :, 0:chan].astype(F32)
    pre = conv_pre(buf, cw, cb, taps, rows)
    sg = sigmoid(pre)
    dpre = dact[...] * (sg * (1.0 + pre * (1.0 - sg)))
    dpre_o[0] = dpre
    for k in range(taps + 1):
        start = TAIL - (taps - 1) + k
        terms = dpre if k == taps else dpre * buf[start : start + rows, :]
        total = jnp.sum(terms, axis=0, keepdims=True)
        for i in range(top + low):
            to = k * top + i if i < top else (taps + 1) * top + k * low + i - top
            small_o[0, to : to + 1, :] = total[:, i * LANE : (i + 1) * LANE]


def conv_back_kernel(taps, dpre, after, ddt, cw, out, buf):
    rows, chan = dpre.shape[1], dpre.shape[2]
    buf[0:rows, :] = dpre[0]
    buf[rows : rows + 8, :] = after[0]
    total = cw[taps - 1 : taps, :] * buf[0:rows, :]
    for k in range(taps - 1):
        start = taps - 1 - k
        total = total + cw[k : k + 1, :] * buf[start : start + rows, :]
    out[0, :, 0:chan] = total.astype(BF16)
    out[0, :, chan : chan + LANE] = ddt[0]


def per_seq(shape):
    block = (shape[0] // 2,) + shape[1:]
    return pl.BlockSpec(block, lambda s: (s,) + (0,) * (len(shape) - 1))


def same(shape):
    return pl.BlockSpec(shape, lambda s: (0,) * len(shape))


def run(kernel, ins, outs, scratch=(), shared=()):
    return pl.pallas_call(
        kernel,
        grid=(2,),
        in_specs=[(same if n in shared else per_seq)(a.shape) for n, a in enumerate(ins)],
        out_specs=[per_seq(o.shape) for o in outs],
        out_shape=list(outs),
        scratch_shapes=list(scratch),
        compiler_params=pltpu.CompilerParams(vmem_limit_bytes=20 * 2**20),
    )(*ins)


def sds(shape, dtype):
    return jax.ShapeDtypeStruct(shape, dtype)


def scan_chunks(pieces, decay, reverse, states, inside, results):
    count, height = pieces.shape[0], pieces.shape[1]
    place = pl.BlockSpec(memory_space=pltpu.VMEM)
    outs = [*results, sds((count, states, LANE), BF16)]
    if decay is None:
        outs = [sds((count, LANE), F32)] + outs
    ins = (pieces,) + (() if decay is None else (decay,)) + inside
    sems = [pltpu.SemaphoreType.DMA((count,))] * 4
    return pl.pallas_call(
        functools.partial(scan_kernel, reverse, decay is None),
        out_shape=outs,
        in_specs=[place] * len(ins),
        out_specs=[place] * len(outs),
        scratch_shapes=[
            pltpu.VMEM((count, height, LANE), BF16),
            pltpu.VMEM((count, states, LANE), BF16),
            *sems,
        ],
        compiler_params=pltpu.CompilerParams(
            collective_id=1 + reverse, has_side_effects=True, vmem_limit_bytes=16 * 2**20
        ),
    )(*ins)


def assemble_kernel(
    head_count, taps, core, e, w, l, v, eo, wo, lo, vo, in_o, out_o, gain_o, conv_o, bias_o, heads_o, og_o
):
    inner = e.shape[1]
    wide = inner // 4
    bc = l.shape[1] - inner - LANE
    zero = core[0] == 0
    i = lax.broadcasted_iota(jnp.int32, (LANE, LANE), 0)
    j = lax.broadcasted_iota(jnp.int32, (LANE, LANE), 1)
    per = head_count // 8
    spot = 2 * per * (i // per) + lax.rem(i, per)
    valid = i < head_count // 2
    first = jnp.where(valid & (j == spot), 1.0, 0.0)
    second = jnp.where(valid & (j == spot + per), 1.0, 0.0)
    mine_to, other_to = jnp.where(zero, first, second), jnp.where(zero, second, first)

    for n in range(4):
        src = slice(n * wide, (n + 1) * wide)
        for base, a, b in ((0, e, eo), (2 * inner, l, lo)):
            mine, other = a[:, src].astype(F32).T, b[:, src].astype(F32).T
            low = base + 2 * n * wide
            in_o[low : low + wide, :] = jnp.where(zero, mine, other)
            in_o[low + wide : low + 2 * wide, :] = jnp.where(zero, other, mine)
    at = slice(inner, inner + bc)
    in_o[4 * inner : 4 * inner + bc, :] = (l[:, at].astype(F32) + lo[:, at].astype(F32)).T
    at = slice(inner + bc, inner + bc + LANE)
    heads = mm(l[:, at], mine_to) + mm(lo[:, at], other_to)
    in_o[4 * inner + bc : 4 * inner + bc + head_count, :] = heads.T[0:head_count, :]
    mine, other = w[...].astype(F32), wo[...].astype(F32)
    out_o[0] = jnp.where(zero, mine, other)
    out_o[1] = jnp.where(zero, other, mine)

    top, low = inner // LANE, bc // LANE
    wide = wide // LANE

    def halves(target, row, source):
        for n in range(top):
            mine, other = v[source + n : source + n + 1, :], vo[source + n : source + n + 1, :]
            to = ((n // wide) * 2 * wide + n % wide) * LANE
            target[row : row + 1, to : to + LANE] = jnp.where(zero, mine, other)
            to += wide * LANE
            target[row : row + 1, to : to + LANE] = jnp.where(zero, other, mine)

    for k in range(taps + 1):
        target, row = (conv_o, k) if k < taps else (bias_o, 0)
        halves(target, row, k * top)
        for n in range(low):
            at = (taps + 1) * top + k * low + n
            to = 2 * inner + n * LANE
            target[row : row + 1, to : to + LANE] = v[at : at + 1, :] + vo[at : at + 1, :]
    at = (taps + 1) * (top + low)

    def exact(a, b):
        return jnp.dot(a, b, precision=HI, preferred_element_type=F32)

    heads_o[...] = exact(v[at : at + 8, :], mine_to) + exact(vo[at : at + 8, :], other_to)
    halves(og_o, 0, at + 3)
    gain_o[...] = v[at + 3 + top : at + 3 + 2 * top, :]


def assemble(core, mine, other, proj, head_count, taps):
    flat = [a.reshape(-1, a.shape[-1]) for a in tuple(mine) + tuple(other)]
    rows, inner = flat[0].shape
    chan = 2 * inner + flat[2].shape[1] - inner - LANE
    place = pl.BlockSpec(memory_space=pltpu.VMEM)
    outs = [
        (proj, rows), (2, rows, inner), (8, LANE), (taps, chan), (1, chan), (8, LANE),
        (1, 2 * inner),
    ]
    return pl.pallas_call(
        functools.partial(assemble_kernel, head_count, taps),
        in_specs=[pl.BlockSpec(memory_space=pltpu.SMEM)] + [place] * 8,
        out_specs=[place] * len(outs),
        out_shape=[sds(shape, F32) for shape in outs],
        compiler_params=pltpu.CompilerParams(vmem_limit_bytes=40 * 2**20),
    )(core.astype(jnp.int32).reshape(1), *flat)


def pack_kernel(head_count, w, o, *refs):
    by_layer, sent, send, recv = (refs[0:3], refs[3:6]), refs[6:9], refs[9], refs[10]
    core = lax.axis_index("section")
    twin = {"section": 1 - core}
    wide = o.shape[0] // 2
    inner = 4 * wide
    bc_at = 4 * inner
    dt_at = w.shape[0] - head_count
    greet([twin])
    per = head_count // 8
    i = lax.broadcasted_iota(jnp.int32, (head_count, LANE), 0)
    j = lax.broadcasted_iota(jnp.int32, (head_count, LANE), 1)

    def pack_x(which, target):
        for n in range(4):
            at = pl.multiple_of(2 * inner + 2 * n * wide + which * wide, wide)
            target[:, n * wide : (n + 1) * wide] = w[pl.ds(at, wide), :].T
        target[:, inner : inner + dt_at - bc_at] = w[bc_at:dt_at, :].T
        pick = (i == 2 * per * (j // per) + per * which + lax.rem(j, per)) & (j < 4 * per)
        heads = mm_tn(w[dt_at:, :], jnp.where(pick, 1.0, 0.0))
        target[:, inner + dt_at - bc_at :] = heads.astype(BF16)

    def pack_z(which, target):
        for n in range(4):
            at = pl.multiple_of(2 * n * wide + which * wide, wide)
            target[:, n * wide : (n + 1) * wide] = w[pl.ds(at, wide), :].T

    def pack_o(which, target):
        target[...] = o[pl.ds(pl.multiple_of(which * wide, wide), wide), :]

    packs = (pack_x, pack_z, pack_o)

    def work(layer):
        copies = []
        for n in range(3):
            packs[n](1 - layer, sent[n])
            copies.append(
                pltpu.make_async_remote_copy(
                    src_ref=sent[n],
                    dst_ref=by_layer[layer][n],
                    send_sem=send.at[n],
                    recv_sem=recv.at[n],
                    device_id=twin,
                    device_id_type=MESH,
                )
            )
            copies[n].start()
        for n in range(3):
            packs[n](layer, by_layer[layer][n])
        for copy in copies:
            copy.wait()

    @pl.when(core == 0)
    def _():
        work(0)

    @pl.when(core == 1)
    def _():
        work(1)


def pack_weights(w, o, head_count):
    wide, rows = o.shape[0] // 2, w.shape[1]
    shapes = [(rows, 4 * wide + 2 * LANE + LANE), (rows, 4 * wide), (wide, o.shape[1])]
    place = pl.BlockSpec(memory_space=pltpu.VMEM)
    out = pl.pallas_call(
        functools.partial(pack_kernel, head_count),
        out_shape=[sds(shape, BF16) for shape in shapes * 2],
        in_specs=[place] * 2,
        out_specs=[place] * 6,
        scratch_shapes=[pltpu.VMEM(shape, BF16) for shape in shapes]
        + [pltpu.SemaphoreType.DMA((3,))] * 2,
        compiler_params=pltpu.CompilerParams(
            collective_id=4, has_side_effects=True, vmem_limit_bytes=24 * 2**20
        ),
    )(w, o)
    return out[0:3], out[3:6]


def spread_kernel(x_own, z_own, o_own, x_all, z_all, o_all, send, recv, local):
    sender = Sender(send, recv)
    q = lax.axis_index("seq")
    x = lax.axis_index("wshard")
    z, y = q // 4, lax.rem(q, 4)
    shards = [lax.rem(x + d, 4) for d in (1, 2, 3)]
    z_up, z_down = lax.rem(z + 1, 4), lax.rem(z + 3, 4)
    y_up, y_down = lax.rem(y + 1, 4), lax.rem(y + 3, 4)
    to_z_up, to_z_down = {"seq": z_up * 4 + y}, {"seq": z_down * 4 + y}
    to_y_up, to_y_down = {"seq": z * 4 + y_up}, {"seq": z * 4 + y_down}
    greet([{"wshard": p} for p in shards] + [to_z_up, to_z_down, to_y_up, to_y_down])
    pairs = ((x_own, x_all), (z_own, z_all), (o_own, o_all))
    x_up, x_down = lax.rem(x + 1, 4), lax.rem(x + 3, 4)
    to_x_up, to_x_down = {"wshard": x_up}, {"wshard": x_down}
    sent = [
        sender.start(own.at[z, y], full.at[x, z, y], {"wshard": p})
        for p in shards
        for own, full in pairs[0:2]
    ]
    o_ways = [sender.start(o_own, o_all.at[x], device) for device in (to_x_up, to_x_down)]
    kept = [
        pltpu.make_async_copy(own, full.at[x], local.at[n]) for n, (own, full) in enumerate(pairs)
    ]
    for copy in kept:
        copy.start()
    for copy in sent:
        copy.wait()
    cut = 10 * LANE
    over_y = ((x_all, slice(0, cut)),)
    over_z = ((z_all, slice(0, z_all.shape[-1])), (x_all, slice(cut, x_all.shape[-1])))
    ups, downs = [], []

    def both_ways(refs, up, down):
        ups.append([sender.start(r, r, up) for r in refs])
        downs.append([sender.start(r, r, down) for r in refs])

    for p in shards:
        both_ways([a.at[p, z, y, :, c] for a, c in over_y], to_y_up, to_y_down)
        both_ways([a.at[p, z, y, :, c] for a, c in over_z], to_z_up, to_z_down)
    rest = []
    for n, p in enumerate(shards):
        for copy in ups[2 * n] + ups[2 * n + 1] + downs[2 * n] + downs[2 * n + 1]:
            copy.wait()
        if n != 1:
            refs = [a.at[p, z, y_down, :, c] for a, c in over_y[0:1]]
            rest += [sender.start(r, r, to_y_up) for r in refs]
            refs = [a.at[p, z_down, y, :, c] for a, c in over_z[: 2 if n == 0 else 1]]
            rest += [sender.start(r, r, to_z_up) for r in refs]
        if n != 0:
            refs = [a.at[p, z, y_up, :, c] for a, c in over_y[0 if n == 1 else 1 :]]
            rest += [sender.start(r, r, to_y_down) for r in refs]
            refs = [a.at[p, z_up, y, :, c] for a, c in over_z[0 if n == 1 else 1 :]]
            rest += [sender.start(r, r, to_z_down) for r in refs]
    for copy in o_ways:
        copy.wait()
    here, there = o_all.at[x_down, 0:2], o_all.at[x_up, 2:4]
    o_rest = [sender.start(here, here, to_x_up), sender.start(there, there, to_x_down)]
    for copy in rest:
        copy.wait()
    ups.clear()
    downs.clear()
    for p in shards:
        both_ways([a.at[p, z, :, :, c] for a, c in over_y], to_z_up, to_z_down)
        both_ways([a.at[p, :, y, :, c] for a, c in over_z], to_y_up, to_y_down)
    rest = []
    low, high = slice(0, 2), slice(2, 4)
    for n, p in enumerate(shards):
        for copy in ups[2 * n] + ups[2 * n + 1] + downs[2 * n] + downs[2 * n + 1]:
            copy.wait()
        for a, c in over_y:
            here, there = a.at[p, z_down, low, :, c], a.at[p, z_up, high, :, c]
            rest += [sender.start(here, here, to_z_up), sender.start(there, there, to_z_down)]
        for a, c in over_z:
            here, there = a.at[p, low, y_down, :, c], a.at[p, high, y_up, :, c]
            rest += [sender.start(here, here, to_y_up), sender.start(there, there, to_y_down)]
    for copy in rest + o_rest:
        copy.wait()
    for copy in kept:
        copy.wait()


def spread_weights(x_own, z_own, o_own):
    own = [a.reshape(4, 4, a.shape[0] // 16, a.shape[1]) for a in (x_own, z_own, o_own)]
    place = pl.BlockSpec(memory_space=pltpu.VMEM)
    count = 6 + 4 + 18 + 9 + 18 + 18
    full = pl.pallas_call(
        spread_kernel,
        out_shape=[sds((4,) + a.shape, BF16) for a in own],
        in_specs=[place] * 3,
        out_specs=[place] * 3,
        scratch_shapes=[
            pltpu.SemaphoreType.DMA((count,)),
            pltpu.SemaphoreType.DMA((count,)),
            pltpu.SemaphoreType.DMA((3,)),
        ],
        compiler_params=pltpu.CompilerParams(
            collective_id=3, has_side_effects=True, vmem_limit_bytes=24 * 2**20
        ),
    )(*own)
    return tuple(a.reshape(-1, a.shape[-1]) for a in full)


class Ring:
    def __init__(self, sender, src, index, me, up, down, buf):
        self.sender, self.src, self.index, self.buf = sender, src, index, buf
        self.me, (self.up, self.to_up), (self.down, self.to_down) = me, up, down

    def start(self):
        src, buf, index = self.src, self.buf, self.index
        far = lax.rem(self.me + 2, 4)
        begin = self.sender.start
        self.copies = [
            begin(src.at[index(far, 0)], buf.at[0], self.to_up),
            begin(src.at[index(far, 1)], buf.at[1], self.to_down),
            begin(src.at[index(self.up, 1)], buf.at[4], self.to_up),
            begin(src.at[index(self.down, 0)], buf.at[5], self.to_down),
        ]

    def middle(self):
        src, buf, index = self.src, self.buf, self.index
        for n, (p, device) in enumerate(((self.up, self.to_up), (self.down, self.to_down))):
            self.copies[n].wait()
            total = buf[n].astype(F32) + src[index(p, n)].astype(F32)
            buf[2 + n] = total.astype(buf.dtype)
            self.copies.append(self.sender.start(buf.at[2 + n], buf.at[6 + n], device))

    def finish(self):
        src, buf, index = self.src, self.buf, self.index
        for copy in self.copies[2:]:
            copy.wait()
        for n, other in ((0, 5), (1, 4)):
            total = src[index(self.me, n)].astype(F32) + buf[other].astype(F32)
            yield n, total + buf[6 + n].astype(F32)


def reduce_kernel(cut, z0, o0, b0, z1, o1, b1, small, *refs):
    g_own, g_other, refs = refs[0:4], refs[4:8], refs[8:]
    xr, xs, bx, ring_x, ring_a, total_a, far_a, sum_a, last_a = refs[0:9]
    rings, totals, far = refs[9:16], refs[16:23], refs[23:30]
    f, o = refs[30:34], refs[34:38]
    sender = Sender(refs[38], refs[39])
    core = lax.axis_index("section")
    q = lax.axis_index("seq")
    x = lax.axis_index("wshard")
    z, y = q // 4, lax.rem(q, 4)

    def on_x(d):
        return {"wshard": lax.rem(x + d, 4)}

    def on_y(d):
        return {"seq": z * 4 + lax.rem(y + d, 4)}

    def on_z(d):
        return {"seq": lax.rem(z + d, 4) * 4 + y}

    twin = {"section": 1 - core}
    greet([on(d) for on in (on_x, on_y, on_z) for d in (1, 2, 3)] + [twin])

    def near(me, on):
        return me, (lax.rem(me + 1, 4), on(1)), (lax.rem(me + 3, 4), on(3))

    halves = (slice(0, 2), slice(2, 4))
    everything = slice(None)
    over_x = Ring(sender, b0, lambda p, h: (p, halves[h]), *near(x, on_x), ring_x)
    over_x.start()
    small_x = [sender.start(small, xr.at[d - 1], on_x(d)) for d in (1, 2, 3)]

    low, high = slice(0, cut), slice(cut, b1.shape[-1])
    parts = [
        (z1, everything, 1, True, 0),
        (o1, everything, 1, False, 1),
        (b1, low, 1, True, 2),
        (b1, high, 1, False, 2),
        (xs.at[0], everything, 0, True, 3),
        (xs.at[1], everything, 1, False, 3),
        (bx, low, 0, True, 2),
        (bx, high, 0, False, 2),
    ]

    def ring_of(n):
        src, cols, _, y_first, _ = parts[n]
        if y_first:
            return Ring(
                sender, src, lambda p, h: (halves[h], p, everything, cols), *near(y, on_y), bufs(n)
            )
        return Ring(
            sender, src, lambda p, h: (p, halves[h], everything, cols), *near(z, on_z), bufs(n)
        )

    def bufs(n):
        return rings[n] if n < 6 else rings[6].at[:, :, :, parts[n][1]]

    def ending(n, ring):
        total = totals[n] if n < 6 else totals[6].at[:, :, parts[n][1]]
        for half, value in ring.finish():
            total[halves[half]] = value.astype(total.dtype)
        y_first = parts[n][3]
        there = far[n] if n < 6 else far[6].at[:, :, parts[n][1]]
        copies = []
        for d in (1, 2, 3):
            to, peer = (lax.rem(z + d, 4), on_z(d)) if y_first else (lax.rem(y + d, 4), on_y(d))
            copies.append(sender.start(total.at[to], there.at[d - 1], peer))
        return total, there, copies

    def closing(n, total, there, copies):
        _, cols, layer, y_first, kind = parts[n]
        for copy in copies:
            copy.wait()
        value = total[z if y_first else y].astype(F32)
        for d in range(3):
            value = value + there[d].astype(F32)
        f[kind][layer, :, cols] = value.astype(f[kind].dtype)

    wide = [
        Ring(sender, z0, lambda p, h: (halves[h], everything, p), *near(y, on_y), ring_a.at[0]),
        Ring(sender, o0, lambda p, h: (halves[h], p), *near(z, on_z), ring_a.at[1]),
    ]
    running = [ring_of(n) for n in range(8)]
    for ring in wide:
        ring.start()
    for n in range(4):
        running[n].start()
    for copy in small_x:
        copy.wait()
    xs[...] = small[...] + xr[0] + xr[1] + xr[2]
    running[4].start()
    running[5].start()
    for ring in wide:
        ring.middle()
    over_x.middle()
    for n in range(6):
        running[n].middle()
    wide_copies = []
    for side, ring in enumerate(wide):
        for half, value in ring.finish():
            total_a[side, halves[half]] = value.astype(BF16)
        for d in (1, 2, 3):
            to, peer = (lax.rem(y + d, 4), on_y(d)) if side else (lax.rem(z + d, 4), on_z(d))
            wide_copies.append(
                sender.start(total_a.at[side, :, to], far_a.at[side, d - 1], peer)
            )
    for half, value in over_x.finish():
        bx[halves[half]] = value.astype(bx.dtype)
    running[6].start()
    running[7].start()
    ended = [ending(n, running[n]) for n in range(6)]
    last_copies = []
    for side in (0, 1):
        for copy in wide_copies[3 * side : 3 * side + 3]:
            copy.wait()
        value = total_a[side, :, y if side else z].astype(F32)
        for d in range(3):
            value = value + far_a[side, d].astype(F32)
        sum_a[side] = value.astype(BF16)
        for d in (1, 2, 3):
            here = sum_a.at[side, lax.rem(x + d, 4)]
            last_copies.append(sender.start(here, last_a.at[side, d - 1], on_x(d)))
    running[6].middle()
    running[7].middle()
    for n in range(6):
        closing(n, *ended[n])
    ended += [ending(n, running[n]) for n in (6, 7)]
    for side in (0, 1):
        for copy in last_copies[3 * side : 3 * side + 3]:
            copy.wait()
        value = sum_a[side, x].astype(F32)
        for d in range(3):
            value = value + last_a[side, d].astype(F32)
        f[side][0] = value.astype(BF16)
    for n in (6, 7):
        closing(n, *ended[n])
    twins = [sender.start(f[n].at[1 - core], o[n], twin) for n in range(4)]
    gather = []
    for n in range(4):
        g_own[n][z, y] = f[n][core]
        for d in (1, 2, 3):
            gather.append(sender.start(f[n].at[core], g_own[n].at[z, y], on_y(d)))
    for copy in twins:
        copy.wait()
    for n in range(4):
        g_other[n][z, y] = o[n][...]
        for d in (1, 2, 3):
            gather.append(sender.start(o[n], g_other[n].at[z, y], on_z(d)))
    for copy in gather:
        copy.wait()
    _, (z_up, to_z_up), (z_down, to_z_down) = near(z, on_z)
    _, (y_up, to_y_up), (y_down, to_y_down) = near(y, on_y)
    gather = []
    for own, other in zip(g_own, g_other):
        for device in (to_z_up, to_z_down):
            gather.append(sender.start(own.at[z], own.at[z], device))
        for device in (to_y_up, to_y_down):
            gather.append(sender.start(other.at[:, y], other.at[:, y], device))
    last = []
    for n, (own, other) in enumerate(zip(g_own, g_other)):
        for copy in gather[4 * n : 4 * n + 4]:
            copy.wait()
        for half, z_to, y_to, z_from, y_from in (
            (halves[0], to_z_up, to_y_up, z_down, y_down),
            (halves[1], to_z_down, to_y_down, z_up, y_up),
        ):
            here = own.at[z_from, half]
            last.append(sender.start(here, here, z_to))
            here = other.at[half, y_from]
            last.append(sender.start(here, here, y_to))
    for copy in last:
        copy.wait()


def reduce_all(z0, o0, b0, z1, o1, b1, small):
    kinds = [(a.shape[2:], a.dtype) for a in (z1, o1, b1, small[0])]
    cut = 6 * LANE
    wide = b1.shape[-1]
    rows, mid = z1.shape[2:]
    thin = [((rows, c), BF16) for c in (cut, wide - cut)]
    full = [sds((4, 4) + shape, dtype) for shape, dtype in kinds]
    order = [kinds[0], kinds[1], thin[0], thin[1], kinds[3], kinds[3], kinds[2]]

    def vmem(shapes, *lead):
        return [pltpu.VMEM(lead + shape, dtype) for shape, dtype in shapes]

    count = 6 + 3 + 2 * 12 + 8 * 9 + 4 + 24 + 16 + 16
    scratch = [
        pltpu.VMEM((3,) + small.shape, F32),
        pltpu.VMEM(small.shape, F32),
        pltpu.VMEM(b1.shape, BF16),
        pltpu.VMEM((8, 2) + b1.shape[1:], BF16),
        pltpu.VMEM((2, 8, 2, 4, rows, mid), BF16),
        pltpu.VMEM((2, 4, 4, rows, mid), BF16),
        pltpu.VMEM((2, 3, 4, rows, mid), BF16),
        pltpu.VMEM((2, 4, rows, mid), BF16),
        pltpu.VMEM((2, 3, rows, mid), BF16),
        *vmem(order, 8, 2), *vmem(order, 4), *vmem(order, 3), *vmem(kinds, 2), *vmem(kinds),
        pltpu.SemaphoreType.DMA((count,)),
        pltpu.SemaphoreType.DMA((count,)),
    ]
    place = pl.BlockSpec(memory_space=pltpu.VMEM)
    out = pl.pallas_call(
        functools.partial(reduce_kernel, cut),
        out_shape=full + full,
        in_specs=[place] * 7,
        out_specs=[place] * 8,
        scratch_shapes=scratch,
        compiler_params=pltpu.CompilerParams(
            collective_id=0, has_side_effects=True, vmem_limit_bytes=48 * 2**20
        ),
    )(z0, o0, b0, z1, o1, b1, small)
    return out[0:4], out[4:8]


def forward(u, w, p):
    w_x, w_z, w_out = w
    gain_in, cw, cb, hp, gain_out = p
    seqs, rows, width = u.shape
    chan = cw.shape[1]
    taps = 4
    inner = gain_out.shape[1]
    states = LANE
    uf = u.astype(F32)
    inv = lax.rsqrt(jnp.mean(uf * uf, axis=-1, keepdims=True) + EPS)
    normed = (uf * inv * gain_in).astype(BF16).reshape(seqs * rows, width)
    xd = jnp.dot(normed, w_x, preferred_element_type=F32).astype(BF16)
    xd = xd.reshape(seqs, rows, chan + LANE)
    z = jnp.dot(normed, w_z, preferred_element_type=F32).reshape(seqs, rows, inner)
    halo = shift(xd[:, rows - TAIL :, :chan], "seq", 1)
    act, cum, step, sloc = run(
        functools.partial(chunk_kernel, taps),
        (xd, halo, cw, cb, hp),
        (
            sds((seqs, rows, chan), F32),
            sds((seqs, rows, LANE), F32),
            sds((seqs, rows, LANE), F32),
            sds((seqs * inner // LANE, states + TAIL, LANE), BF16),
        ),
        [pltpu.VMEM((TAIL + rows, chan), F32)],
        (2, 3, 4),
    )
    decay, yi, sin = scan_chunks(
        sloc, None, False, states, (act, cum, step), [sds((seqs, rows, inner), F32)]
    )
    yy, gg, ss = run(
        finish_kernel,
        (act, cum, yi, sin, z, hp, gain_out),
        (
            sds((seqs, rows, inner), F32),
            sds((seqs, rows, inner), BF16),
            sds((seqs, rows, 1), F32),
        ),
        (),
        (5, 6),
    )
    mine = jnp.dot(gg.reshape(seqs * rows, inner), w_out, preferred_element_type=F32)
    mine = mine.astype(BF16).reshape(seqs, rows, width)
    theirs, ss_theirs = swap(mine), swap(ss)
    branch = mine.astype(F32) + theirs.astype(F32)
    rn = lax.rsqrt((ss + ss_theirs) * (1.0 / (2 * inner)) + EPS)
    result = (uf + rn * branch).astype(BF16)
    kept = (u, inv, normed, z, xd, halo, act, cum, step, decay, sin, yy, branch, rn)
    return result, kept


def backward(e, kept, w, p, over_wshard):
    w_x, w_z, w_out = w
    gain_in, cw, cb, hp, gain_out = p
    u, inv, normed, z, xd, halo, act, cum, step, decay, sin, yy, branch, rn = kept
    seqs, rows, width = e.shape
    chan = cw.shape[1]
    taps = 4
    inner = gain_out.shape[1]
    states = LANE
    ef = e.astype(F32)
    e2 = e.reshape(seqs * rows, width)
    nt = (((1,), (1,)), ((), ()))
    tn = (((0,), (0,)), ((), ()))
    gr = lax.dot_general(e2, w_out, nt, preferred_element_type=F32).reshape(seqs, rows, inner)
    rs = jnp.sum(ef * branch, axis=-1, keepdims=True)
    dy, gz, dsl, dgain, gated = run(
        gate_back_kernel,
        (gr, z, yy, act, cum, rn, rs, hp, gain_out),
        (
            sds((seqs, rows, inner), BF16),
            sds((seqs, rows, inner), BF16),
            sds((seqs * inner // LANE, states, LANE), BF16),
            sds((seqs, inner // LANE, LANE), F32),
            sds((seqs, rows, inner), BF16),
        ),
        (),
        (7, 8),
    )
    gz = gz.reshape(seqs * rows, inner)
    part_z = lax.dot_general(gz, w_z, nt, preferred_element_type=F32)
    early_z = lax.dot_general(normed, gz, tn, preferred_element_type=F32).astype(BF16)
    early_o = lax.dot_general(
        gated.reshape(seqs * rows, inner), e2, tn, preferred_element_type=F32
    ).astype(BF16)
    if over_wshard:
        early_z, early_o = (
            lax.psum_scatter(a, "wshard", scatter_dimension=0, tiled=True)
            for a in (early_z, early_o)
        )
    dxs, dbc, dci, grad = scan_chunks(
        dsl,
        decay,
        True,
        states,
        (act, cum, step, dy),
        [
            sds((seqs, rows, inner), F32),
            sds((seqs, rows, 2 * LANE), F32),
            sds((seqs, rows, LANE), F32),
        ],
    )
    dpre, ddt, small = run(
        functools.partial(mix_back_kernel, taps),
        (xd, halo, cw, cb, hp, act, cum, step, dy, dxs, dbc, dci, grad, sin),
        (
            sds((seqs, rows, chan), F32),
            sds((seqs, rows, LANE), BF16),
            sds((seqs, 56, LANE), F32),
        ),
        [pltpu.VMEM((TAIL + rows, chan), F32), pltpu.VMEM((rows, chan), F32)],
        (2, 3, 4),
    )
    after = shift(dpre[:, :8], "seq", -1)
    (gp,) = run(
        functools.partial(conv_back_kernel, taps),
        (dpre, after, ddt, cw),
        (sds((seqs, rows, chan + LANE), BF16),),
        [pltpu.VMEM((rows + 8, chan), F32)],
        (3,),
    )
    gp = gp.reshape(seqs * rows, -1)
    mine = part_z + lax.dot_general(gp, w_x, nt, preferred_element_type=F32)
    mine = mine.astype(BF16).reshape(seqs, rows, width)
    theirs = swap(mine)
    gn = mine.astype(F32) + theirs.astype(F32)
    uf = u.astype(F32)
    unit = uf * inv
    g_gain_in = jnp.sum(gn * unit, axis=(0, 1))
    scaled = gn * gain_in
    dot = jnp.mean(scaled * unit, axis=-1, keepdims=True)
    grad_u = ef + inv * (scaled - unit * dot)
    late = lax.dot_general(normed, gp, tn, preferred_element_type=F32).astype(BF16)
    if over_wshard:
        late = lax.psum_scatter(late, "wshard", scatter_dimension=0, tiled=True)
    rows_of = [small.sum(0)[: small.shape[1] - 3], dgain.sum(0), g_gain_in.reshape(-1, LANE)]
    used = sum(a.shape[0] for a in rows_of)
    smalls = jnp.concatenate(rows_of + [jnp.zeros((16 * 8 - used, LANE), F32)], axis=0)
    return grad_u, (early_z, early_o, late), smalls.reshape(4, 4, 8, LANE)


def body(
    hidden, out_grad, norm_gain, in_weight, conv_weight, conv_bias, dt_bias, a_log, d_skip,
    out_gain, out_weight,
):
    core = lax.axis_index("section")
    width = hidden.shape[2]
    full = out_gain.shape[1]
    taps = conv_weight.shape[1]
    head_count = dt_bias.shape[1]
    proj = in_weight.shape[2]

    shards = pack_weights(in_weight[0].T, out_weight[0], head_count)
    sizes = (norm_gain, conv_weight, conv_bias, dt_bias, a_log, d_skip, out_gain)
    flat = jnp.concatenate([a[0].reshape(-1) for a in sizes])
    flat_other = swap(flat)

    def params(layer):
        mine = core == layer
        w = shards[layer]
        if layer == 0:
            w = spread_weights(*w)
        else:
            w = tuple(lax.all_gather(a, "wshard", axis=0, tiled=True) for a in w)
        v = jnp.where(mine, flat, flat_other)
        parts, at = [], 0
        for a in sizes:
            count = a[0].size
            parts.append(v[at : at + count].reshape(a[0].shape))
            at += count
        gain_in, cw, cb, dtb, al, ds, gain_out = parts

        def channels(a):
            return jnp.concatenate([half(a[..., :full], core), a[..., full:]], axis=-1)

        hp = jnp.stack([half(a, core) for a in (dtb, al, ds)])
        hp = jnp.pad(hp, ((0, 5), (0, LANE - hp.shape[1])))
        cw = jnp.pad(channels(cw), ((0, 8 - taps), (0, 0)))
        return w, (
            gain_in[None],
            cw,
            channels(cb)[None],
            hp,
            half(gain_out, core)[None],
        )

    w0, p0 = params(0)
    w1, p1 = params(1)
    first, kept0 = forward(hidden, w0, p0)
    second, kept1 = forward(first, w1, p1)
    layer_out = jnp.where(core == 0, first, second)[None]
    grad1, products1, smalls1 = backward(out_grad, kept1, w1, p1, True)
    passed = grad1.astype(BF16)
    grad0, products0, smalls0 = backward(passed, kept0, w0, p0, False)
    section_grad = jnp.where(core == 0, grad0, passed.astype(F32))[None]

    rows = width // 64
    first = [a.reshape(4, 4, 4, rows, a.shape[1]) for a in products0]
    second = [a.reshape(4, 4, rows, a.shape[1]) for a in products1]
    mine, other = reduce_all(*first, *second, jnp.stack([smalls0, smalls1]))
    grad_in, grad_out, gains, conv_g, bias_g, heads_g, out_gains = assemble(
        core, mine, other, proj, head_count, taps
    )
    return (
        layer_out,
        section_grad,
        gains.reshape(1, width),
        grad_in.T[None],
        conv_g[None],
        bias_g,
        heads_g[0:1, :head_count],
        heads_g[1:2, :head_count],
        heads_g[2:3, :head_count],
        out_gains,
        grad_out.reshape(1, -1, width),
    )


def solution(mesh):
    by_layer = P("section", None)
    weights = P("section", "wshard", None)
    tokens = P("wshard", "seq", None)
    stacked = P("section", "wshard", "seq", None)
    conv = P("section", None, None)
    in_specs = (
        tokens, tokens, by_layer, weights, conv, by_layer, by_layer, by_layer, by_layer, by_layer,
        weights,
    )
    out_specs = (
        stacked, stacked, by_layer, weights, conv, by_layer, by_layer, by_layer, by_layer,
        by_layer, weights,
    )
    return jax.shard_map(body, mesh=mesh, in_specs=in_specs, out_specs=out_specs, check_vma=False)
```

```python
import functools

import jax
import jax.numpy as jnp
from jax import lax
from jax.experimental import pallas as pl
from jax.experimental.pallas import tpu as pltpu
from jax.sharding import PartitionSpec as P

F32 = jnp.float32
BF16 = jnp.bfloat16
HI = lax.Precision.HIGHEST
EPS = 1e-05
HDIM = 64
LANE = 128
TAIL = 16


def shift(x, axis, by):
    devices = lax.axis_size(axis)
    pairs = [(i, i + by) for i in range(devices) if 0 <= i + by < devices]
    return lax.ppermute(x, axis, pairs)


def swap(x):
    return lax.ppermute(x, "section", [(0, 1), (1, 0)])


def half(a, which):
    width = a.shape[-1] // 8
    b = a.reshape(a.shape[:-1] + (4, 2, width))
    b = lax.dynamic_index_in_dim(b, which, axis=b.ndim - 2, keepdims=False)
    return b.reshape(a.shape[:-1] + (4 * width,))


def whole(own, other, core):
    width = own.shape[-1] // 4
    lead = own.shape[:-1]
    own, other = own.reshape(lead + (4, 1, width)), other.reshape(lead + (4, 1, width))
    first, second = jnp.where(core == 0, own, other), jnp.where(core == 0, other, own)
    return jnp.concatenate([first, second], axis=-2).reshape(lead + (8 * width,))


def mm(a, b):
    return jnp.dot(a.astype(BF16), b.astype(BF16), preferred_element_type=F32)


def mm_nt(a, b):
    return lax.dot_general(
        a.astype(BF16), b.astype(BF16), (((1,), (1,)), ((), ())), preferred_element_type=F32
    )


def mm_tn(a, b):
    return lax.dot_general(
        a.astype(BF16), b.astype(BF16), (((0,), (0,)), ((), ())), preferred_element_type=F32
    )


def spread_matrix(width):
    head = lax.broadcasted_iota(jnp.int32, (LANE, width), 0)
    lane = lax.broadcasted_iota(jnp.int32, (LANE, width), 1)
    return jnp.where(lane // HDIM == head, 1.0, 0.0).astype(BF16)


def split(v):
    high = v.astype(BF16)
    return high, (v - high.astype(F32)).astype(BF16)


def spread(heads, matrix):
    high, rest = split(heads)
    return mm(high, matrix) + mm(rest, matrix)


def gather_heads(lanes, matrix):
    high, rest = split(lanes)
    return mm_nt(high, matrix) + mm_nt(rest, matrix)


def tri(rows, upper):
    r = lax.broadcasted_iota(jnp.int32, (rows, rows), 0)
    c = lax.broadcasted_iota(jnp.int32, (rows, rows), 1)
    return jnp.where((c >= r) if upper else (r >= c), 1.0, 0.0).astype(F32)


def steps(dt, hp):
    shifted = dt + hp[0:1, :]
    step = jnp.maximum(shifted, 0.0) + jnp.log1p(jnp.exp(-jnp.abs(shifted)))
    rate = -jnp.exp(hp[1:2, :])
    return shifted, step, rate


def sigmoid(v):
    return 1.0 / (1.0 + jnp.exp(-v))


def conv_pre(buf, cw, cb, taps, rows):
    pre = cb[0:1, :]
    for k in range(taps):
        start = TAIL - (taps - 1) + k
        pre = pre + cw[k : k + 1, :] * buf[start : start + rows, :]
    return pre


MESH = pl.DeviceIdType.MESH


class Sender:
    def __init__(self, send, recv):
        self.send, self.recv, self.used = send, recv, 0

    def start(self, src, dst, device):
        n = self.used
        self.used += 1
        copy = pltpu.make_async_remote_copy(
            src_ref=src,
            dst_ref=dst,
            send_sem=self.send.at[n],
            recv_sem=self.recv.at[n],
            device_id=device,
            device_id_type=MESH,
        )
        copy.start()
        return copy


def greet(devices):
    barrier = pltpu.get_barrier_semaphore()
    for device in devices:
        pl.semaphore_signal(barrier, inc=1, device_id=device, device_id_type=MESH)
    pl.semaphore_wait(barrier, len(devices))


def chunk_kernel(taps, xd, halo, cw, cb, hp, act_o, cum_o, step_o, sloc_o, buf):
    rows, inner, chan = xd.shape[1], sloc_o.shape[0] * LANE, cw.shape[1]
    buf[0:TAIL, :] = halo[0].astype(F32)
    buf[TAIL : TAIL + rows, :] = xd[0, :, 0:chan].astype(F32)
    pre = conv_pre(buf, cw, cb, taps, rows)
    act = pre * sigmoid(pre)
    act_o[0] = act
    _, step, rate = steps(xd[0, :, chan : chan + LANE].astype(F32), hp)
    cum = jnp.dot(tri(rows, False), step * rate, precision=HI, preferred_element_type=F32)
    cum_o[0] = cum
    step_o[0] = step
    last = cum[rows - 1 : rows, :]
    matrix = spread_matrix(inner)
    weight = spread(jnp.exp(last - cum) * step, matrix)
    decay = spread(jnp.broadcast_to(jnp.exp(last), (8, LANE)), matrix)[0:1, :]
    d_hi = decay.astype(BF16).astype(F32)
    d_mid = (decay - d_hi).astype(BF16).astype(F32)
    d_lo = decay - d_hi - d_mid
    row = lax.broadcasted_iota(jnp.int32, (TAIL, inner), 0)
    extra = jnp.where(row == 0, d_hi, jnp.where(row == 1, d_mid, jnp.where(row == 2, d_lo, 0.0)))
    extra = extra.astype(BF16)
    xw = (act[:, :inner] * weight).astype(BF16)
    b = act[:, inner : inner + LANE].astype(BF16)
    sloc = mm_tn(b, xw).astype(BF16)
    states = sloc.shape[0]
    for i in range(inner // LANE):
        sloc_o[i, 0:states, :] = sloc[:, i * LANE : (i + 1) * LANE]
        sloc_o[i, states : states + TAIL, :] = extra[:, i * LANE : (i + 1) * LANE]


def one(ref, s):
    count = ref.shape[0] // 2
    return ref.at[pl.ds(s * count, count)]


def scan_kernel(reverse, with_decay, pieces_ref, *refs):
    got, done, send_a, recv_a, send_b, recv_b = refs[-6:]
    if with_decay:
        decay, out = refs[3], refs[5]
        inside, ins, outs = intra_kernel, refs[0:3], refs[4:5]
    else:
        decay, out = refs[0], refs[9]
        inside, ins, outs = intra_back_kernel, refs[1:6], refs[6:9]
    count, states = out.shape[0], out.shape[1]
    q = lax.axis_index("seq")
    peers = [lax.rem(q + d, count) for d in range(1, count)]
    greet([{"seq": p} for p in peers])

    def copy(src, dst, send, recv, n, peer, slot):
        return pltpu.make_async_remote_copy(
            src_ref=src.at[peer],
            dst_ref=dst.at[slot],
            send_sem=send.at[n],
            recv_sem=recv.at[slot],
            device_id={"seq": peer},
            device_id_type=MESH,
        )

    sent = [copy(pieces_ref, got, send_a, recv_a, n, p, q) for n, p in enumerate(peers)]
    for c in sent:
        c.start()
    got[q] = pieces_ref[q]
    for s in range(2):
        inside(*[one(a, s) for a in ins + outs])
    for n, p in enumerate(peers):
        copy(pieces_ref, got, send_a, recv_a, n, p, p).wait_recv()
    carry = jnp.zeros((states, LANE), F32)
    order = range(count - 1, -1, -1) if reverse else range(count)
    for j in order:
        if with_decay:
            tail = got[j, states : states + TAIL, :].astype(F32)
            decay[j : j + 1, :] = tail[0:1, :] + tail[1:2, :] + tail[2:3, :]
        done[j] = carry.astype(BF16)
        carry = carry * decay[j : j + 1, :] + got[j, 0:states, :].astype(F32)
    back = [copy(done, out, send_b, recv_b, n, p, q) for n, p in enumerate(peers)]
    for c in back:
        c.start()
    out[q] = done[q]
    for n, p in enumerate(peers):
        copy(done, out, send_b, recv_b, n, p, p).wait_recv()
    for c in sent + back:
        c.wait_send()


def intra_kernel(act, cum, step, yi_o):
    rows, inner = yi_o.shape[1], yi_o.shape[2]
    b = act[0, :, inner : inner + LANE]
    c = act[0, :, inner + LANE : inner + 2 * LANE]
    cb = mm_nt(c, b)
    cum_v = cum[0]
    cum_t = jnp.transpose(cum_v)
    xs = act[0, :, :inner] * spread(step[0], spread_matrix(inner))
    keep = tri(rows, False) > 0
    low = lax.broadcasted_iota(jnp.int32, (rows, LANE), 1) < HDIM
    for i in range(inner // LANE):
        xs_i = xs[:, i * LANE : (i + 1) * LANE].astype(BF16)
        parts = []
        for h in (2 * i, 2 * i + 1):
            diff = cum_v[:, h : h + 1] - cum_t[h : h + 1, :]
            decay = jnp.exp(jnp.where(keep, diff, -1e30))
            parts.append(mm(cb * decay, xs_i))
        yi_o[0, :, i * LANE : (i + 1) * LANE] = jnp.where(low, parts[0], parts[1])


def finish_kernel(act, cum, yi, sin, z, hp, gain, yy_o, gg_o, ss_o):
    inner = yi.shape[2]
    matrix = spread_matrix(inner)
    grown = spread(jnp.exp(cum[0]), matrix)
    skip = spread(jnp.broadcast_to(hp[2:3, :], (8, LANE)), matrix)[0:1, :]
    c = act[0, :, inner + LANE : inner + 2 * LANE].astype(BF16)
    total = jnp.zeros((yi.shape[1], LANE), F32)
    for i in range(inner // LANE):
        at = slice(i * LANE, (i + 1) * LANE)
        yy = yi[0, :, at] + grown[:, at] * mm(c, sin[i])
        yy_o[0, :, at] = yy
        mixed = (yy + skip[:, at] * act[0, :, at]).astype(BF16).astype(F32)
        zi = z[0, :, at]
        g = mixed * (zi * sigmoid(zi))
        total = total + g * g
        gg_o[0, :, at] = (g * gain[0:1, at]).astype(BF16)
    ss_o[0] = jnp.sum(total, axis=1, keepdims=True)


def gate_back_kernel(
    gr, z, yy, act, cum, rn, rs, hp, gain, dy_o, gz_o, dsl_o, dgain_o, gated_o
):
    inner = gr.shape[2]
    matrix = spread_matrix(inner)
    grown = spread(jnp.exp(cum[0]), matrix)
    skip = spread(jnp.broadcast_to(hp[2:3, :], (8, LANE)), matrix)[0:1, :]
    c = act[0, :, inner + LANE : inner + 2 * LANE].astype(BF16)
    r = rn[0]
    k = r * r * r * rs[0] * (1.0 / (2 * inner))
    for i in range(inner // LANE):
        at = slice(i * LANE, (i + 1) * LANE)
        mixed = (yy[0, :, at] + skip[:, at] * act[0, :, at]).astype(BF16).astype(F32)
        zi = z[0, :, at]
        sg = sigmoid(zi)
        silu = zi * sg
        g = mixed * silu
        gr_i = gr[0, :, at]
        gain_i = gain[0:1, at]
        normal = g * r
        dgain_o[0, i : i + 1, :] = jnp.sum(gr_i * normal, axis=0, keepdims=True)
        gated_o[0, :, at] = (normal * gain_i).astype(BF16)
        dg = r * (gain_i * gr_i) - g * k
        dy = (dg * silu).astype(BF16)
        dy_o[0, :, at] = dy
        gz_o[0, :, at] = (dg * mixed * (sg * (1.0 + zi * (1.0 - sg)))).astype(BF16)
        dsl_o[i] = mm_tn(c, dy.astype(F32) * grown[:, at]).astype(BF16)


def intra_back_kernel(act, cum, step, dy, sin, dxs_o, dbc_o, dcum_o):
    rows, inner = dxs_o.shape[1], dxs_o.shape[2]
    b = act[0, :, inner : inner + LANE].astype(BF16)
    c = act[0, :, inner + LANE : inner + 2 * LANE].astype(BF16)
    cb = mm_nt(c, b)
    cum_v = cum[0]
    cum_t = jnp.transpose(cum_v)
    matrix = spread_matrix(inner)
    xs = act[0, :, :inner] * spread(step[0], matrix)
    grown = spread(jnp.exp(cum_v), matrix)
    carried = jnp.zeros((rows, LANE), F32)
    dc = jnp.zeros((rows, LANE), F32)
    keep = tri(rows, False) > 0
    low = lax.broadcasted_iota(jnp.int32, (rows, LANE), 1) < HDIM
    dcb = jnp.zeros((rows, rows), F32)
    lane = lax.broadcasted_iota(jnp.int32, (rows, LANE), 1)
    row_sums = jnp.zeros((rows, LANE), F32)
    col_sums = []
    for i in range(inner // LANE):
        at = slice(i * LANE, (i + 1) * LANE)
        xs_i = xs[:, at]
        dy_i = dy[0, :, at].astype(F32)
        parts = []
        for n, h in enumerate((2 * i, 2 * i + 1)):
            diff = cum_v[:, h : h + 1] - cum_t[h : h + 1, :]
            decay = jnp.exp(jnp.where(keep, diff, -1e30))
            mine = jnp.where(low, dy_i, 0.0) if n == 0 else jnp.where(low, 0.0, dy_i)
            flow = mm_nt(mine, xs_i) * decay
            dcb = dcb + flow
            both = flow * cb
            row_sums = jnp.where(lane == h, jnp.sum(both, axis=1, keepdims=True), row_sums)
            col_sums.append(jnp.sum(both, axis=0, keepdims=True))
            parts.append(mm_tn(cb * decay, dy_i))
        dxs_o[0, :, at] = jnp.where(low, parts[0], parts[1])
        dy_grown, s_i = dy_i * grown[:, at], sin[i]
        carried = carried + gather_heads(dy_grown * mm(c, s_i), matrix[:, at])
        dc = dc + mm_nt(dy_grown, s_i)
    col_sums.append(jnp.zeros((LANE - len(col_sums), rows), F32))
    dcum_o[0] = carried + row_sums - jnp.transpose(jnp.concatenate(col_sums, axis=0))
    dbc_o[0, :, 0:LANE] = mm_tn(dcb, c)
    dbc_o[0, :, LANE : 2 * LANE] = dc + mm(dcb, b)


def mix_back_kernel(
    taps, xd, halo, cw, cb, hp, act, cum, step, dy, dxs, dbc, dci, grad, sin,
    dpre_o, ddt_o, small_o, buf, dact,
):
    rows, inner, chan = dy.shape[1], dy.shape[2], cw.shape[1]
    matrix = spread_matrix(inner)
    cum_v, step_v = cum[0], step[0]
    last = cum_v[rows - 1 : rows, :]
    step_e = spread(step_v, matrix)
    tail_e = spread(jnp.exp(last - cum_v), matrix)
    d_e = spread(jnp.broadcast_to(jnp.exp(last), (8, LANE)), matrix)[0:1, :]
    skip = spread(jnp.broadcast_to(hp[2:3, :], (8, LANE)), matrix)[0:1, :]
    b = act[0, :, inner : inner + LANE].astype(BF16)
    q1 = dci[0]
    qb = jnp.zeros((rows, LANE), F32)
    q2 = jnp.zeros((rows, LANE), F32)
    flows = jnp.zeros((8, LANE), F32)
    skips = jnp.zeros((8, LANE), F32)
    db, dc = dbc[0, :, 0:LANE], dbc[0, :, LANE : 2 * LANE]
    for i in range(inner // LANE):
        at = slice(i * LANE, (i + 1) * LANE)
        g = grad[i]
        x = act[0, :, at]
        dy_i = dy[0, :, at].astype(F32)
        s_i = sin[i]
        back = tail_e[:, at] * mm(b, g)
        v = dxs[0, :, at] + back
        dact[:, at] = step_e[:, at] * v + skip[:, at] * dy_i
        part = matrix[:, at]
        q2 = q2 + gather_heads(x * v, part)
        qb = qb + gather_heads(x * back, part)
        flow = d_e[:, at] * jnp.sum(g.astype(F32) * s_i.astype(F32), axis=0, keepdims=True)
        flows = flows + gather_heads(jnp.broadcast_to(flow, (8, LANE)), part)
        skip_i = jnp.sum(dy_i * x, axis=0, keepdims=True)
        skips = skips + gather_heads(jnp.broadcast_to(skip_i, (8, LANE)), part)
        db = db + mm_nt(tail_e[:, at] * step_e[:, at] * x, g)
    dact[:, inner : inner + LANE] = db
    dact[:, inner + LANE : inner + 2 * LANE] = dc
    shifted, _, rate = steps(xd[0, :, chan : chan + LANE].astype(F32), hp)
    later = jnp.dot(tri(rows, True), q1, precision=HI, preferred_element_type=F32)
    strict = 1.0 - tri(rows, True)
    sooner = jnp.dot(strict, step_v * qb, precision=HI, preferred_element_type=F32)
    da = later + sooner + flows[0:1, :]
    ddt = (q2 + rate * da) * sigmoid(shifted)
    ddt_o[0] = ddt.astype(BF16)
    small_o[0] = jnp.zeros(small_o.shape[1:], F32)
    top, low = inner // LANE, 2
    at = (taps + 1) * (top + low)
    small_o[0, at : at + 1, :] = jnp.sum(ddt, axis=0, keepdims=True)
    small_o[0, at + 1 : at + 2, :] = jnp.sum(da * step_v, axis=0, keepdims=True) * rate
    small_o[0, at + 2 : at + 3, :] = skips[0:1, :]
    buf[0:TAIL, :] = halo[0].astype(F32)
    buf[TAIL : TAIL + rows, :] = xd[0, :, 0:chan].astype(F32)
    pre = conv_pre(buf, cw, cb, taps, rows)
    sg = sigmoid(pre)
    dpre = dact[...] * (sg * (1.0 + pre * (1.0 - sg)))
    dpre_o[0] = dpre
    for k in range(taps + 1):
        start = TAIL - (taps - 1) + k
        terms = dpre if k == taps else dpre * buf[start : start + rows, :]
        total = jnp.sum(terms, axis=0, keepdims=True)
        for i in range(top + low):
            to = k * top + i if i < top else (taps + 1) * top + k * low + i - top
            small_o[0, to : to + 1, :] = total[:, i * LANE : (i + 1) * LANE]


def conv_back_kernel(taps, dpre, after, ddt, cw, out, buf):
    rows, chan = dpre.shape[1], dpre.shape[2]
    buf[0:rows, :] = dpre[0]
    buf[rows : rows + 8, :] = after[0]
    total = cw[taps - 1 : taps, :] * buf[0:rows, :]
    for k in range(taps - 1):
        start = taps - 1 - k
        total = total + cw[k : k + 1, :] * buf[start : start + rows, :]
    out[0, :, 0:chan] = total.astype(BF16)
    out[0, :, chan : chan + LANE] = ddt[0]


def per_seq(shape):
    block = (shape[0] // 2,) + shape[1:]
    return pl.BlockSpec(block, lambda s: (s,) + (0,) * (len(shape) - 1))


def same(shape):
    return pl.BlockSpec(shape, lambda s: (0,) * len(shape))


def run(kernel, ins, outs, scratch=(), shared=()):
    return pl.pallas_call(
        kernel,
        grid=(2,),
        in_specs=[(same if n in shared else per_seq)(a.shape) for n, a in enumerate(ins)],
        out_specs=[per_seq(o.shape) for o in outs],
        out_shape=list(outs),
        scratch_shapes=list(scratch),
        compiler_params=pltpu.CompilerParams(vmem_limit_bytes=20 * 2**20),
    )(*ins)


def sds(shape, dtype):
    return jax.ShapeDtypeStruct(shape, dtype)


def scan_chunks(pieces, decay, reverse, states, inside, results):
    count, height = pieces.shape[0], pieces.shape[1]
    place = pl.BlockSpec(memory_space=pltpu.VMEM)
    outs = [*results, sds((count, states, LANE), BF16)]
    if decay is None:
        outs = [sds((count, LANE), F32)] + outs
    ins = (pieces,) + (() if decay is None else (decay,)) + inside
    sems = [pltpu.SemaphoreType.DMA((count,))] * 4
    return pl.pallas_call(
        functools.partial(scan_kernel, reverse, decay is None),
        out_shape=outs,
        in_specs=[place] * len(ins),
        out_specs=[place] * len(outs),
        scratch_shapes=[
            pltpu.VMEM((count, height, LANE), BF16),
            pltpu.VMEM((count, states, LANE), BF16),
            *sems,
        ],
        compiler_params=pltpu.CompilerParams(
            collective_id=1 + reverse, has_side_effects=True, vmem_limit_bytes=16 * 2**20
        ),
    )(*ins)


def assemble_kernel(
    head_count, taps, core, e, w, l, v, eo, wo, lo, vo, in_o, out_o, gain_o, conv_o, bias_o, heads_o, og_o
):
    inner = e.shape[1]
    wide = inner // 4
    bc = l.shape[1] - inner - LANE
    zero = core[0] == 0
    i = lax.broadcasted_iota(jnp.int32, (LANE, LANE), 0)
    j = lax.broadcasted_iota(jnp.int32, (LANE, LANE), 1)
    per = head_count // 8
    spot = 2 * per * (i // per) + lax.rem(i, per)
    valid = i < head_count // 2
    first = jnp.where(valid & (j == spot), 1.0, 0.0)
    second = jnp.where(valid & (j == spot + per), 1.0, 0.0)
    mine_to, other_to = jnp.where(zero, first, second), jnp.where(zero, second, first)

    for n in range(4):
        src = slice(n * wide, (n + 1) * wide)
        for base, a, b in ((0, e, eo), (2 * inner, l, lo)):
            mine, other = a[:, src].astype(F32).T, b[:, src].astype(F32).T
            low = base + 2 * n * wide
            in_o[low : low + wide, :] = jnp.where(zero, mine, other)
            in_o[low + wide : low + 2 * wide, :] = jnp.where(zero, other, mine)
    at = slice(inner, inner + bc)
    in_o[4 * inner : 4 * inner + bc, :] = (l[:, at].astype(F32) + lo[:, at].astype(F32)).T
    at = slice(inner + bc, inner + bc + LANE)
    heads = mm(l[:, at], mine_to) + mm(lo[:, at], other_to)
    in_o[4 * inner + bc : 4 * inner + bc + head_count, :] = heads.T[0:head_count, :]
    mine, other = w[...].astype(F32), wo[...].astype(F32)
    out_o[0] = jnp.where(zero, mine, other)
    out_o[1] = jnp.where(zero, other, mine)

    top, low = inner // LANE, bc // LANE
    wide = wide // LANE

    def halves(target, row, source):
        for n in range(top):
            mine, other = v[source + n : source + n + 1, :], vo[source + n : source + n + 1, :]
            to = ((n // wide) * 2 * wide + n % wide) * LANE
            target[row : row + 1, to : to + LANE] = jnp.where(zero, mine, other)
            to += wide * LANE
            target[row : row + 1, to : to + LANE] = jnp.where(zero, other, mine)

    for k in range(taps + 1):
        target, row = (conv_o, k) if k < taps else (bias_o, 0)
        halves(target, row, k * top)
        for n in range(low):
            at = (taps + 1) * top + k * low + n
            to = 2 * inner + n * LANE
            target[row : row + 1, to : to + LANE] = v[at : at + 1, :] + vo[at : at + 1, :]
    at = (taps + 1) * (top + low)

    def exact(a, b):
        return jnp.dot(a, b, precision=HI, preferred_element_type=F32)

    heads_o[...] = exact(v[at : at + 8, :], mine_to) + exact(vo[at : at + 8, :], other_to)
    halves(og_o, 0, at + 3)
    gain_o[...] = v[at + 3 + top : at + 3 + 2 * top, :]


def assemble(core, mine, other, proj, head_count, taps):
    flat = [a.reshape(-1, a.shape[-1]) for a in tuple(mine) + tuple(other)]
    rows, inner = flat[0].shape
    chan = 2 * inner + flat[2].shape[1] - inner - LANE
    place = pl.BlockSpec(memory_space=pltpu.VMEM)
    outs = [
        (proj, rows), (2, rows, inner), (8, LANE), (taps, chan), (1, chan), (8, LANE),
        (1, 2 * inner),
    ]
    return pl.pallas_call(
        functools.partial(assemble_kernel, head_count, taps),
        in_specs=[pl.BlockSpec(memory_space=pltpu.SMEM)] + [place] * 8,
        out_specs=[place] * len(outs),
        out_shape=[sds(shape, F32) for shape in outs],
        compiler_params=pltpu.CompilerParams(vmem_limit_bytes=40 * 2**20),
    )(core.astype(jnp.int32).reshape(1), *flat)


def pack_kernel(head_count, w, o, *refs):
    by_layer, sent, send, recv = (refs[0:3], refs[3:6]), refs[6:9], refs[9], refs[10]
    core = lax.axis_index("section")
    twin = {"section": 1 - core}
    wide = o.shape[0] // 2
    inner = 4 * wide
    bc_at = 4 * inner
    dt_at = w.shape[0] - head_count
    greet([twin])
    per = head_count // 8
    i = lax.broadcasted_iota(jnp.int32, (head_count, LANE), 0)
    j = lax.broadcasted_iota(jnp.int32, (head_count, LANE), 1)

    def pack_x(which, target):
        for n in range(4):
            at = pl.multiple_of(2 * inner + 2 * n * wide + which * wide, wide)
            target[:, n * wide : (n + 1) * wide] = w[pl.ds(at, wide), :].T
        target[:, inner : inner + dt_at - bc_at] = w[bc_at:dt_at, :].T
        pick = (i == 2 * per * (j // per) + per * which + lax.rem(j, per)) & (j < 4 * per)
        heads = mm_tn(w[dt_at:, :], jnp.where(pick, 1.0, 0.0))
        target[:, inner + dt_at - bc_at :] = heads.astype(BF16)

    def pack_z(which, target):
        for n in range(4):
            at = pl.multiple_of(2 * n * wide + which * wide, wide)
            target[:, n * wide : (n + 1) * wide] = w[pl.ds(at, wide), :].T

    def pack_o(which, target):
        target[...] = o[pl.ds(pl.multiple_of(which * wide, wide), wide), :]

    packs = (pack_x, pack_z, pack_o)

    def work(layer):
        copies = []
        for n in range(3):
            packs[n](1 - layer, sent[n])
            copies.append(
                pltpu.make_async_remote_copy(
                    src_ref=sent[n],
                    dst_ref=by_layer[layer][n],
                    send_sem=send.at[n],
                    recv_sem=recv.at[n],
                    device_id=twin,
                    device_id_type=MESH,
                )
            )
            copies[n].start()
        for n in range(3):
            packs[n](layer, by_layer[layer][n])
        for copy in copies:
            copy.wait()

    @pl.when(core == 0)
    def _():
        work(0)

    @pl.when(core == 1)
    def _():
        work(1)


def pack_weights(w, o, head_count):
    wide, rows = o.shape[0] // 2, w.shape[1]
    shapes = [(rows, 4 * wide + 2 * LANE + LANE), (rows, 4 * wide), (wide, o.shape[1])]
    place = pl.BlockSpec(memory_space=pltpu.VMEM)
    out = pl.pallas_call(
        functools.partial(pack_kernel, head_count),
        out_shape=[sds(shape, BF16) for shape in shapes * 2],
        in_specs=[place] * 2,
        out_specs=[place] * 6,
        scratch_shapes=[pltpu.VMEM(shape, BF16) for shape in shapes]
        + [pltpu.SemaphoreType.DMA((3,))] * 2,
        compiler_params=pltpu.CompilerParams(
            collective_id=4, has_side_effects=True, vmem_limit_bytes=24 * 2**20
        ),
    )(w, o)
    return out[0:3], out[3:6]


def spread_kernel(x_own, z_own, o_own, x_all, z_all, o_all, send, recv, local):
    sender = Sender(send, recv)
    q = lax.axis_index("seq")
    x = lax.axis_index("wshard")
    z, y = q // 4, lax.rem(q, 4)
    shards = [lax.rem(x + d, 4) for d in (1, 2, 3)]
    z_up, z_down = lax.rem(z + 1, 4), lax.rem(z + 3, 4)
    y_up, y_down = lax.rem(y + 1, 4), lax.rem(y + 3, 4)
    to_z_up, to_z_down = {"seq": z_up * 4 + y}, {"seq": z_down * 4 + y}
    to_y_up, to_y_down = {"seq": z * 4 + y_up}, {"seq": z * 4 + y_down}
    greet([{"wshard": p} for p in shards] + [to_z_up, to_z_down, to_y_up, to_y_down])
    pairs = ((x_own, x_all), (z_own, z_all), (o_own, o_all))
    x_up, x_down = lax.rem(x + 1, 4), lax.rem(x + 3, 4)
    to_x_up, to_x_down = {"wshard": x_up}, {"wshard": x_down}
    sent = [
        sender.start(own.at[z, y], full.at[x, z, y], {"wshard": p})
        for p in shards
        for own, full in pairs[0:2]
    ]
    o_ways = [sender.start(o_own, o_all.at[x], device) for device in (to_x_up, to_x_down)]
    kept = [
        pltpu.make_async_copy(own, full.at[x], local.at[n]) for n, (own, full) in enumerate(pairs)
    ]
    for copy in kept:
        copy.start()
    for copy in sent:
        copy.wait()
    cut = 10 * LANE
    over_y = ((x_all, slice(0, cut)),)
    over_z = ((z_all, slice(0, z_all.shape[-1])), (x_all, slice(cut, x_all.shape[-1])))
    ups, downs = [], []

    def both_ways(refs, up, down):
        ups.append([sender.start(r, r, up) for r in refs])
        downs.append([sender.start(r, r, down) for r in refs])

    for p in shards:
        both_ways([a.at[p, z, y, :, c] for a, c in over_y], to_y_up, to_y_down)
        both_ways([a.at[p, z, y, :, c] for a, c in over_z], to_z_up, to_z_down)
    rest = []
    for n, p in enumerate(shards):
        for copy in ups[2 * n] + ups[2 * n + 1] + downs[2 * n] + downs[2 * n + 1]:
            copy.wait()
        if n != 1:
            refs = [a.at[p, z, y_down, :, c] for a, c in over_y[0:1]]
            rest += [sender.start(r, r, to_y_up) for r in refs]
            refs = [a.at[p, z_down, y, :, c] for a, c in over_z[: 2 if n == 0 else 1]]
            rest += [sender.start(r, r, to_z_up) for r in refs]
        if n != 0:
            refs = [a.at[p, z, y_up, :, c] for a, c in over_y[0 if n == 1 else 1 :]]
            rest += [sender.start(r, r, to_y_down) for r in refs]
            refs = [a.at[p, z_up, y, :, c] for a, c in over_z[0 if n == 1 else 1 :]]
            rest += [sender.start(r, r, to_z_down) for r in refs]
    for copy in o_ways:
        copy.wait()
    here, there = o_all.at[x_down, 0:2], o_all.at[x_up, 2:4]
    o_rest = [sender.start(here, here, to_x_up), sender.start(there, there, to_x_down)]
    for copy in rest:
        copy.wait()
    ups.clear()
    downs.clear()
    for p in shards:
        both_ways([a.at[p, z, :, :, c] for a, c in over_y], to_z_up, to_z_down)
        both_ways([a.at[p, :, y, :, c] for a, c in over_z], to_y_up, to_y_down)
    rest = []
    low, high = slice(0, 2), slice(2, 4)
    for n, p in enumerate(shards):
        for copy in ups[2 * n] + ups[2 * n + 1] + downs[2 * n] + downs[2 * n + 1]:
            copy.wait()
        for a, c in over_y:
            here, there = a.at[p, z_down, low, :, c], a.at[p, z_up, high, :, c]
            rest += [sender.start(here, here, to_z_up), sender.start(there, there, to_z_down)]
        for a, c in over_z:
            here, there = a.at[p, low, y_down, :, c], a.at[p, high, y_up, :, c]
            rest += [sender.start(here, here, to_y_up), sender.start(there, there, to_y_down)]
    for copy in rest + o_rest:
        copy.wait()
    for copy in kept:
        copy.wait()


def spread_weights(x_own, z_own, o_own):
    own = [a.reshape(4, 4, a.shape[0] // 16, a.shape[1]) for a in (x_own, z_own, o_own)]
    place = pl.BlockSpec(memory_space=pltpu.VMEM)
    count = 6 + 4 + 18 + 9 + 18 + 18
    full = pl.pallas_call(
        spread_kernel,
        out_shape=[sds((4,) + a.shape, BF16) for a in own],
        in_specs=[place] * 3,
        out_specs=[place] * 3,
        scratch_shapes=[
            pltpu.SemaphoreType.DMA((count,)),
            pltpu.SemaphoreType.DMA((count,)),
            pltpu.SemaphoreType.DMA((3,)),
        ],
        compiler_params=pltpu.CompilerParams(
            collective_id=3, has_side_effects=True, vmem_limit_bytes=24 * 2**20
        ),
    )(*own)
    return tuple(a.reshape(-1, a.shape[-1]) for a in full)


class Ring:
    def __init__(self, sender, src, index, me, up, down, buf):
        self.sender, self.src, self.index, self.buf = sender, src, index, buf
        self.me, (self.up, self.to_up), (self.down, self.to_down) = me, up, down

    def start(self):
        src, buf, index = self.src, self.buf, self.index
        far = lax.rem(self.me + 2, 4)
        begin = self.sender.start
        self.copies = [
            begin(src.at[index(far, 0)], buf.at[0], self.to_up),
            begin(src.at[index(far, 1)], buf.at[1], self.to_down),
            begin(src.at[index(self.up, 1)], buf.at[4], self.to_up),
            begin(src.at[index(self.down, 0)], buf.at[5], self.to_down),
        ]

    def middle(self):
        src, buf, index = self.src, self.buf, self.index
        for n, (p, device) in enumerate(((self.up, self.to_up), (self.down, self.to_down))):
            self.copies[n].wait()
            total = buf[n].astype(F32) + src[index(p, n)].astype(F32)
            buf[2 + n] = total.astype(buf.dtype)
            self.copies.append(self.sender.start(buf.at[2 + n], buf.at[6 + n], device))

    def finish(self):
        src, buf, index = self.src, self.buf, self.index
        for copy in self.copies[2:]:
            copy.wait()
        for n, other in ((0, 5), (1, 4)):
            total = src[index(self.me, n)].astype(F32) + buf[other].astype(F32)
            yield n, total + buf[6 + n].astype(F32)


def reduce_kernel(cut, z0, o0, b0, z1, o1, b1, small, *refs):
    g_own, g_other, refs = refs[0:4], refs[4:8], refs[8:]
    xr, xs, bx, ring_x, ring_a, total_a, far_a, sum_a, last_a = refs[0:9]
    rings, totals, far = refs[9:16], refs[16:23], refs[23:30]
    f, o = refs[30:34], refs[34:38]
    sender = Sender(refs[38], refs[39])
    core = lax.axis_index("section")
    q = lax.axis_index("seq")
    x = lax.axis_index("wshard")
    z, y = q // 4, lax.rem(q, 4)

    def on_x(d):
        return {"wshard": lax.rem(x + d, 4)}

    def on_y(d):
        return {"seq": z * 4 + lax.rem(y + d, 4)}

    def on_z(d):
        return {"seq": lax.rem(z + d, 4) * 4 + y}

    twin = {"section": 1 - core}
    greet([on(d) for on in (on_x, on_y, on_z) for d in (1, 2, 3)] + [twin])

    def near(me, on):
        return me, (lax.rem(me + 1, 4), on(1)), (lax.rem(me + 3, 4), on(3))

    halves = (slice(0, 2), slice(2, 4))
    everything = slice(None)
    over_x = Ring(sender, b0, lambda p, h: (p, halves[h]), *near(x, on_x), ring_x)
    over_x.start()
    small_x = [sender.start(small, xr.at[d - 1], on_x(d)) for d in (1, 2, 3)]

    low, high = slice(0, cut), slice(cut, b1.shape[-1])
    parts = [
        (z1, everything, 1, True, 0),
        (o1, everything, 1, False, 1),
        (b1, low, 1, True, 2),
        (b1, high, 1, False, 2),
        (xs.at[0], everything, 0, True, 3),
        (xs.at[1], everything, 1, False, 3),
        (bx, low, 0, True, 2),
        (bx, high, 0, False, 2),
    ]

    def ring_of(n):
        src, cols, _, y_first, _ = parts[n]
        if y_first:
            return Ring(
                sender, src, lambda p, h: (halves[h], p, everything, cols), *near(y, on_y), bufs(n)
            )
        return Ring(
            sender, src, lambda p, h: (p, halves[h], everything, cols), *near(z, on_z), bufs(n)
        )

    def bufs(n):
        return rings[n] if n < 6 else rings[6].at[:, :, :, parts[n][1]]

    def ending(n, ring):
        total = totals[n] if n < 6 else totals[6].at[:, :, parts[n][1]]
        for half, value in ring.finish():
            total[halves[half]] = value.astype(total.dtype)
        y_first = parts[n][3]
        there = far[n] if n < 6 else far[6].at[:, :, parts[n][1]]
        copies = []
        for d in (1, 2, 3):
            to, peer = (lax.rem(z + d, 4), on_z(d)) if y_first else (lax.rem(y + d, 4), on_y(d))
            copies.append(sender.start(total.at[to], there.at[d - 1], peer))
        return total, there, copies

    def closing(n, total, there, copies):
        _, cols, layer, y_first, kind = parts[n]
        for copy in copies:
            copy.wait()
        value = total[z if y_first else y].astype(F32)
        for d in range(3):
            value = value + there[d].astype(F32)
        f[kind][layer, :, cols] = value.astype(f[kind].dtype)

    wide = [
        Ring(sender, z0, lambda p, h: (halves[h], everything, p), *near(y, on_y), ring_a.at[0]),
        Ring(sender, o0, lambda p, h: (halves[h], p), *near(z, on_z), ring_a.at[1]),
    ]
    running = [ring_of(n) for n in range(8)]
    for ring in wide:
        ring.start()
    for n in range(4):
        running[n].start()
    for copy in small_x:
        copy.wait()
    xs[...] = small[...] + xr[0] + xr[1] + xr[2]
    running[4].start()
    running[5].start()
    for ring in wide:
        ring.middle()
    over_x.middle()
    for n in range(6):
        running[n].middle()
    wide_copies = []
    for side, ring in enumerate(wide):
        for half, value in ring.finish():
            total_a[side, halves[half]] = value.astype(BF16)
        for d in (1, 2, 3):
            to, peer = (lax.rem(y + d, 4), on_y(d)) if side else (lax.rem(z + d, 4), on_z(d))
            wide_copies.append(
                sender.start(total_a.at[side, :, to], far_a.at[side, d - 1], peer)
            )
    for half, value in over_x.finish():
        bx[halves[half]] = value.astype(bx.dtype)
    running[6].start()
    running[7].start()
    ended = [ending(n, running[n]) for n in range(6)]
    last_copies = []
    for side in (0, 1):
        for copy in wide_copies[3 * side : 3 * side + 3]:
            copy.wait()
        value = total_a[side, :, y if side else z].astype(F32)
        for d in range(3):
            value = value + far_a[side, d].astype(F32)
        sum_a[side] = value.astype(BF16)
        for d in (1, 2, 3):
            here = sum_a.at[side, lax.rem(x + d, 4)]
            last_copies.append(sender.start(here, last_a.at[side, d - 1], on_x(d)))
    running[6].middle()
    running[7].middle()
    for n in range(6):
        closing(n, *ended[n])
    ended += [ending(n, running[n]) for n in (6, 7)]
    for side in (0, 1):
        for copy in last_copies[3 * side : 3 * side + 3]:
            copy.wait()
        value = sum_a[side, x].astype(F32)
        for d in range(3):
            value = value + last_a[side, d].astype(F32)
        f[side][0] = value.astype(BF16)
    for n in (6, 7):
        closing(n, *ended[n])
    twins = [sender.start(f[n].at[1 - core], o[n], twin) for n in range(4)]
    gather = []
    for n in range(4):
        g_own[n][z, y] = f[n][core]
        for d in (1, 2, 3):
            gather.append(sender.start(f[n].at[core], g_own[n].at[z, y], on_y(d)))
    for copy in twins:
        copy.wait()
    for n in range(4):
        g_other[n][z, y] = o[n][...]
        for d in (1, 2, 3):
            gather.append(sender.start(o[n], g_other[n].at[z, y], on_z(d)))
    for copy in gather:
        copy.wait()
    _, (z_up, to_z_up), (z_down, to_z_down) = near(z, on_z)
    _, (y_up, to_y_up), (y_down, to_y_down) = near(y, on_y)
    gather = []
    for own, other in zip(g_own, g_other):
        for device in (to_z_up, to_z_down):
            gather.append(sender.start(own.at[z], own.at[z], device))
        for device in (to_y_up, to_y_down):
            gather.append(sender.start(other.at[:, y], other.at[:, y], device))
    last = []
    for n, (own, other) in enumerate(zip(g_own, g_other)):
        for copy in gather[4 * n : 4 * n + 4]:
            copy.wait()
        for half, z_to, y_to, z_from, y_from in (
            (halves[0], to_z_up, to_y_up, z_down, y_down),
            (halves[1], to_z_down, to_y_down, z_up, y_up),
        ):
            here = own.at[z_from, half]
            last.append(sender.start(here, here, z_to))
            here = other.at[half, y_from]
            last.append(sender.start(here, here, y_to))
    for copy in last:
        copy.wait()


def reduce_all(z0, o0, b0, z1, o1, b1, small):
    kinds = [(a.shape[2:], a.dtype) for a in (z1, o1, b1, small[0])]
    cut = 6 * LANE
    wide = b1.shape[-1]
    rows, mid = z1.shape[2:]
    thin = [((rows, c), BF16) for c in (cut, wide - cut)]
    full = [sds((4, 4) + shape, dtype) for shape, dtype in kinds]
    order = [kinds[0], kinds[1], thin[0], thin[1], kinds[3], kinds[3], kinds[2]]

    def vmem(shapes, *lead):
        return [pltpu.VMEM(lead + shape, dtype) for shape, dtype in shapes]

    count = 6 + 3 + 2 * 12 + 8 * 9 + 4 + 24 + 16 + 16
    scratch = [
        pltpu.VMEM((3,) + small.shape, F32),
        pltpu.VMEM(small.shape, F32),
        pltpu.VMEM(b1.shape, BF16),
        pltpu.VMEM((8, 2) + b1.shape[1:], BF16),
        pltpu.VMEM((2, 8, 2, 4, rows, mid), BF16),
        pltpu.VMEM((2, 4, 4, rows, mid), BF16),
        pltpu.VMEM((2, 3, 4, rows, mid), BF16),
        pltpu.VMEM((2, 4, rows, mid), BF16),
        pltpu.VMEM((2, 3, rows, mid), BF16),
        *vmem(order, 8, 2), *vmem(order, 4), *vmem(order, 3), *vmem(kinds, 2), *vmem(kinds),
        pltpu.SemaphoreType.DMA((count,)),
        pltpu.SemaphoreType.DMA((count,)),
    ]
    place = pl.BlockSpec(memory_space=pltpu.VMEM)
    out = pl.pallas_call(
        functools.partial(reduce_kernel, cut),
        out_shape=full + full,
        in_specs=[place] * 7,
        out_specs=[place] * 8,
        scratch_shapes=scratch,
        compiler_params=pltpu.CompilerParams(
            collective_id=0, has_side_effects=True, vmem_limit_bytes=48 * 2**20
        ),
    )(z0, o0, b0, z1, o1, b1, small)
    return out[0:4], out[4:8]


def forward(u, w, p):
    w_x, w_z, w_out = w
    gain_in, cw, cb, hp, gain_out = p
    seqs, rows, width = u.shape
    chan = cw.shape[1]
    taps = 4
    inner = gain_out.shape[1]
    states = LANE
    uf = u.astype(F32)
    inv = lax.rsqrt(jnp.mean(uf * uf, axis=-1, keepdims=True) + EPS)
    normed = (uf * inv * gain_in).astype(BF16).reshape(seqs * rows, width)
    xd = jnp.dot(normed, w_x, preferred_element_type=F32).astype(BF16)
    xd = xd.reshape(seqs, rows, chan + LANE)
    z = jnp.dot(normed, w_z, preferred_element_type=F32).reshape(seqs, rows, inner)
    halo = shift(xd[:, rows - TAIL :, :chan], "seq", 1)
    act, cum, step, sloc = run(
        functools.partial(chunk_kernel, taps),
        (xd, halo, cw, cb, hp),
        (
            sds((seqs, rows, chan), F32),
            sds((seqs, rows, LANE), F32),
            sds((seqs, rows, LANE), F32),
            sds((seqs * inner // LANE, states + TAIL, LANE), BF16),
        ),
        [pltpu.VMEM((TAIL + rows, chan), F32)],
        (2, 3, 4),
    )
    decay, yi, sin = scan_chunks(
        sloc, None, False, states, (act, cum, step), [sds((seqs, rows, inner), F32)]
    )
    yy, gg, ss = run(
        finish_kernel,
        (act, cum, yi, sin, z, hp, gain_out),
        (
            sds((seqs, rows, inner), F32),
            sds((seqs, rows, inner), BF16),
            sds((seqs, rows, 1), F32),
        ),
        (),
        (5, 6),
    )
    mine = jnp.dot(gg.reshape(seqs * rows, inner), w_out, preferred_element_type=F32)
    mine = mine.astype(BF16).reshape(seqs, rows, width)
    theirs, ss_theirs = swap(mine), swap(ss)
    branch = mine.astype(F32) + theirs.astype(F32)
    rn = lax.rsqrt((ss + ss_theirs) * (1.0 / (2 * inner)) + EPS)
    result = (uf + rn * branch).astype(BF16)
    kept = (u, inv, normed, z, xd, halo, act, cum, step, decay, sin, yy, branch, rn)
    return result, kept


def backward(e, kept, w, p, over_wshard):
    w_x, w_z, w_out = w
    gain_in, cw, cb, hp, gain_out = p
    u, inv, normed, z, xd, halo, act, cum, step, decay, sin, yy, branch, rn = kept
    seqs, rows, width = e.shape
    chan = cw.shape[1]
    taps = 4
    inner = gain_out.shape[1]
    states = LANE
    ef = e.astype(F32)
    e2 = e.reshape(seqs * rows, width)
    nt = (((1,), (1,)), ((), ()))
    tn = (((0,), (0,)), ((), ()))
    gr = lax.dot_general(e2, w_out, nt, preferred_element_type=F32).reshape(seqs, rows, inner)
    rs = jnp.sum(ef * branch, axis=-1, keepdims=True)
    dy, gz, dsl, dgain, gated = run(
        gate_back_kernel,
        (gr, z, yy, act, cum, rn, rs, hp, gain_out),
        (
            sds((seqs, rows, inner), BF16),
            sds((seqs, rows, inner), BF16),
            sds((seqs * inner // LANE, states, LANE), BF16),
            sds((seqs, inner // LANE, LANE), F32),
            sds((seqs, rows, inner), BF16),
        ),
        (),
        (7, 8),
    )
    gz = gz.reshape(seqs * rows, inner)
    part_z = lax.dot_general(gz, w_z, nt, preferred_element_type=F32)
    early_z = lax.dot_general(normed, gz, tn, preferred_element_type=F32).astype(BF16)
    early_o = lax.dot_general(
        gated.reshape(seqs * rows, inner), e2, tn, preferred_element_type=F32
    ).astype(BF16)
    if over_wshard:
        early_z, early_o = (
            lax.psum_scatter(a, "wshard", scatter_dimension=0, tiled=True)
            for a in (early_z, early_o)
        )
    dxs, dbc, dci, grad = scan_chunks(
        dsl,
        decay,
        True,
        states,
        (act, cum, step, dy, sin),
        [
            sds((seqs, rows, inner), F32),
            sds((seqs, rows, 2 * LANE), F32),
            sds((seqs, rows, LANE), F32),
        ],
    )
    dpre, ddt, small = run(
        functools.partial(mix_back_kernel, taps),
        (xd, halo, cw, cb, hp, act, cum, step, dy, dxs, dbc, dci, grad, sin),
        (
            sds((seqs, rows, chan), F32),
            sds((seqs, rows, LANE), BF16),
            sds((seqs, 56, LANE), F32),
        ),
        [pltpu.VMEM((TAIL + rows, chan), F32), pltpu.VMEM((rows, chan), F32)],
        (2, 3, 4),
    )
    after = shift(dpre[:, :8], "seq", -1)
    (gp,) = run(
        functools.partial(conv_back_kernel, taps),
        (dpre, after, ddt, cw),
        (sds((seqs, rows, chan + LANE), BF16),),
        [pltpu.VMEM((rows + 8, chan), F32)],
        (3,),
    )
    gp = gp.reshape(seqs * rows, -1)
    mine = part_z + lax.dot_general(gp, w_x, nt, preferred_element_type=F32)
    mine = mine.astype(BF16).reshape(seqs, rows, width)
    theirs = swap(mine)
    gn = mine.astype(F32) + theirs.astype(F32)
    uf = u.astype(F32)
    unit = uf * inv
    g_gain_in = jnp.sum(gn * unit, axis=(0, 1))
    scaled = gn * gain_in
    dot = jnp.mean(scaled * unit, axis=-1, keepdims=True)
    grad_u = ef + inv * (scaled - unit * dot)
    late = lax.dot_general(normed, gp, tn, preferred_element_type=F32).astype(BF16)
    if over_wshard:
        late = lax.psum_scatter(late, "wshard", scatter_dimension=0, tiled=True)
    rows_of = [small.sum(0)[: small.shape[1] - 3], dgain.sum(0), g_gain_in.reshape(-1, LANE)]
    used = sum(a.shape[0] for a in rows_of)
    smalls = jnp.concatenate(rows_of + [jnp.zeros((16 * 8 - used, LANE), F32)], axis=0)
    return grad_u, (early_z, early_o, late), smalls.reshape(4, 4, 8, LANE)


def body(
    hidden, out_grad, norm_gain, in_weight, conv_weight, conv_bias, dt_bias, a_log, d_skip,
    out_gain, out_weight,
):
    core = lax.axis_index("section")
    width = hidden.shape[2]
    full = out_gain.shape[1]
    taps = conv_weight.shape[1]
    head_count = dt_bias.shape[1]
    proj = in_weight.shape[2]

    shards = pack_weights(in_weight[0].T, out_weight[0], head_count)
    sizes = (norm_gain, conv_weight, conv_bias, dt_bias, a_log, d_skip, out_gain)
    flat = jnp.concatenate([a[0].reshape(-1) for a in sizes])
    flat_other = swap(flat)

    def params(layer):
        mine = core == layer
        w = shards[layer]
        if layer == 0:
            w = spread_weights(*w)
        else:
            w = tuple(lax.all_gather(a, "wshard", axis=0, tiled=True) for a in w)
        v = jnp.where(mine, flat, flat_other)
        parts, at = [], 0
        for a in sizes:
            count = a[0].size
            parts.append(v[at : at + count].reshape(a[0].shape))
            at += count
        gain_in, cw, cb, dtb, al, ds, gain_out = parts

        def channels(a):
            return jnp.concatenate([half(a[..., :full], core), a[..., full:]], axis=-1)

        hp = jnp.stack([half(a, core) for a in (dtb, al, ds)])
        hp = jnp.pad(hp, ((0, 5), (0, LANE - hp.shape[1])))
        cw = jnp.pad(channels(cw), ((0, 8 - taps), (0, 0)))
        return w, (
            gain_in[None],
            cw,
            channels(cb)[None],
            hp,
            half(gain_out, core)[None],
        )

    w0, p0 = params(0)
    w1, p1 = params(1)
    first, kept0 = forward(hidden, w0, p0)
    second, kept1 = forward(first, w1, p1)
    layer_out = jnp.where(core == 0, first, second)[None]
    grad1, products1, smalls1 = backward(out_grad, kept1, w1, p1, True)
    passed = grad1.astype(BF16)
    grad0, products0, smalls0 = backward(passed, kept0, w0, p0, False)
    section_grad = jnp.where(core == 0, grad0, passed.astype(F32))[None]

    rows = width // 64
    first = [a.reshape(4, 4, 4, rows, a.shape[1]) for a in products0]
    second = [a.reshape(4, 4, rows, a.shape[1]) for a in products1]
    mine, other = reduce_all(*first, *second, jnp.stack([smalls0, smalls1]))
    grad_in, grad_out, gains, conv_g, bias_g, heads_g, out_gains = assemble(
        core, mine, other, proj, head_count, taps
    )
    return (
        layer_out,
        section_grad,
        gains.reshape(1, width),
        grad_in.T[None],
        conv_g[None],
        bias_g,
        heads_g[0:1, :head_count],
        heads_g[1:2, :head_count],
        heads_g[2:3, :head_count],
        out_gains,
        grad_out.reshape(1, -1, width),
    )


def solution(mesh):
    by_layer = P("section", None)
    weights = P("section", "wshard", None)
    tokens = P("wshard", "seq", None)
    stacked = P("section", "wshard", "seq", None)
    conv = P("section", None, None)
    in_specs = (
        tokens, tokens, by_layer, weights, conv, by_layer, by_layer, by_layer, by_layer, by_layer,
        weights,
    )
    out_specs = (
        stacked, stacked, by_layer, weights, conv, by_layer, by_layer, by_layer, by_layer,
        by_layer, weights,
    )
    return jax.shard_map(body, mesh=mesh, in_specs=in_specs, out_specs=out_specs, check_vma=False)
```
